32 devices in a mesh: batch: 16 (over z, y, x), tp: 2 (over core).
Axes of the slice: x: 2, y: 2, z: 4, core: 2. Of those that a mesh axis runs over, the one named last changes fastest.
Arguments:
- tokens: bfloat16 [19456, 768], P('batch'), may hold values from -6 to 6
- seq_ids: int32 [19456], P('batch'), may hold values from 0 to 5, as said below
- cotangent: bfloat16 [19456, 768], P('batch'), may hold values from -6 to 6
- norm1_gain: float32 [768], replicated, may hold values from 0.1 to 1.9
- norm1_shift: float32 [768], replicated, may hold values from -3 to 3
- w_qkv: bfloat16 [768, 3, 768], P(None, None, 'tp'), may hold values from -0.21875 to 0.21875
- qv_bias: float32 [2, 768], P(None, 'tp'), may hold values from -3 to 3
- w_out: bfloat16 [768, 768], P('tp'), may hold values from -1.75 to 1.75
- out_bias: float32 [768], replicated, may hold values from -3 to 3
- norm2_gain: float32 [768], replicated, may hold values from 0.1 to 1.9
- norm2_shift: float32 [768], replicated, may hold values from -3 to 3
- w_in: bfloat16 [768, 3072], P(None, 'tp'), may hold values from -0.21875 to 0.21875
- in_bias: float32 [3072], P('tp'), may hold values from -3 to 3
- w_back: bfloat16 [3072, 768], P('tp'), may hold values from -0.109375 to 0.109375
- back_bias: float32 [768], replicated, may hold values from -3 to 3
Outputs:
- layer_out: bfloat16 [19456, 768], P('batch')
- tokens_grad: bfloat16 [19456, 768], P('batch')
- norm1_gain_grad: float32 [768], P('batch')
- norm1_shift_grad: float32 [768], P('batch')
- w_qkv_grad: float32 [768, 3, 768], P('batch', None, 'tp')
- qv_bias_grad: float32 [2, 768], P(None, ('tp', 'batch'))
- w_out_grad: float32 [768, 768], P('tp', 'batch')
- out_bias_grad: float32 [768], P('batch')
- norm2_gain_grad: float32 [768], P('batch')
- norm2_shift_grad: float32 [768], P('batch')
- w_in_grad: float32 [768, 3072], P('batch', 'tp')
- in_bias_grad: float32 [3072], P(('tp', 'batch'))
- w_back_grad: float32 [3072, 768], P('tp', 'batch')
- back_bias_grad: float32 [768], P('batch')
The draws below stay inside these ranges and needn't reach their ends.
Inputs may be any that keep to these rules, and one draw needn't show every extreme that they name: `seq_ids`: in each aligned block of 1216 tokens, ids start at 0 and never fall; sequences of 608 tokens come first, then sequences of 228; the last may be cut by the block's end; some block holds only sequences of 228.
All inputs are finite; a program needn't handle non-finite values.
Results may differ from the reference program's by a relative error of at most 0.012.
Values sent between devices are 32-bit elements; how exact they have to be, the bound alone decides.
A program may use at most 192 MiB of HBM per device.

```python
import jax
import jax.numpy as jnp
from jax import lax

D = 768
HEADS = 12
HEAD_DIM = 64
FF = 3072
LONG = 608
SHORT = 228
QBLOCK = 608
TOK_DEV = 1216
TOKENS = 19456
N_BATCH = 16


def draw_seq_ids(key, part):
    key = jax.random.fold_in(key, 7)
    shards = TOKENS // TOK_DEV
    key_count, key_pick = jax.random.split(key)
    long_count = jax.random.randint(key_count, (shards,), 0, TOK_DEV // LONG + 1)
    chosen_shard = jax.random.randint(key_pick, (), 0, shards)
    long_count = jnp.where(jnp.arange(shards) == chosen_shard, 0, long_count)
    positions = jnp.arange(TOK_DEV)[None, :]
    long_edge = long_count[:, None] * LONG
    segment_ids = jnp.where(positions < long_edge, positions // LONG, long_count[:, None] + (positions - long_edge) // SHORT)
    return segment_ids.reshape(TOKENS).astype(jnp.int32)


def shard_levels(stream_key, shape, cuts, least, largest):
    level, own = 1.0, jax.random.fold_in(stream_key, 6)
    for axis_at, parts in cuts:
        heights = jnp.exp(jax.random.uniform(jax.random.fold_in(own, axis_at), (parts,), jnp.float32, least / len(cuts), largest / len(cuts)))
        level = level * jnp.repeat(heights, shape[axis_at] // parts).reshape([-1 if axis == axis_at else 1 for axis in range(len(shape))])
    return level


def centred(rng, extent, scale, bound, cuts=(), kind=jnp.bfloat16):
    values = scale * jax.random.normal(rng, extent, jnp.float32)
    if cuts:
        values = values * shard_levels(rng, extent, cuts, -0.22, 0.18)
    return jnp.clip(values, -bound, bound).astype(kind)


def setup_inputs(seed: int = 0) -> dict:
    key_of = jax.random.split(jax.random.key(seed), 16)
    tokens = centred(key_of[0], (TOKENS, D), 1.0, 6.0, ((0, 16),))
    seq_ids = draw_seq_ids(jax.random.fold_in(key_of[15], 71), 0)
    cotangent = centred(key_of[2], (TOKENS, D), 1.0, 6.0, ((0, 16),))
    norm1_gain = jnp.clip(1.0 + 0.18 * jax.random.normal(key_of[3], (D,), jnp.float32), 0.1, 1.9)
    norm1_shift = centred(key_of[4], (D,), 0.3, 3.0, (), jnp.float32)
    w_qkv = centred(key_of[5], (D, 3, D), D ** -0.5, 0.21875, ((2, 2),))
    qv_bias = centred(key_of[6], (2, D), 0.5, 3.0, ((1, 2),), jnp.float32)
    w_out = centred(key_of[7], (D, D), (D // 64) ** -0.5, 1.75, ((0, 2),))
    out_bias = centred(key_of[8], (D,), 0.5, 3.0, (), jnp.float32)
    norm2_gain = jnp.clip(1.0 + 0.18 * jax.random.normal(key_of[9], (D,), jnp.float32), 0.1, 1.9)
    norm2_shift = centred(key_of[10], (D,), 0.3, 3.0, (), jnp.float32)
    w_in = centred(key_of[11], (D, FF), D ** -0.5, 0.21875, ((1, 2),))
    in_bias = centred(key_of[12], (FF,), 0.5, 3.0, ((0, 2),), jnp.float32)
    w_back = centred(key_of[13], (FF, D), FF ** -0.5, 0.109375, ((0, 2),))
    back_bias = centred(key_of[14], (D,), 0.5, 3.0, (), jnp.float32)
    return dict(tokens=tokens, seq_ids=seq_ids, cotangent=cotangent, norm1_gain=norm1_gain, norm1_shift=norm1_shift, w_qkv=w_qkv, qv_bias=qv_bias, w_out=w_out, out_bias=out_bias, norm2_gain=norm2_gain, norm2_shift=norm2_shift, w_in=w_in, in_bias=in_bias, w_back=w_back, back_bias=back_bias)


HIGH = lax.Precision.HIGHEST

@jax.custom_vjp
def low(v):
    return lax.optimization_barrier(v.astype(jnp.bfloat16)).astype(jnp.float32)

@jax.custom_vjp
def low_back(v):
    return v

def low_keep(v):
    return (low(v), None)

def low_pass(kept, grad):
    return (grad,)

def back_keep(v):
    return (v, None)

def back_low(kept, grad):
    return (low(grad),)
low.defvjp(low_keep, low_pass)
low_back.defvjp(back_keep, back_low)

def normalize(values, norm_gain, norm_shift):
    center = values - lax.optimization_barrier(jnp.mean(values, -1, keepdims=True))
    spread = lax.optimization_barrier(jnp.mean(center * center, -1, keepdims=True))
    return center * lax.rsqrt(spread + 1e-06) * norm_gain + norm_shift

def attention(query, keys, values, segment):
    count = TOK_DEV // QBLOCK
    scale = HEAD_DIM ** (-0.5)
    query_blocks = query.reshape(count, QBLOCK, HEADS, HEAD_DIM)
    segment_blocks = segment.reshape(count, QBLOCK)

    def one_block(item):
        rows, row_ids = item
        scores = low_back(jnp.einsum('qhe,khe->hqk', rows, keys, precision=HIGH) * scale)
        allowed = (row_ids[:, None] == segment[None, :])[None]
        scores = jnp.where(allowed, scores, -1000000000.0)
        top = lax.optimization_barrier(jnp.max(scores, -1, keepdims=True))
        expo = jnp.exp(scores - top)
        probs = low(expo / lax.optimization_barrier(jnp.sum(expo, -1, keepdims=True)))
        return jnp.einsum('hqk,khe->qhe', probs, values, precision=HIGH)
    mixed = lax.map(jax.checkpoint(one_block), (query_blocks, segment_blocks))
    return mixed.reshape(TOK_DEV, HEADS * HEAD_DIM)

def layer(inputs, segment, norm1_gain, norm1_shift, w_qkv, qv_bias, w_out, out_bias, norm2_gain, norm2_shift, w_in, in_bias, w_back, back_bias):
    normed = low(normalize(inputs, norm1_gain, norm1_shift))
    proj = jnp.einsum('td,dcf->tcf', normed, w_qkv, precision=HIGH)
    query = low(low_back(proj[:, 0] + qv_bias[0])).reshape(TOK_DEV, HEADS, HEAD_DIM)
    keys = low(low_back(proj[:, 1])).reshape(TOK_DEV, HEADS, HEAD_DIM)
    values = low(low_back(proj[:, 2] + qv_bias[1])).reshape(TOK_DEV, HEADS, HEAD_DIM)
    mixed = low(low_back(attention(query, keys, values, segment)))
    branch = low_back(jnp.dot(mixed, w_out, precision=HIGH) + out_bias)
    middle = inputs + branch
    normed_two = low(normalize(middle, norm2_gain, norm2_shift))
    hidden_pre = low_back(jnp.dot(normed_two, w_in, precision=HIGH) + in_bias)
    hidden = low(jax.nn.gelu(hidden_pre))
    mlp_out = low_back(jnp.dot(hidden, w_back, precision=HIGH) + back_bias)
    return middle + mlp_out

def reference(tokens, seq_ids, cotangent, norm1_gain, norm1_shift, w_qkv, qv_bias, w_out, out_bias, norm2_gain, norm2_shift, w_in, in_bias, w_back, back_bias):
    params = tuple((item.astype(jnp.float32) for item in (norm1_gain, norm1_shift, w_qkv, qv_bias, w_out, out_bias, norm2_gain, norm2_shift, w_in, in_bias, w_back, back_bias)))
    inputs = tokens.astype(jnp.float32).reshape(N_BATCH, TOK_DEV, D)
    segments = seq_ids.reshape(N_BATCH, TOK_DEV)
    grads_in = cotangent.astype(jnp.float32).reshape(N_BATCH, TOK_DEV, D)

    def one_shard(carry, item):
        shard_in, shard_ids, shard_grad = item

        def forward(values, *weights):
            return layer(values, shard_ids, *weights)
        result, pull = jax.vjp(forward, shard_in, *params)
        grads = pull(shard_grad)
        carry = tuple((total + part for total, part in zip(carry, grads[1:])))
        return (carry, (result.astype(jnp.bfloat16), grads[0].astype(jnp.bfloat16)))
    start = tuple((jnp.zeros_like(item) for item in params))
    sums, (outputs, input_grads) = lax.scan(one_shard, start, (inputs, segments, grads_in))
    return (outputs.reshape(TOKENS, D), input_grads.reshape(TOKENS, D), sums[0], sums[1], sums[2], sums[3], sums[4], sums[5], sums[6], sums[7], sums[8], sums[9], sums[10], sums[11])
```

```python
import functools

import jax
import jax.numpy as jnp
from jax import lax
from jax.experimental import pallas as pl
from jax.experimental.pallas import tpu as pltpu
from jax.sharding import PartitionSpec as P

HEAD_DIM = 64
PAIR = 2 * HEAD_DIM
HALF = 608
TILE = 304
WINDOWS = ((0, 688), (448, 1216))
f32 = jnp.float32
bf16 = jnp.bfloat16


def params(mib):
    return pltpu.CompilerParams(vmem_limit_bytes=mib << 20)


def cost(flops, nbytes, trans=0):
    return pl.CostEstimate(flops=int(flops), bytes_accessed=int(nbytes), transcendentals=int(trans))


def nn(a, b):
    return jnp.dot(a, b, preferred_element_type=f32)


def nt(a, b):
    return lax.dot_general(a, b, (((1,), (1,)), ((), ())), preferred_element_type=f32)


def tn(a, b):
    return lax.dot_general(a, b, (((0,), (0,)), ((), ())), preferred_element_type=f32)


def standardize(values):
    center = values - jnp.mean(values, -1, keepdims=True)
    spread = jnp.mean(center * center, -1, keepdims=True)
    inv = lax.rsqrt(spread + 1e-06)
    return center * inv, inv


def norm_back(unit, inv, gain, grad):
    scaled = grad * gain
    return inv * (
        scaled
        - jnp.mean(scaled, -1, keepdims=True)
        - unit * jnp.mean(scaled * unit, -1, keepdims=True)
    )


def whole(shape):
    return pl.BlockSpec(shape, lambda *_: (0,) * len(shape))


def project_kernel(x_ref, gain_ref, shift_ref, w_ref, bias_ref, n_ref, q_ref, k_ref, v_ref):
    unit, _ = standardize(x_ref[...].astype(f32))
    normed = (unit * gain_ref[...] + shift_ref[...]).astype(bf16)
    n_ref[...] = normed
    scale = HEAD_DIM ** (-0.5)
    q_ref[...] = ((nn(normed, w_ref[0]) + bias_ref[0:1]).astype(bf16).astype(f32) * scale).astype(bf16)
    k_ref[...] = nn(normed, w_ref[1]).astype(bf16)
    v_ref[...] = (nn(normed, w_ref[2]) + bias_ref[1:2]).astype(bf16)


def project(tokens, gain, shift, w3, qv_bias):
    tok, dim = tokens.shape
    width = w3.shape[2]
    rows = lambda n: pl.BlockSpec((TILE, n), lambda i: (i, 0))
    out = jax.ShapeDtypeStruct((tok, width), bf16)
    return pl.pallas_call(
        project_kernel,
        grid=(tok // TILE,),
        in_specs=[rows(dim), whole((1, dim)), whole((1, dim)), whole(w3.shape), whole((2, width))],
        out_specs=[rows(dim), rows(width), rows(width), rows(width)],
        out_shape=[jax.ShapeDtypeStruct((tok, dim), bf16), out, out, out],
        compiler_params=params(32),
        cost_estimate=cost(2 * tok * dim * 3 * width, tok * (2 * dim + 3 * width) * 2 + w3.size * 2),
        name="project",
    )(tokens, gain, shift, w3, qv_bias)


def attend_kernel(half, q_ref, k_ref, v_ref, col_ref, row_ref, w_ref, *refs):
    o_ref, lse_ref, part_ref, mask_ref = refs[-4:]
    low, high = WINDOWS[half]
    step = pl.program_id(0)

    @pl.when(step == 0)
    def _():
        same = col_ref[...] == row_ref[:, low:high]
        mask_ref[...] = jnp.where(same, 0.0, -1000000000.0)

    first = lax.broadcasted_iota(jnp.int32, (1, PAIR), 1) < HEAD_DIM
    keys = k_ref[low:high, :]
    values = v_ref[low:high, :]
    zero = jnp.zeros((), bf16)
    one = jnp.ones((), bf16)
    with_ones = (jnp.where(first, values, one), jnp.where(first, one, values))
    for at in range(0, HALF, TILE):
        rows = q_ref[at : at + TILE, :]
        mask = mask_ref[at : at + TILE, :]
        outs, logs = [], []
        for head in range(2):
            own = jnp.where(first, rows, zero) if head == 0 else jnp.where(first, zero, rows)
            scores = nt(own, keys) + mask
            top = jnp.max(scores, -1, keepdims=True)
            expo = jnp.exp(scores - top).astype(bf16)
            mixed = nn(expo, with_ones[head])
            total = pltpu.roll(mixed, HEAD_DIM, 1)
            outs.append(mixed / total)
            logs.append(top + jnp.log(total))
        mixed = jnp.where(first, outs[0], outs[1]).astype(bf16)
        o_ref[at : at + TILE, :] = mixed
        lse_ref[at : at + TILE, :] = jnp.where(first, logs[0], logs[1])
        part = nn(mixed, w_ref[...])

        @pl.when(step == 0)
        def _():
            part_ref[at : at + TILE, :] = part

        @pl.when(step > 0)
        def _():
            part_ref[at : at + TILE, :] += part


def attend(half, q, k, v, ids_col, ids_row, w_out, before=()):
    tok, width = q.shape
    dim = w_out.shape[1]
    low, high = WINDOWS[half]
    pair_rows = pl.BlockSpec((HALF, PAIR), lambda p: (half, p))
    pair_all = pl.BlockSpec((tok, PAIR), lambda p: (0, p))
    return pl.pallas_call(
        functools.partial(attend_kernel, half),
        grid=(width // PAIR,),
        in_specs=[
            pair_rows,
            pair_all,
            pair_all,
            pl.BlockSpec((HALF, 1), lambda p: (half, 0)),
            whole((1, tok)),
            pl.BlockSpec((PAIR, dim), lambda p: (p, 0)),
        ]
        + [pl.BlockSpec(memory_space=pl.ANY)] * len(before),
        out_specs=[pair_rows, pair_rows, whole((HALF, dim))],
        out_shape=[
            jax.ShapeDtypeStruct((tok, width), bf16),
            jax.ShapeDtypeStruct((tok, width), f32),
            jax.ShapeDtypeStruct((HALF, dim), f32),
        ],
        scratch_shapes=[pltpu.VMEM((HALF, high - low), f32)],
        input_output_aliases={6 + i: i for i in range(len(before))},
        compiler_params=params(48),
        cost_estimate=cost(16 * HALF * (high - low) * width, tok * width * 6 + HALF * dim * 4),
        name="attend",
    )(q, k, v, ids_col, ids_row, w_out, *before)


def hidden_kernel(x_ref, own_ref, peer_ref, ob_ref, gain_ref, shift_ref, w_ref, ib_ref, *refs):
    mid_ref, n_ref, hid_ref, slope_ref = refs[-4:]
    middle = x_ref[...].astype(f32) + (own_ref[...] + peer_ref[...]) + ob_ref[...]
    mid_ref[...] = middle
    unit, _ = standardize(middle)
    normed = (unit * gain_ref[...] + shift_ref[...]).astype(bf16)
    n_ref[...] = normed
    width = w_ref.shape[1]
    piece = 512
    c0 = 0.7978845608028654
    for at in range(0, width, piece):
        u = nn(normed, w_ref[:, at : at + piece]) + ib_ref[:, at : at + piece]
        sq = u * u
        t = jnp.tanh(u * (c0 + (c0 * 0.044715) * sq))
        cdf = 0.5 + 0.5 * t
        hid_ref[:, at : at + piece] = (u * cdf).astype(bf16)
        slope = cdf + (0.5 * u) * (1.0 - t * t) * (c0 + (3.0 * 0.044715 * c0) * sq)
        slope_ref[:, at : at + piece] = slope.astype(bf16)


def hidden_layer(half, tokens, own, peer, out_bias, gain, shift, w_in, in_bias, before=()):
    tok, dim = tokens.shape
    width = w_in.shape[1]
    per = HALF // TILE
    glob = lambda n: pl.BlockSpec((TILE, n), lambda i: (i + per * half, 0))
    loc = lambda n: pl.BlockSpec((TILE, n), lambda i: (i, 0))
    return pl.pallas_call(
        hidden_kernel,
        grid=(per,),
        in_specs=[
            glob(dim),
            loc(dim),
            loc(dim),
            whole((1, dim)),
            whole((1, dim)),
            whole((1, dim)),
            whole(w_in.shape),
            whole((1, width)),
        ]
        + [pl.BlockSpec(memory_space=pl.ANY)] * len(before),
        out_specs=[glob(dim), glob(dim), glob(width), glob(width)],
        out_shape=[
            jax.ShapeDtypeStruct((tok, dim), f32),
            jax.ShapeDtypeStruct((tok, dim), bf16),
            jax.ShapeDtypeStruct((tok, width), bf16),
            jax.ShapeDtypeStruct((tok, width), bf16),
        ],
        input_output_aliases={8 + i: i for i in range(len(before))},
        compiler_params=params(40),
        cost_estimate=cost(2 * HALF * dim * width, HALF * (dim * 16 + width * 4) + w_in.size * 2, HALF * width),
        name="hidden_layer",
    )(tokens, own, peer, out_bias, gain, shift, w_in, in_bias, *before)


def matmul_kernel(a_ref, b_ref, o_ref):
    o_ref[...] = nn(a_ref[...], b_ref[...])


def rows_matmul(a, b):
    tok, depth = a.shape
    width = b.shape[1]
    return pl.pallas_call(
        matmul_kernel,
        grid=(tok // TILE,),
        in_specs=[pl.BlockSpec((TILE, depth), lambda i: (i, 0)), whole(b.shape)],
        out_specs=pl.BlockSpec((TILE, width), lambda i: (i, 0)),
        out_shape=jax.ShapeDtypeStruct((tok, width), f32),
        compiler_params=params(32),
        cost_estimate=cost(2 * tok * depth * width, tok * (depth * 2 + width * 4) + b.size * 2),
        name="mlp_out",
    )(a, b)


def hidden_back_kernel(g_ref, slope_ref, wb_ref, wi_ref, du_ref, dn_ref, db_ref, gb_ref):
    step = pl.program_id(0)
    grad = g_ref[...]
    width = slope_ref.shape[1]
    piece = 512
    total = None
    sums = []
    for at in range(0, width, piece):
        back = nt(grad, wb_ref[at : at + piece, :])
        du = (back * slope_ref[:, at : at + piece].astype(f32)).astype(bf16)
        du_ref[:, at : at + piece] = du
        sums.append(jnp.sum(du.astype(f32), 0, keepdims=True))
    dn_ref[...] = nt(du_ref[...], wi_ref[...])

    @pl.when(step == 0)
    def _():
        db_ref[...] = jnp.zeros_like(db_ref)
        gb_ref[...] = jnp.zeros_like(gb_ref)

    for i, at in enumerate(range(0, width, piece)):
        db_ref[:, at : at + piece] += sums[i]
    gb_ref[...] += jnp.sum(grad.astype(f32), 0, keepdims=True)


def hidden_back(cotangent, slope, w_back, w_in):
    tok, dim = cotangent.shape
    width = slope.shape[1]
    rows = lambda n: pl.BlockSpec((TILE, n), lambda i: (i, 0))
    return pl.pallas_call(
        hidden_back_kernel,
        grid=(tok // TILE,),
        in_specs=[rows(dim), rows(width), whole(w_back.shape), whole(w_in.shape)],
        out_specs=[rows(width), rows(dim), whole((1, width)), whole((1, dim))],
        out_shape=[
            jax.ShapeDtypeStruct((tok, width), bf16),
            jax.ShapeDtypeStruct((tok, dim), f32),
            jax.ShapeDtypeStruct((1, width), f32),
            jax.ShapeDtypeStruct((1, dim), f32),
        ],
        compiler_params=params(40),
        cost_estimate=cost(4 * tok * dim * width, tok * (dim * 6 + width * 4) + w_in.size * 4),
        name="hidden_back",
    )(cotangent, slope, w_back, w_in)


def middle_back_kernel(mid_ref, own_ref, peer_ref, g_ref, gain_ref, w_ref, dh_ref, dr_ref, do_ref, sum_ref):
    step = pl.program_id(0)
    unit, inv = standardize(mid_ref[...])
    grad = own_ref[...] + peer_ref[...]
    dh = g_ref[...].astype(f32) + norm_back(unit, inv, gain_ref[...], grad)
    dh_ref[...] = dh
    dr = dh.astype(bf16)
    dr_ref[...] = dr
    do_ref[...] = nt(dr, w_ref[...]).astype(bf16)

    @pl.when(step == 0)
    def _():
        sum_ref[...] = jnp.zeros_like(sum_ref)

    sum_ref[0:1] += jnp.sum(grad * unit, 0, keepdims=True)
    sum_ref[1:2] += jnp.sum(grad, 0, keepdims=True)
    sum_ref[2:3] += jnp.sum(dr.astype(f32), 0, keepdims=True)


def middle_back(middle, own, peer, cotangent, gain, w_out):
    tok, dim = middle.shape
    width = w_out.shape[0]
    rows = lambda n: pl.BlockSpec((TILE, n), lambda i: (i, 0))
    return pl.pallas_call(
        middle_back_kernel,
        grid=(tok // TILE,),
        in_specs=[rows(dim), rows(dim), rows(dim), rows(dim), whole((1, dim)), whole(w_out.shape)],
        out_specs=[rows(dim), rows(dim), rows(width), whole((8, dim))],
        out_shape=[
            jax.ShapeDtypeStruct((tok, dim), f32),
            jax.ShapeDtypeStruct((tok, dim), bf16),
            jax.ShapeDtypeStruct((tok, width), bf16),
            jax.ShapeDtypeStruct((8, dim), f32),
        ],
        compiler_params=params(32),
        cost_estimate=cost(2 * tok * dim * width, tok * (dim * 20 + width * 2) + w_out.size * 2),
        name="middle_back",
    )(middle, own, peer, cotangent, gain, w_out)


def attend_back_kernel(q_ref, k_ref, v_ref, do_ref, lse_ref, col_ref, row_ref, dq_ref, dk_ref, dv_ref, sum_ref, acc_k, acc_v):
    first = lax.broadcasted_iota(jnp.int32, (1, PAIR), 1) < HEAD_DIM
    zero = jnp.zeros((), bf16)
    for half in range(2):
        low, high = WINDOWS[half]
        span = slice(half * HALF, half * HALF + HALF)
        rows = q_ref[span, :]
        grads = do_ref[span, :]
        keys = k_ref[low:high, :]
        values = v_ref[low:high, :]
        logs = jnp.transpose(lse_ref[span, :])
        mask = jnp.where(col_ref[low:high, :] == row_ref[:, span], 0.0, -1000000000.0)
        parts = []
        for head in range(2):
            pick = lambda a: jnp.where(first, a, zero) if head == 0 else jnp.where(first, zero, a)
            lse = logs[head * HEAD_DIM : head * HEAD_DIM + 1, :]
            probs = jnp.exp(nt(keys, pick(rows)) + mask - lse)
            back = nt(values, pick(grads))
            inner = jnp.sum(probs * back, 0, keepdims=True)
            slant = (probs * (back - inner)).astype(bf16)
            dv = nn(probs.astype(bf16), grads)
            dk = nn(slant, rows)
            dq = tn(slant, keys)
            parts.append((dq, dk, dv))
        dq, dk, dv = (jnp.where(first, a, b) for a, b in zip(*parts))
        dq = (dq * HEAD_DIM ** (-0.5)).astype(bf16)
        dq_ref[span, :] = dq
        top = jnp.sum(dq.astype(f32), 0, keepdims=True)
        if half == 0:
            sum_ref[...] = jnp.zeros_like(sum_ref)
            acc_k[low:high, :] = dk
            acc_v[low:high, :] = dv
        else:
            edge = WINDOWS[0][1]
            acc_k[low:edge, :] += dk[: edge - low]
            acc_v[low:edge, :] += dv[: edge - low]
            acc_k[edge:high, :] = dk[edge - low :]
            acc_v[edge:high, :] = dv[edge - low :]
        sum_ref[0:1, :] += top
    dk_ref[...] = acc_k[...].astype(bf16)
    dv = acc_v[...].astype(bf16)
    dv_ref[...] = dv
    sum_ref[1:2, :] = jnp.sum(dv.astype(f32), 0, keepdims=True)


def attend_back(q, k, v, do, lse, ids_col, ids_row):
    tok, width = q.shape
    pair = pl.BlockSpec((tok, PAIR), lambda p: (0, p))
    out = jax.ShapeDtypeStruct((tok, width), bf16)
    return pl.pallas_call(
        attend_back_kernel,
        grid=(width // PAIR,),
        in_specs=[pair, pair, pair, pair, pair, whole((tok, 1)), whole((1, tok))],
        out_specs=[pair, pair, pair, pl.BlockSpec((8, PAIR), lambda p: (0, p))],
        out_shape=[out, out, out, jax.ShapeDtypeStruct((8, width), f32)],
        scratch_shapes=[pltpu.VMEM((tok, PAIR), f32), pltpu.VMEM((tok, PAIR), f32)],
        compiler_params=params(56),
        cost_estimate=cost(4 * 10 * tok * HALF * width, tok * width * 18),
        name="attend_back",
    )(q, k, v, do, lse, ids_col, ids_row)


def normed_back_kernel(dq_ref, dk_ref, dv_ref, w_ref, o_ref):
    o_ref[...] = nt(dq_ref[...], w_ref[0]) + nt(dk_ref[...], w_ref[1]) + nt(dv_ref[...], w_ref[2])


def normed_back(dq, dk, dv, w3):
    tok, width = dq.shape
    dim = w3.shape[1]
    rows = lambda n: pl.BlockSpec((TILE, n), lambda i: (i, 0))
    return pl.pallas_call(
        normed_back_kernel,
        grid=(tok // TILE,),
        in_specs=[rows(width), rows(width), rows(width), whole(w3.shape)],
        out_specs=rows(dim),
        out_shape=jax.ShapeDtypeStruct((tok, dim), f32),
        compiler_params=params(32),
        cost_estimate=cost(6 * tok * dim * width, tok * (dim * 4 + width * 6) + w3.size * 2),
        name="normed_back",
    )(dq, dk, dv, w3)


def input_back_kernel(x_ref, own_ref, peer_ref, dh_ref, gain_ref, o_ref, sum_ref):
    step = pl.program_id(0)
    unit, inv = standardize(x_ref[...].astype(f32))
    grad = own_ref[...] + peer_ref[...]
    o_ref[...] = (dh_ref[...] + norm_back(unit, inv, gain_ref[...], grad)).astype(bf16)

    @pl.when(step == 0)
    def _():
        sum_ref[...] = jnp.zeros_like(sum_ref)

    sum_ref[0:1] += jnp.sum(grad * unit, 0, keepdims=True)
    sum_ref[1:2] += jnp.sum(grad, 0, keepdims=True)


def input_back(tokens, own, peer, dh, gain):
    tok, dim = tokens.shape
    rows = pl.BlockSpec((TILE, dim), lambda i: (i, 0))
    return pl.pallas_call(
        input_back_kernel,
        grid=(tok // TILE,),
        in_specs=[rows, rows, rows, rows, whole((1, dim))],
        out_specs=[rows, whole((8, dim))],
        out_shape=[jax.ShapeDtypeStruct((tok, dim), bf16), jax.ShapeDtypeStruct((8, dim), f32)],
        compiler_params=params(32),
        cost_estimate=cost(20 * tok * dim, tok * dim * 16),
        name="input_back",
    )(tokens, own, peer, dh, gain)


def grad_kernel(parts, group, place_ref, a_ref, b_ref, *refs):
    outs, turned = refs[:parts], refs[parts]

    @pl.when(pl.program_id(0) == 0)
    def _():
        flat = jnp.transpose(a_ref[...])
        if group:
            for g in range(flat.shape[0] // group):
                at = pl.multiple_of(place_ref[g] * group, group)
                turned[pl.ds(at, group), :] = flat[g * group : (g + 1) * group, :]
        else:
            turned[...] = flat

    total = nn(turned[...], b_ref[...])
    rows = total.shape[0] // parts
    for i, out in enumerate(outs):
        out[...] = total[i * rows : (i + 1) * rows, :]


def weight_grad(parts, place, a, b):
    tok, dim = a.shape
    width = b.shape[1]
    step = 384
    count = place.shape[0]
    group = dim // count
    if group % 16:
        order = jnp.argsort(place)
        rows = (order[:, None] * group + jnp.arange(group)[None, :]).reshape(dim)
        a = jnp.take(a, rows, axis=1)
        group = 0
    rows = dim // parts
    return pl.pallas_call(
        functools.partial(grad_kernel, parts, group),
        grid_spec=pltpu.PrefetchScalarGridSpec(
            num_scalar_prefetch=1,
            grid=(width // step,),
            in_specs=[
                pl.BlockSpec((tok, dim), lambda i, *_: (0, 0)),
                pl.BlockSpec((tok, step), lambda i, *_: (0, i)),
            ],
            out_specs=[pl.BlockSpec((rows, step), lambda i, *_: (0, i))] * parts,
            scratch_shapes=[pltpu.VMEM((dim, tok), bf16)],
        ),
        out_shape=[jax.ShapeDtypeStruct((rows, width), f32)] * parts,
        compiler_params=params(40),
        cost_estimate=cost(2 * tok * dim * width, tok * (dim + width) * 2 + dim * width * 4),
        name="weight_grad",
    )(place, a, b)


class Exchange:
    def __init__(self, batch):
        side = 1
        while side * side * 4 < batch:
            side *= 2
        self.batch = batch
        sizes = (batch // (side * side), side, side)
        strides = (side * side, side, 1)
        axes = list(zip(sizes, strides))
        slow, mid, fast = axes
        self.orders = ((fast, mid, slow), (mid, fast, slow))
        me = lax.axis_index("batch")
        core = lax.axis_index("tp")
        away = jnp.arange(batch, dtype=jnp.int32) ^ me
        places = []
        for order in self.orders:
            place = jnp.zeros_like(away)
            for size, stride in order:
                place = place * size + (away // stride) % size
            places.append(place)
        self.place = jnp.where(core == 0, places[0], places[1]).astype(jnp.int32)

    def first_parts(self):
        return self.orders[0][0][0]

    def swap(self, block, phase, k):
        perm = []
        for i in range(self.batch):
            for core in range(2):
                _, stride = self.orders[core][phase]
                perm.append((2 * i + core, 2 * (i ^ (k * stride)) + core))
        return lax.ppermute(block, ("batch", "tp"), perm)

    def reduce(self, parts):
        for phase in range(3):
            got = [self.swap(parts[k], phase, k) for k in range(1, len(parts))]
            if phase == 2:
                total = parts[0]
                for g in got:
                    total = total + g
                return total
            size = self.orders[0][phase + 1][0]
            rows = parts[0].shape[0] // size
            cut = lambda a, i: lax.slice_in_dim(a, i * rows, (i + 1) * rows, axis=0)
            following = []
            for i in range(size):
                total = cut(parts[0], i)
                for g in got:
                    total = total + cut(g, i)
                following.append(total)
            parts = following


def other_core(values):
    return lax.ppermute(values, "tp", [(0, 1), (1, 0)])


def shards(
    tokens,
    seq_ids,
    cotangent,
    norm1_gain,
    norm1_shift,
    w_qkv,
    qv_bias,
    w_out,
    out_bias,
    norm2_gain,
    norm2_shift,
    w_in,
    in_bias,
    w_back,
    back_bias,
    batch,
):
    tok, dim = tokens.shape
    row = lambda a: a.reshape(1, -1)
    ids_col, ids_row = seq_ids.reshape(tok, 1), seq_ids.reshape(1, tok)
    w3 = jnp.transpose(w_qkv, (1, 0, 2))
    exchange = Exchange(batch)
    parts = exchange.first_parts()

    normed, q, k, v = project(tokens, row(norm1_gain), row(norm1_shift), w3, qv_bias)
    mixed, lse, part_a = attend(0, q, k, v, ids_col, ids_row, w_out)
    peer_a = other_core(part_a)
    mixed, lse, part_b = attend(1, q, k, v, ids_col, ids_row, w_out, (mixed, lse))
    peer_b = other_core(part_b)
    mlp = (row(out_bias), row(norm2_gain), row(norm2_shift), w_in, row(in_bias))
    state = hidden_layer(0, tokens, part_a, peer_a, *mlp)
    state = hidden_layer(1, tokens, part_b, peer_b, *mlp, before=tuple(state))
    middle, normed_two, hidden, slope = state

    back_parts = weight_grad(parts, exchange.place, cotangent, hidden)
    du, dn2, in_bias_sum, back_bias_sum = hidden_back(cotangent, slope, w_back, w_in)
    dn2_peer = other_core(dn2)
    in_parts = weight_grad(parts, exchange.place, normed_two, du)
    mlp_own = rows_matmul(hidden, w_back)
    mlp_peer = other_core(mlp_own)
    dh, dr, do, middle_sums = middle_back(middle, dn2, dn2_peer, cotangent, row(norm2_gain), w_out)
    out_parts = weight_grad(parts, exchange.place, dr, mixed)
    layer_out = (middle + (mlp_own + mlp_peer) + back_bias).astype(bf16)
    dq, dk, dv, qv_sums = attend_back(q, k, v, do, lse, ids_col, ids_row)
    q_parts = weight_grad(parts, exchange.place, normed, dq)
    k_parts = weight_grad(parts, exchange.place, normed, dk)
    v_parts = weight_grad(parts, exchange.place, normed, dv)
    dn1 = normed_back(dq, dk, dv, w3)
    dn1_peer = other_core(dn1)
    tokens_grad, input_sums = input_back(tokens, dn1, dn1_peer, dh, row(norm1_gain))

    w_back_grad = jnp.transpose(exchange.reduce(back_parts))
    w_in_grad = exchange.reduce(in_parts)
    w_out_grad = jnp.transpose(exchange.reduce(out_parts))
    w_qkv_grad = jnp.stack([exchange.reduce(p) for p in (q_parts, k_parts, v_parts)], 1)

    pieces = [input_sums[0], input_sums[1], middle_sums[2], middle_sums[0], middle_sums[1], back_bias_sum[0]]
    pieces += [qv_sums[0], qv_sums[1], in_bias_sum[0]]
    packed = jnp.concatenate([p.reshape(batch, -1) for p in pieces], 1)
    vectors = lax.psum_scatter(packed, "batch", scatter_dimension=0, tiled=True)[0]
    out, at = [], 0
    for p in pieces:
        n = p.shape[0] // batch
        out.append(vectors[at : at + n])
        at += n
    n1g, n1s, obg, n2g, n2s, bbg, qb, vb, ibg = out
    return (
        layer_out,
        tokens_grad,
        n1g,
        n1s,
        w_qkv_grad,
        jnp.stack([qb, vb]),
        w_out_grad,
        obg,
        n2g,
        n2s,
        w_in_grad,
        ibg,
        w_back_grad,
        bbg,
    )


def solution(mesh):
    in_specs = (
        P("batch", None),
        P("batch"),
        P("batch", None),
        P(),
        P(),
        P(None, None, "tp"),
        P(None, "tp"),
        P("tp", None),
        P(),
        P(),
        P(),
        P(None, "tp"),
        P("tp"),
        P("tp", None),
        P(),
    )
    out_specs = (
        P("batch", None),
        P("batch", None),
        P("batch"),
        P("batch"),
        P("batch", None, "tp"),
        P(None, ("tp", "batch")),
        P("tp", "batch"),
        P("batch"),
        P("batch"),
        P("batch"),
        P("batch", "tp"),
        P(("tp", "batch")),
        P("tp", "batch"),
        P("batch"),
    )
    body = functools.partial(shards, batch=mesh.shape["batch"])
    return jax.shard_map(body, mesh=mesh, in_specs=in_specs, out_specs=out_specs, check_vma=False)
```

```python
import functools

import jax
import jax.numpy as jnp
from jax import lax
from jax.experimental import pallas as pl
from jax.experimental.pallas import tpu as pltpu
from jax.sharding import PartitionSpec as P

HEAD_DIM = 64
PAIR = 2 * HEAD_DIM
HALF = 608
TILE = 304
LANES = 384
VMEM_LIMIT = 63 << 20
TILES = ((0, 256, 0, 608), (256, 352, 0, 688), (608, 256, 448, 1216), (864, 352, 608, 1216))
f32 = jnp.float32
bf16 = jnp.bfloat16


def params(mib):
    return pltpu.CompilerParams(vmem_limit_bytes=mib << 20)


def cost(flops, nbytes, trans=0):
    return pl.CostEstimate(flops=int(flops), bytes_accessed=int(nbytes), transcendentals=int(trans))


def nn(a, b):
    return jnp.dot(a, b, preferred_element_type=f32)


def nt(a, b):
    return lax.dot_general(a, b, (((1,), (1,)), ((), ())), preferred_element_type=f32)


def tn(a, b):
    return lax.dot_general(a, b, (((0,), (0,)), ((), ())), preferred_element_type=f32)


def standardize(values):
    center = values - jnp.mean(values, -1, keepdims=True)
    spread = jnp.mean(center * center, -1, keepdims=True)
    inv = lax.rsqrt(spread + 1e-06)
    return center * inv, inv


def norm_back(unit, inv, gain, grad):
    scaled = grad * gain
    return inv * (
        scaled
        - jnp.mean(scaled, -1, keepdims=True)
        - unit * jnp.mean(scaled * unit, -1, keepdims=True)
    )


def whole(shape):
    return pl.BlockSpec(shape, lambda *_: (0,) * len(shape))


def project_kernel(x_ref, gain_ref, shift_ref, w_ref, bias_ref, n_ref, q_ref, k_ref, v_ref):
    unit, _ = standardize(x_ref[...].astype(f32))
    normed = (unit * gain_ref[...] + shift_ref[...]).astype(bf16)
    n_ref[...] = normed
    scale = HEAD_DIM ** (-0.5)
    q_ref[...] = ((nn(normed, w_ref[0]) + bias_ref[0:1]).astype(bf16).astype(f32) * scale).astype(bf16)
    k_ref[...] = nn(normed, w_ref[1]).astype(bf16)
    v_ref[...] = (nn(normed, w_ref[2]) + bias_ref[1:2]).astype(bf16)


def project(tokens, gain, shift, w3, qv_bias):
    tok, dim = tokens.shape
    width = w3.shape[2]
    rows = lambda n: pl.BlockSpec((TILE, n), lambda i: (i, 0))
    out = jax.ShapeDtypeStruct((tok, width), bf16)
    return pl.pallas_call(
        project_kernel,
        grid=(tok // TILE,),
        in_specs=[rows(dim), whole((1, dim)), whole((1, dim)), whole(w3.shape), whole((2, width))],
        out_specs=[rows(dim), rows(width), rows(width), rows(width)],
        out_shape=[jax.ShapeDtypeStruct((tok, dim), bf16), out, out, out],
        compiler_params=params(60),
        cost_estimate=cost(2 * tok * dim * 3 * width, tok * (2 * dim + 3 * width) * 2 + w3.size * 2),
        name="project",
    )(tokens, gain, shift, w3, qv_bias)


def attend_kernel(half, q_ref, k_ref, v_ref, col_ref, row_ref, w_ref, *refs):
    o_ref, lse_ref, part_ref, *mask_refs = refs[-5:]
    step = pl.program_id(0)
    tiles = TILES[2 * half : 2 * half + 2]

    @pl.when(step == 0)
    def _():
        for (start, count, low, high), mask_ref in zip(tiles, mask_refs):
            at = start - half * HALF
            same = col_ref[at : at + count, :] == row_ref[:, low:high]
            mask_ref[...] = jnp.where(same, 0.0, -1000000000.0)

    first = lax.broadcasted_iota(jnp.int32, (1, PAIR), 1) < HEAD_DIM
    zero = jnp.zeros((), bf16)
    one = jnp.ones((), bf16)
    for tile, ((start, count, low, high), mask_ref) in enumerate(zip(tiles, mask_refs)):
        at = start - half * HALF
        rows = q_ref[at : at + count, :]
        keys = k_ref[low:high, :]
        values = v_ref[low:high, :]
        with_ones = (jnp.where(first, values, one), jnp.where(first, one, values))
        mask = mask_ref[...]
        outs, logs = [], []
        for head in range(2):
            own = jnp.where(first, rows, zero) if head == 0 else jnp.where(first, zero, rows)
            scores = nt(own, keys) + mask
            top = jnp.max(scores, -1, keepdims=True)
            expo = jnp.exp(scores - top).astype(bf16)
            mixed = nn(expo, with_ones[head])
            total = pltpu.roll(mixed, HEAD_DIM, 1)
            outs.append(mixed / total)
            logs.append(top + jnp.log(total))
        mixed = jnp.where(first, outs[0], outs[1]).astype(bf16)
        o_ref[at : at + count, :] = mixed
        turned = jnp.transpose(jnp.where(first, logs[0], logs[1]))
        lse_ref[tile, pl.ds(2 * step, 1), 0:count] = turned[0:1, :]
        lse_ref[tile, pl.ds(2 * step + 1, 1), 0:count] = turned[HEAD_DIM : HEAD_DIM + 1, :]
        part = nn(mixed, w_ref[...])

        @pl.when(step == 0)
        def _():
            part_ref[at : at + count, :] = part

        @pl.when(step > 0)
        def _():
            part_ref[at : at + count, :] += part


def attend(half, q, k, v, ids_col, ids_row, w_out, before=()):
    tok, width = q.shape
    dim = w_out.shape[1]
    pair_rows = pl.BlockSpec((HALF, PAIR), lambda p: (half, p))
    pair_all = pl.BlockSpec((tok, PAIR), lambda p: (0, p))
    tiles = TILES[2 * half : 2 * half + 2]
    return pl.pallas_call(
        functools.partial(attend_kernel, half),
        grid=(width // PAIR,),
        in_specs=[
            pair_rows,
            pair_all,
            pair_all,
            pl.BlockSpec((HALF, 1), lambda p: (half, 0)),
            whole((1, tok)),
            pl.BlockSpec((PAIR, dim), lambda p: (p, 0)),
        ]
        + [pl.BlockSpec(memory_space=pl.ANY)] * len(before),
        out_specs=[pair_rows, whole((2, 8, LANES)), whole((HALF, dim))],
        out_shape=[
            jax.ShapeDtypeStruct((tok, width), bf16),
            jax.ShapeDtypeStruct((2, 8, LANES), f32),
            jax.ShapeDtypeStruct((HALF, dim), f32),
        ],
        scratch_shapes=[pltpu.VMEM((count, high - low), f32) for _, count, low, high in tiles],
        input_output_aliases={6 + i: i for i in range(len(before))},
        compiler_params=params(60),
        cost_estimate=cost(16 * HALF * 650 * width, tok * width * 6 + HALF * dim * 4),
        name="attend",
    )(q, k, v, ids_col, ids_row, w_out, *before)


def hidden_kernel(x_ref, own_ref, peer_ref, ob_ref, gain_ref, shift_ref, w_ref, ib_ref, *refs):
    mid_ref, n_ref, hid_ref, slope_ref = refs[-4:]
    middle = x_ref[...].astype(f32) + (own_ref[...] + peer_ref[...]) + ob_ref[...]
    mid_ref[...] = middle
    unit, _ = standardize(middle)
    normed = (unit * gain_ref[...] + shift_ref[...]).astype(bf16)
    n_ref[...] = normed
    width = w_ref.shape[1]
    piece = 512
    c0 = 0.7978845608028654
    for at in range(0, width, piece):
        u = nn(normed, w_ref[:, at : at + piece]) + ib_ref[:, at : at + piece]
        sq = u * u
        t = jnp.tanh(u * (c0 + (c0 * 0.044715) * sq))
        cdf = 0.5 + 0.5 * t
        hid_ref[:, at : at + piece] = (u * cdf).astype(bf16)
        slope = cdf + (0.5 * u) * (1.0 - t * t) * (c0 + (3.0 * 0.044715 * c0) * sq)
        slope_ref[:, at : at + piece] = slope.astype(bf16)


def hidden_layer(half, tokens, own, peer, out_bias, gain, shift, w_in, in_bias, before=()):
    tok, dim = tokens.shape
    width = w_in.shape[1]
    per = HALF // TILE
    glob = lambda n: pl.BlockSpec((TILE, n), lambda i: (i + per * half, 0))
    loc = lambda n: pl.BlockSpec((TILE, n), lambda i: (i, 0))
    return pl.pallas_call(
        hidden_kernel,
        grid=(per,),
        in_specs=[
            glob(dim),
            loc(dim),
            loc(dim),
            whole((1, dim)),
            whole((1, dim)),
            whole((1, dim)),
            whole(w_in.shape),
            whole((1, width)),
        ]
        + [pl.BlockSpec(memory_space=pl.ANY)] * len(before),
        out_specs=[glob(dim), glob(dim), glob(width), glob(width)],
        out_shape=[
            jax.ShapeDtypeStruct((tok, dim), f32),
            jax.ShapeDtypeStruct((tok, dim), bf16),
            jax.ShapeDtypeStruct((tok, width), bf16),
            jax.ShapeDtypeStruct((tok, width), bf16),
        ],
        input_output_aliases={8 + i: i for i in range(len(before))},
        compiler_params=params(60),
        cost_estimate=cost(2 * HALF * dim * width, HALF * (dim * 16 + width * 4) + w_in.size * 2, HALF * width),
        name="hidden_layer",
    )(tokens, own, peer, out_bias, gain, shift, w_in, in_bias, *before)


def matmul_kernel(a_ref, b_ref, o_ref):
    o_ref[...] = nn(a_ref[...], b_ref[...])


def rows_matmul(a, b):
    tok, depth = a.shape
    width = b.shape[1]
    return pl.pallas_call(
        matmul_kernel,
        grid=(tok // TILE,),
        in_specs=[pl.BlockSpec((TILE, depth), lambda i: (i, 0)), whole(b.shape)],
        out_specs=pl.BlockSpec((TILE, width), lambda i: (i, 0)),
        out_shape=jax.ShapeDtypeStruct((tok, width), f32),
        compiler_params=params(60),
        cost_estimate=cost(2 * tok * depth * width, tok * (depth * 2 + width * 4) + b.size * 2),
        name="mlp_out",
    )(a, b)


def hidden_back_kernel(g_ref, slope_ref, wb_ref, wi_ref, du_ref, dn_ref, db_ref, gb_ref):
    step = pl.program_id(0)
    grad = g_ref[...]
    width = slope_ref.shape[1]
    piece = 512
    total = None
    sums = []
    for at in range(0, width, piece):
        back = nt(grad, wb_ref[at : at + piece, :])
        du = (back * slope_ref[:, at : at + piece].astype(f32)).astype(bf16)
        du_ref[:, at : at + piece] = du
        sums.append(jnp.sum(du.astype(f32), 0, keepdims=True))
    dn_ref[...] = nt(du_ref[...], wi_ref[...])

    @pl.when(step == 0)
    def _():
        db_ref[...] = jnp.zeros_like(db_ref)
        gb_ref[...] = jnp.zeros_like(gb_ref)

    for i, at in enumerate(range(0, width, piece)):
        db_ref[:, at : at + piece] += sums[i]
    gb_ref[...] += jnp.sum(grad.astype(f32), 0, keepdims=True)


def hidden_back(cotangent, slope, w_back, w_in):
    tok, dim = cotangent.shape
    width = slope.shape[1]
    rows = lambda n: pl.BlockSpec((TILE, n), lambda i: (i, 0))
    return pl.pallas_call(
        hidden_back_kernel,
        grid=(tok // TILE,),
        in_specs=[rows(dim), rows(width), whole(w_back.shape), whole(w_in.shape)],
        out_specs=[rows(width), rows(dim), whole((1, width)), whole((1, dim))],
        out_shape=[
            jax.ShapeDtypeStruct((tok, width), bf16),
            jax.ShapeDtypeStruct((tok, dim), f32),
            jax.ShapeDtypeStruct((1, width), f32),
            jax.ShapeDtypeStruct((1, dim), f32),
        ],
        compiler_params=params(60),
        cost_estimate=cost(4 * tok * dim * width, tok * (dim * 6 + width * 4) + w_in.size * 4),
        name="hidden_back",
    )(cotangent, slope, w_back, w_in)


def middle_back_kernel(mid_ref, own_ref, peer_ref, g_ref, gain_ref, w_ref, dh_ref, dr_ref, do_ref, sum_ref):
    step = pl.program_id(0)
    unit, inv = standardize(mid_ref[...])
    grad = own_ref[...] + peer_ref[...]
    dh = g_ref[...].astype(f32) + norm_back(unit, inv, gain_ref[...], grad)
    dh_ref[...] = dh
    dr = dh.astype(bf16)
    dr_ref[...] = dr
    do_ref[...] = nt(dr, w_ref[...]).astype(bf16)

    @pl.when(step == 0)
    def _():
        sum_ref[...] = jnp.zeros_like(sum_ref)

    sum_ref[0:1] += jnp.sum(grad * unit, 0, keepdims=True)
    sum_ref[1:2] += jnp.sum(grad, 0, keepdims=True)
    sum_ref[2:3] += jnp.sum(dr.astype(f32), 0, keepdims=True)


def middle_back(middle, own, peer, cotangent, gain, w_out):
    tok, dim = middle.shape
    width = w_out.shape[0]
    rows = lambda n: pl.BlockSpec((TILE, n), lambda i: (i, 0))
    return pl.pallas_call(
        middle_back_kernel,
        grid=(tok // TILE,),
        in_specs=[rows(dim), rows(dim), rows(dim), rows(dim), whole((1, dim)), whole(w_out.shape)],
        out_specs=[rows(dim), rows(dim), rows(width), whole((8, dim))],
        out_shape=[
            jax.ShapeDtypeStruct((tok, dim), f32),
            jax.ShapeDtypeStruct((tok, dim), bf16),
            jax.ShapeDtypeStruct((tok, width), bf16),
            jax.ShapeDtypeStruct((8, dim), f32),
        ],
        compiler_params=params(60),
        cost_estimate=cost(2 * tok * dim * width, tok * (dim * 20 + width * 2) + w_out.size * 2),
        name="middle_back",
    )(middle, own, peer, cotangent, gain, w_out)


def attend_back_tile(tile, keys, values, rows, grads, mask, lse_rows):
    first = lax.broadcasted_iota(jnp.int32, (1, PAIR), 1) < HEAD_DIM
    zero = jnp.zeros((), bf16)
    parts = []
    for head in range(2):
        pick = lambda a: jnp.where(first, a, zero) if head == 0 else jnp.where(first, zero, a)
        probs = jnp.exp(nt(keys, pick(rows)) + mask - lse_rows[head])
        back = nt(values, pick(grads))
        inner = jnp.sum(probs * back, 0, keepdims=True)
        slant = (probs * (back - inner)).astype(bf16)
        dv = nn(probs.astype(bf16), grads)
        dk = nn(slant, rows)
        dq = tn(slant, keys)
        parts.append((dq, dk, dv))
    dq, dk, dv = (jnp.where(first, a, b) for a, b in zip(*parts))
    return (dq * HEAD_DIM ** (-0.5)).astype(bf16), dk, dv


def attend_back_pair(q, k, v, do, lse, col_ref, row_ref, put_dq, acc_k, acc_v):
    total = None
    for tile, (start, count, low, high) in enumerate(TILES):
        span = slice(start, start + count)
        mask = jnp.where(col_ref[low:high, :] == row_ref[:, span], 0.0, -1000000000.0)
        dq, dk, dv = attend_back_tile(
            tile, k(slice(low, high)), v(slice(low, high)), q(span), do(span), mask, lse(tile, count)
        )
        put_dq(span, dq)
        top = jnp.sum(dq.astype(f32), 0, keepdims=True)
        total = top if total is None else total + top
        edge = 0 if tile == 0 else TILES[tile - 1][3]
        for acc, part in ((acc_k, dk), (acc_v, dv)):
            if edge > low:
                acc[low:edge, :] += part[: edge - low]
            if edge < high:
                acc[edge:high, :] = part[max(edge - low, 0) :]
    return total


def attend_back_kernel(q_ref, k_ref, v_ref, do_ref, lse_a, lse_b, col_ref, row_ref, dq_ref, dk_ref, dv_ref, sum_ref, acc_k, acc_v):
    step = pl.program_id(0)

    def lse(tile, count):
        ref = lse_a if tile < 2 else lse_b
        return [ref[tile % 2, pl.ds(2 * step + head, 1), 0:count] for head in range(2)]

    def put_dq(span, value):
        dq_ref[span, :] = value

    take = lambda ref: lambda span: ref[span, :]
    total = attend_back_pair(
        take(q_ref), take(k_ref), take(v_ref), take(do_ref), lse, col_ref, row_ref, put_dq, acc_k, acc_v
    )
    dk_ref[...] = acc_k[...].astype(bf16)
    dv = acc_v[...].astype(bf16)
    dv_ref[...] = dv
    sum_ref[...] = jnp.zeros_like(sum_ref)
    sum_ref[0:1, :] = total
    sum_ref[1:2, :] = jnp.sum(dv.astype(f32), 0, keepdims=True)


def attend_back(q, k, v, do, lse_a, lse_b, ids_col, ids_row):
    tok, width = q.shape
    pair = pl.BlockSpec((tok, PAIR), lambda p: (0, p))
    out = jax.ShapeDtypeStruct((tok, width), bf16)
    return pl.pallas_call(
        attend_back_kernel,
        grid=(width // PAIR,),
        in_specs=[pair, pair, pair, pair, whole(lse_a.shape), whole(lse_b.shape), whole((tok, 1)), whole((1, tok))],
        out_specs=[pair, pair, pair, pl.BlockSpec((8, PAIR), lambda p: (0, p))],
        out_shape=[out, out, out, jax.ShapeDtypeStruct((8, width), f32)],
        scratch_shapes=[pltpu.VMEM((tok, PAIR), f32), pltpu.VMEM((tok, PAIR), f32)],
        compiler_params=params(60),
        cost_estimate=cost(4 * 10 * tok * HALF * width, tok * width * 18),
        name="attend_back",
    )(q, k, v, do, lse_a, lse_b, ids_col, ids_row)


def normed_back_kernel(dq_ref, dk_ref, dv_ref, w_ref, o_ref):
    o_ref[...] = nt(dq_ref[...], w_ref[0]) + nt(dk_ref[...], w_ref[1]) + nt(dv_ref[...], w_ref[2])


def normed_back(dq, dk, dv, w3):
    tok, width = dq.shape
    dim = w3.shape[1]
    rows = lambda n: pl.BlockSpec((TILE, n), lambda i: (i, 0))
    return pl.pallas_call(
        normed_back_kernel,
        grid=(tok // TILE,),
        in_specs=[rows(width), rows(width), rows(width), whole(w3.shape)],
        out_specs=rows(dim),
        out_shape=jax.ShapeDtypeStruct((tok, dim), f32),
        compiler_params=params(60),
        cost_estimate=cost(6 * tok * dim * width, tok * (dim * 4 + width * 6) + w3.size * 2),
        name="normed_back",
    )(dq, dk, dv, w3)


def input_back_kernel(x_ref, own_ref, peer_ref, dh_ref, gain_ref, o_ref, sum_ref):
    step = pl.program_id(0)
    unit, inv = standardize(x_ref[...].astype(f32))
    grad = own_ref[...] + peer_ref[...]
    o_ref[...] = (dh_ref[...] + norm_back(unit, inv, gain_ref[...], grad)).astype(bf16)

    @pl.when(step == 0)
    def _():
        sum_ref[...] = jnp.zeros_like(sum_ref)

    sum_ref[0:1] += jnp.sum(grad * unit, 0, keepdims=True)
    sum_ref[1:2] += jnp.sum(grad, 0, keepdims=True)


def input_back(tokens, own, peer, dh, gain):
    tok, dim = tokens.shape
    rows = pl.BlockSpec((TILE, dim), lambda i: (i, 0))
    return pl.pallas_call(
        input_back_kernel,
        grid=(tok // TILE,),
        in_specs=[rows, rows, rows, rows, whole((1, dim))],
        out_specs=[rows, whole((8, dim))],
        out_shape=[jax.ShapeDtypeStruct((tok, dim), bf16), jax.ShapeDtypeStruct((8, dim), f32)],
        compiler_params=params(60),
        cost_estimate=cost(20 * tok * dim, tok * dim * 16),
        name="input_back",
    )(tokens, own, peer, dh, gain)


def grad_kernel(parts, group, place_ref, a_ref, b_ref, *refs):
    outs, turned = refs[:parts], refs[parts]

    @pl.when(pl.program_id(0) == 0)
    def _():
        flat = jnp.transpose(a_ref[...])
        if group:
            for g in range(flat.shape[0] // group):
                at = pl.multiple_of(place_ref[g] * group, group)
                turned[pl.ds(at, group), :] = flat[g * group : (g + 1) * group, :]
        else:
            turned[...] = flat

    total = nn(turned[...], b_ref[...])
    rows = total.shape[0] // parts
    for i, out in enumerate(outs):
        out[...] = total[i * rows : (i + 1) * rows, :]


def weight_grad(parts, place, a, b):
    tok, dim = a.shape
    width = b.shape[1]
    step = 384
    count = place.shape[0]
    group = dim // count
    if group % 16:
        order = jnp.argsort(place)
        rows = (order[:, None] * group + jnp.arange(group)[None, :]).reshape(dim)
        a = jnp.take(a, rows, axis=1)
        group = 0
    rows = dim // parts
    return pl.pallas_call(
        functools.partial(grad_kernel, parts, group),
        grid_spec=pltpu.PrefetchScalarGridSpec(
            num_scalar_prefetch=1,
            grid=(width // step,),
            in_specs=[
                pl.BlockSpec((tok, dim), lambda i, *_: (0, 0)),
                pl.BlockSpec((tok, step), lambda i, *_: (0, i)),
            ],
            out_specs=[pl.BlockSpec((rows, step), lambda i, *_: (0, i))] * parts,
            scratch_shapes=[pltpu.VMEM((dim, tok), bf16)],
        ),
        out_shape=[jax.ShapeDtypeStruct((rows, width), f32)] * parts,
        compiler_params=params(60),
        cost_estimate=cost(2 * tok * dim * width, tok * (dim + width) * 2 + dim * width * 4),
        name="weight_grad",
    )(place, a, b)


class Exchange:
    def __init__(self, batch):
        side = 1
        while side * side * 4 < batch:
            side *= 2
        self.batch = batch
        sizes = (batch // (side * side), side, side)
        strides = (side * side, side, 1)
        axes = list(zip(sizes, strides))
        slow, mid, fast = axes
        self.orders = ((fast, mid, slow), (mid, fast, slow))
        me = lax.axis_index("batch")
        core = lax.axis_index("tp")
        away = jnp.arange(batch, dtype=jnp.int32) ^ me
        places = []
        for order in self.orders:
            place = jnp.zeros_like(away)
            for size, stride in order:
                place = place * size + (away // stride) % size
            places.append(place)
        self.place = jnp.where(core == 0, places[0], places[1]).astype(jnp.int32)

    def first_parts(self):
        return self.orders[0][0][0]

    def swap(self, block, phase, k):
        perm = []
        for i in range(self.batch):
            for core in range(2):
                _, stride = self.orders[core][phase]
                perm.append((2 * i + core, 2 * (i ^ (k * stride)) + core))
        return lax.ppermute(block, ("batch", "tp"), perm)

    def reduce(self, parts):
        for phase in range(3):
            got = [self.swap(parts[k], phase, k) for k in range(1, len(parts))]
            if phase == 2:
                total = parts[0]
                for g in got:
                    total = total + g
                return total
            size = self.orders[0][phase + 1][0]
            rows = parts[0].shape[0] // size
            cut = lambda a, i: lax.slice_in_dim(a, i * rows, (i + 1) * rows, axis=0)
            following = []
            for i in range(size):
                total = cut(parts[0], i)
                for g in got:
                    total = total + cut(g, i)
                following.append(total)
            parts = following


def other_core(values):
    return lax.ppermute(values, "tp", [(0, 1), (1, 0)])


COUNT = 12
SLOTS = 9
STEPS = 4


class Route:
    def __init__(self):
        self.me = lax.axis_index("batch")
        self.core = lax.axis_index("tp")
        self.bits = {s: lax.rem(self.me // s, 2) for s in (1, 2, 4, 8)}
        near = {s: self.me + s * (1 - 2 * self.bits[s]) for s in (1, 2, 4, 8)}
        core = self.core
        side = near[1] * (1 - core) + near[2] * core
        other = near[2] * (1 - core) + near[1] * core
        self.plain = (side, other, near[4], near[8])
        self.turned = (near[4], side, other, near[8])
        self.plain_weight = {1: 8 - 4 * core, 2: 4 + 4 * core, 4: 2, 8: 1}
        self.turned_weight = {4: 8, 1: 4 - 2 * core, 2: 2 + 2 * core, 8: 1}

    def kind(self, chunk):
        return lax.rem(chunk, 3) // 2

    def partner(self, chunk, step):
        kind = self.kind(chunk)
        return self.plain[step] + kind * (self.turned[step] - self.plain[step])

    def places(self, chunk):
        kind = self.kind(chunk)
        terms = {}
        for s in (1, 2, 4, 8):
            weight = self.plain_weight[s] + kind * (self.turned_weight[s] - self.plain_weight[s])
            terms[s] = (self.bits[s] * weight, (1 - self.bits[s]) * weight)
        return [sum(terms[s][(g // s) % 2] for s in (1, 2, 4, 8)) for g in range(16)]


def tail_kernel(
    g_h, hid_h, slope_h, n2_h, mid_h, wi_h, wb_h, wo_h, w3_h, q_h, k_h, v_h, o_h, n1_h, tok_h,
    lse_a, lse_b, col_ref, row_ref, gain1_ref, gain2_ref, bb_ref,
    layer_h, input_h, grads_h, sums_ref,
    buf_h, buf_d, buf_n, buf_g, buf_t, buf_m, own, peer, wi, wb, wo, stage, acc_k, acc_v,
    chunks, recv0, recv1, recv2, recv3, sums_in,
    load_sem, stage_sem, send_sem, recv_sem, grad_sem, swap_send, swap_recv, sums_send, sums_recv, put_sem, free_sem,
):
    mesh_id = pl.DeviceIdType.MESH
    route = Route()
    me, core = route.me, route.core
    tok, dim = buf_g.shape
    width = buf_h.shape[1]
    third = q_h.shape[1]
    tiles = tok // TILE
    recvs = (recv0, recv1, recv2, recv3)

    barrier = pltpu.get_barrier_semaphore()
    for other in route.plain:
        pl.semaphore_signal(barrier, inc=1, device_id=(other, core), device_id_type=mesh_id)
    pl.semaphore_signal(barrier, inc=1, device_id=(me, 1 - core), device_id_type=mesh_id)

    def load(source, target, at):
        return pltpu.make_async_copy(source, target, load_sem.at[at])

    first_loads = [
        load(g_h, buf_g, 0),
        load(hid_h, buf_h, 1),
        load(wb_h, wb, 2),
        load(slope_h, buf_d, 3),
        load(wi_h, wi, 4),
        load(n2_h, buf_n, 5),
        load(mid_h, buf_m, 6),
        load(wo_h, wo, 7),
    ]
    for item in first_loads:
        item.start()


    def slot_of(chunk):
        return lax.rem(chunk, SLOTS)

    def hop(chunk, step):
        half = 8 >> step
        return pltpu.make_async_remote_copy(
            src_ref=chunks.at[slot_of(chunk), pl.ds(half, half)],
            dst_ref=recvs[step].at[chunk],
            send_sem=send_sem.at[step, chunk],
            recv_sem=recv_sem.at[step, chunk],
            device_id=(route.partner(chunk, step), core),
            device_id_type=mesh_id,
        )

    def deliver(chunk):
        return pltpu.make_async_copy(chunks.at[slot_of(chunk), 0], grads_h.at[chunk], grad_sem.at[chunk])

    def finish(chunk, step):
        got = hop(chunk, step)
        got.wait_send()
        got.wait_recv()
        slot = slot_of(chunk)

        def add(g, carry):
            chunks[slot, g] += recvs[step][chunk, g]
            return carry

        lax.fori_loop(0, 8 >> step, add, 0)
        if step < STEPS - 1:
            hop(chunk, step + 1).start()
        else:
            deliver(chunk).start()

    def tick(at, known=True):
        for step in range(STEPS - 1, -1, -1):
            if not known or 0 <= at - step < COUNT:
                finish(at - step, step)

    def gradient(chunk, right):
        places = route.places(chunk)
        slot = slot_of(chunk)
        total = nn(buf_t[...], right)
        rows = dim // 16
        for g in range(16):
            chunks[slot, places[g]] = total[g * rows : (g + 1) * rows, :]

    def turn(source):
        def body(i, carry):
            at = pl.multiple_of(i * PAIR, PAIR)
            buf_t[pl.ds(at, PAIR), :] = jnp.transpose(source[:, pl.ds(at, PAIR)])
            return carry

        lax.fori_loop(0, dim // PAIR, body, 0)

    def columns(ref, at):
        return ref[:, pl.ds(pl.multiple_of(at, PAIR), LANES)]

    def rows_of(i):
        return pl.ds(pl.multiple_of(i * TILE, TILE), TILE)


    def swap(turn_at, i):
        return pltpu.make_async_remote_copy(
            src_ref=own.at[rows_of(i)],
            dst_ref=peer.at[rows_of(i)],
            send_sem=swap_send.at[turn_at, i],
            recv_sem=swap_recv.at[turn_at, i],
            device_id=(me, 1 - core),
            device_id_type=mesh_id,
        )

    def swapped(turn_at, i):
        got = swap(turn_at, i)
        got.wait_send()
        got.wait_recv()
        return own[rows_of(i), :] + peer[rows_of(i), :]

    def peer_is_free():
        pl.semaphore_signal(free_sem, inc=1, device_id=(me, 1 - core), device_id_type=mesh_id)


    first_loads[0].wait()
    turn(buf_g)
    pl.semaphore_wait(barrier, STEPS + 1)
    first_loads[1].wait()
    for chunk in range(1):

        def body(i, carry):
            gradient(i, columns(buf_h, i * LANES))
            hop(i, 0).start()
            return carry

        lax.fori_loop(0, 4, body, 0)


    sums_ref[...] = jnp.zeros_like(sums_ref)
    for item in first_loads[2:5]:
        item.wait()

    def body(i, carry):
        grad = buf_g[rows_of(i), :]
        for at in range(0, width, 512):
            back = nt(grad, wb[at : at + 512, :])
            du = (back * buf_d[rows_of(i), at : at + 512].astype(f32)).astype(bf16)
            buf_d[rows_of(i), at : at + 512] = du
            sums_ref[4:5, at : at + 512] += jnp.sum(du.astype(f32), 0, keepdims=True)
        own[rows_of(i), :] = nt(buf_d[rows_of(i), :], wi[...])
        swap(0, i).start()
        sums_ref[2:3, dim : 2 * dim] += jnp.sum(grad.astype(f32), 0, keepdims=True)
        return carry

    lax.fori_loop(0, tiles, body, 0)


    first_loads[5].wait()
    turn(buf_n)
    late_load = [load(w3_h.at[c], wi.at[:, pl.ds(c * third, third)], 8 + c) for c in range(3)]
    for item in late_load:
        item.start()

    def body(i, carry):
        gradient(4 + i, columns(buf_d, i * LANES))
        return carry

    lax.fori_loop(0, 2, body, 0)
    hop(4, 0).start()
    hop(5, 0).start()
    tick(0)

    def body(i, carry):
        gradient(6 + i, columns(buf_d, i * LANES + 2 * LANES))
        return carry

    lax.fori_loop(0, 2, body, 0)
    hop(6, 0).start()
    tick(1)
    hop(7, 0).start()


    first_loads[6].wait()
    first_loads[7].wait()

    def body(i, carry):
        grad = swapped(0, i)
        unit, inv = standardize(buf_m[rows_of(i), :])
        dh = buf_g[rows_of(i), :].astype(f32) + norm_back(unit, inv, gain2_ref[...], grad)
        buf_m[rows_of(i), :] = dh
        dr = dh.astype(bf16)
        buf_n[rows_of(i), :] = dr
        buf_d[rows_of(i), 0:third] = nt(dr, wo[...]).astype(bf16)
        sums_ref[1:2, dim : 2 * dim] += jnp.sum(grad * unit, 0, keepdims=True)
        sums_ref[2:3, 0:dim] += jnp.sum(grad, 0, keepdims=True)
        sums_ref[1:2, 0:dim] += jnp.sum(dr.astype(f32), 0, keepdims=True)
        return carry

    lax.fori_loop(0, tiles, body, 0)
    peer_is_free()
    tick(2)


    def fetch(i):
        return pltpu.make_async_copy(mid_h.at[rows_of(i)], stage.at[lax.rem(i, 2)], stage_sem.at[lax.rem(i, 2)])

    fetch(0).start()
    turn(buf_n)
    n1_load = load(n1_h, buf_n, 11)
    n1_load.start()
    pl.semaphore_wait(free_sem, 1)

    def body(i, carry):
        own[rows_of(i), :] = nn(buf_h[rows_of(i), :], wb[...])
        swap(1, i).start()
        return carry

    lax.fori_loop(0, tiles, body, 0)
    heads_load = [load(ref, buf_h.at[:, pl.ds(c * third, third)], 12 + c) for c, ref in enumerate((q_h, k_h, v_h, o_h))]
    for item in heads_load:
        item.start()

    def body(i, carry):
        @pl.when(i + 1 < tiles)
        def _():
            fetch(i + 1).start()

        fetch(i).wait()
        buf_g[rows_of(i), :] = (stage[lax.rem(i, 2)] + swapped(1, i) + bb_ref[...]).astype(bf16)
        return carry

    lax.fori_loop(0, tiles, body, 0)
    peer_is_free()
    layer_put = pltpu.make_async_copy(buf_g, layer_h, put_sem.at[0])
    layer_put.start()


    for item in heads_load:
        item.wait()
    gradient(8, buf_h[:, 3 * third : 4 * third])
    tick(3)
    hop(8, 0).start()
    layer_put.wait()
    tok_load = load(tok_h, buf_g, 16)
    tok_load.start()


    def body(p, carry):
        def take(ref, block):
            at = pl.multiple_of(block * third + p * PAIR, PAIR)
            return lambda span: ref[span, pl.ds(at, PAIR)]

        def put(block):
            at = pl.multiple_of(block * third + p * PAIR, PAIR)

            def store(span, value):
                buf_d[span, pl.ds(at, PAIR)] = value

            return store

        def lse(tile, count):
            ref = lse_a if tile < 2 else lse_b
            return [ref[tile % 2, pl.ds(2 * p + head, 1), 0:count] for head in range(2)]

        total = attend_back_pair(
            take(buf_h, 0), take(buf_h, 1), take(buf_h, 2), take(buf_d, 0), lse, col_ref, row_ref, put(1), acc_k, acc_v
        )
        put(2)(slice(0, tok), acc_k[...].astype(bf16))
        dv = acc_v[...].astype(bf16)
        put(3)(slice(0, tok), dv)
        lane = pl.multiple_of(p * PAIR, PAIR)
        sums_ref[3:4, pl.ds(lane, PAIR)] = total
        sums_ref[3:4, pl.ds(pl.multiple_of(third + p * PAIR, PAIR), PAIR)] = jnp.sum(dv.astype(f32), 0, keepdims=True)
        tick(4 + p, known=False)
        return carry

    lax.fori_loop(0, third // PAIR, body, 0)


    for item in late_load:
        item.wait()
    pl.semaphore_wait(free_sem, 1)

    def body(i, carry):
        own[rows_of(i), :] = nt(buf_d[rows_of(i), third : 4 * third], wi[:, 0 : 3 * third])
        swap(2, i).start()
        return carry

    lax.fori_loop(0, tiles, body, 0)
    n1_load.wait()
    turn(buf_n)
    for chunk in range(COUNT - SLOTS):
        deliver(chunk).wait()

    def body(i, carry):
        gradient(9 + i, columns(buf_d, i * LANES + third))
        hop(9 + i, 0).start()
        return carry

    lax.fori_loop(0, 3, body, 0)
    tick(7)


    tok_load.wait()

    def body(i, carry):
        grad = swapped(2, i)
        unit, inv = standardize(buf_g[rows_of(i), :].astype(f32))
        buf_g[rows_of(i), :] = (buf_m[rows_of(i), :] + norm_back(unit, inv, gain1_ref[...], grad)).astype(bf16)
        sums_ref[0:1, 0:dim] += jnp.sum(grad * unit, 0, keepdims=True)
        sums_ref[0:1, dim : 2 * dim] += jnp.sum(grad, 0, keepdims=True)
        return carry

    lax.fori_loop(0, tiles, body, 0)
    input_put = pltpu.make_async_copy(buf_g, input_h, put_sem.at[1])
    input_put.start()


    def whole_hop(step):
        return pltpu.make_async_remote_copy(
            src_ref=sums_ref,
            dst_ref=sums_in.at[step],
            send_sem=sums_send.at[step],
            recv_sem=sums_recv.at[step],
            device_id=(route.plain[step], core),
            device_id_type=mesh_id,
        )

    for step in range(STEPS):
        whole_hop(step).start()
        tick(8 + step)
        whole_hop(step).wait()
        sums_ref[...] += sums_in[step]
    for at in range(8 + STEPS, COUNT + STEPS - 1):
        tick(at)
    for chunk in range(COUNT - SLOTS, COUNT):
        deliver(chunk).wait()
    input_put.wait()


def tail(g, hid, slope, n2, mid, wi, wb, wo, w3, q, k, v, o, n1, tokens, lse_a, lse_b, col, row, gain1, gain2, bb):
    tok, dim = g.shape
    width = hid.shape[1]
    third = q.shape[1]
    rows = dim // 16
    hbm = pl.BlockSpec(memory_space=pl.ANY)
    vmem = pl.BlockSpec(memory_space=pltpu.VMEM)
    dma = pltpu.SemaphoreType.DMA
    return pl.pallas_call(
        tail_kernel,
        in_specs=[hbm] * 15 + [vmem] * 7,
        out_specs=[hbm, hbm, hbm, vmem],
        out_shape=[
            jax.ShapeDtypeStruct((tok, dim), bf16),
            jax.ShapeDtypeStruct((tok, dim), bf16),
            jax.ShapeDtypeStruct((COUNT, rows, LANES), f32),
            jax.ShapeDtypeStruct((8, width), f32),
        ],
        scratch_shapes=[
            pltpu.VMEM((tok, width), bf16),
            pltpu.VMEM((tok, width), bf16),
            pltpu.VMEM((tok, dim), bf16),
            pltpu.VMEM((tok, dim), bf16),
            pltpu.VMEM((dim, tok), bf16),
            pltpu.VMEM((tok, dim), f32),
            pltpu.VMEM((tok, dim), f32),
            pltpu.VMEM((tok, dim), f32),
            pltpu.VMEM((dim, width), bf16),
            pltpu.VMEM((width, dim), bf16),
            pltpu.VMEM((third, dim), bf16),
            pltpu.VMEM((2, TILE, dim), f32),
            pltpu.VMEM((tok, PAIR), f32),
            pltpu.VMEM((tok, PAIR), f32),
            pltpu.VMEM((SLOTS, 16, rows, LANES), f32),
            pltpu.VMEM((COUNT, 8, rows, LANES), f32),
            pltpu.VMEM((COUNT, 4, rows, LANES), f32),
            pltpu.VMEM((COUNT, 2, rows, LANES), f32),
            pltpu.VMEM((COUNT, 1, rows, LANES), f32),
            pltpu.VMEM((STEPS, 8, width), f32),
            dma((17,)),
            dma((2,)),
            dma((STEPS, COUNT)),
            dma((STEPS, COUNT)),
            dma((COUNT,)),
            dma((3, tok // TILE)),
            dma((3, tok // TILE)),
            dma((STEPS,)),
            dma((STEPS,)),
            dma((2,)),
            pltpu.SemaphoreType.REGULAR,
        ],
        compiler_params=pltpu.CompilerParams(vmem_limit_bytes=VMEM_LIMIT, collective_id=0, has_side_effects=True),
        cost_estimate=cost(24e9, 40e6),
        name="tail",
    )(g, hid, slope, n2, mid, wi, wb, wo, w3, q, k, v, o, n1, tokens, lse_a, lse_b, col, row, gain1, gain2, bb)


def shards(
    tokens,
    seq_ids,
    cotangent,
    norm1_gain,
    norm1_shift,
    w_qkv,
    qv_bias,
    w_out,
    out_bias,
    norm2_gain,
    norm2_shift,
    w_in,
    in_bias,
    w_back,
    back_bias,
    batch,
):
    tok, dim = tokens.shape
    row = lambda a: a.reshape(1, -1)
    ids_col, ids_row = seq_ids.reshape(tok, 1), seq_ids.reshape(1, tok)
    w3 = jnp.transpose(w_qkv, (1, 0, 2))
    exchange = Exchange(batch)
    parts = exchange.first_parts()

    normed, q, k, v = project(tokens, row(norm1_gain), row(norm1_shift), w3, qv_bias)
    mixed, lse_a, part_a = attend(0, q, k, v, ids_col, ids_row, w_out)
    peer_a = other_core(part_a)
    mixed, lse_b, part_b = attend(1, q, k, v, ids_col, ids_row, w_out, (mixed,))
    peer_b = other_core(part_b)
    mlp = (row(out_bias), row(norm2_gain), row(norm2_shift), w_in, row(in_bias))
    state = hidden_layer(0, tokens, part_a, peer_a, *mlp)
    state = hidden_layer(1, tokens, part_b, peer_b, *mlp, before=tuple(state))
    middle, normed_two, hidden, slope = state

    if batch == 16:
        layer_out, tokens_grad, grads, sums = tail(
            cotangent, hidden, slope, normed_two, middle, w_in, w_back, w_out, w3, q, k, v, mixed, normed, tokens,
            lse_a, lse_b, ids_col, ids_row, row(norm1_gain), row(norm2_gain), row(back_bias),
        )
        wide = lambda part: jnp.transpose(part, (0, 2, 1)).reshape(-1, dim // batch)
        w_back_grad = wide(grads[0:4])
        w_in_grad = jnp.transpose(grads[4:8], (1, 0, 2)).reshape(dim // batch, -1)
        w_out_grad = wide(grads[8:9])
        w_qkv_grad = jnp.transpose(grads[9:12], (1, 0, 2))
        third = q.shape[1]
        pieces = [sums[0, :dim], sums[0, dim:], sums[1, :dim], sums[1, dim:], sums[2, :dim], sums[2, dim:]]
        pieces += [sums[3, :third], sums[3, third : 2 * third], sums[4]]
        packed = jnp.concatenate([p.reshape(batch, -1) for p in pieces], 1)
        vectors = lax.dynamic_index_in_dim(packed, lax.axis_index("batch"), 0, keepdims=False)
    else:
        back_parts = weight_grad(parts, exchange.place, cotangent, hidden)
        du, dn2, in_bias_sum, back_bias_sum = hidden_back(cotangent, slope, w_back, w_in)
        dn2_peer = other_core(dn2)
        in_parts = weight_grad(parts, exchange.place, normed_two, du)
        mlp_own = rows_matmul(hidden, w_back)
        mlp_peer = other_core(mlp_own)
        dh, dr, do, middle_sums = middle_back(middle, dn2, dn2_peer, cotangent, row(norm2_gain), w_out)
        out_parts = weight_grad(parts, exchange.place, dr, mixed)
        layer_out = (middle + (mlp_own + mlp_peer) + back_bias).astype(bf16)
        dq, dk, dv, qv_sums = attend_back(q, k, v, do, lse_a, lse_b, ids_col, ids_row)
        qkv_parts = [weight_grad(parts, exchange.place, normed, a) for a in (dq, dk, dv)]
        dn1 = normed_back(dq, dk, dv, w3)
        dn1_peer = other_core(dn1)
        tokens_grad, input_sums = input_back(tokens, dn1, dn1_peer, dh, row(norm1_gain))

        w_back_grad = jnp.transpose(exchange.reduce(back_parts))
        w_in_grad = exchange.reduce(in_parts)
        w_out_grad = jnp.transpose(exchange.reduce(out_parts))
        w_qkv_grad = jnp.stack([exchange.reduce(p) for p in qkv_parts], 1)

        pieces = [input_sums[0], input_sums[1], middle_sums[2], middle_sums[0], middle_sums[1], back_bias_sum[0]]
        pieces += [qv_sums[0], qv_sums[1], in_bias_sum[0]]
        packed = jnp.concatenate([p.reshape(batch, -1) for p in pieces], 1)
        vectors = lax.psum_scatter(packed, "batch", scatter_dimension=0, tiled=True)[0]
    out, at = [], 0
    for p in pieces:
        n = p.shape[0] // batch
        out.append(vectors[at : at + n])
        at += n
    n1g, n1s, obg, n2g, n2s, bbg, qb, vb, ibg = out
    return (
        layer_out,
        tokens_grad,
        n1g,
        n1s,
        w_qkv_grad,
        jnp.stack([qb, vb]),
        w_out_grad,
        obg,
        n2g,
        n2s,
        w_in_grad,
        ibg,
        w_back_grad,
        bbg,
    )


def solution(mesh):
    in_specs = (
        P("batch", None),
        P("batch"),
        P("batch", None),
        P(),
        P(),
        P(None, None, "tp"),
        P(None, "tp"),
        P("tp", None),
        P(),
        P(),
        P(),
        P(None, "tp"),
        P("tp"),
        P("tp", None),
        P(),
    )
    out_specs = (
        P("batch", None),
        P("batch", None),
        P("batch"),
        P("batch"),
        P("batch", None, "tp"),
        P(None, ("tp", "batch")),
        P("tp", "batch"),
        P("batch"),
        P("batch"),
        P("batch"),
        P("batch", "tp"),
        P(("tp", "batch")),
        P("tp", "batch"),
        P("batch"),
    )
    body = functools.partial(shards, batch=mesh.shape["batch"])
    return jax.shard_map(body, mesh=mesh, in_specs=in_specs, out_specs=out_specs, check_vma=False)
```

```python
import functools

import jax
import jax.numpy as jnp
from jax import lax
from jax.experimental import pallas as pl
from jax.experimental.pallas import tpu as pltpu
from jax.sharding import PartitionSpec as P

HEAD_DIM = 64
PAIR = 2 * HEAD_DIM
HALF = 608
TILE = 304
LANES = 384
VMEM_LIMIT = 63 << 20
TILES = ((0, 256, 0, 608), (256, 352, 0, 688), (608, 256, 448, 1216), (864, 352, 608, 1216))
f32 = jnp.float32
bf16 = jnp.bfloat16


def params(mib):
    return pltpu.CompilerParams(vmem_limit_bytes=mib << 20)


def cost(flops, nbytes, trans=0):
    return pl.CostEstimate(flops=int(flops), bytes_accessed=int(nbytes), transcendentals=int(trans))


def nn(a, b):
    return jnp.dot(a, b, preferred_element_type=f32)


def nt(a, b):
    return lax.dot_general(a, b, (((1,), (1,)), ((), ())), preferred_element_type=f32)


def tn(a, b):
    return lax.dot_general(a, b, (((0,), (0,)), ((), ())), preferred_element_type=f32)


def standardize(values):
    center = values - jnp.mean(values, -1, keepdims=True)
    spread = jnp.mean(center * center, -1, keepdims=True)
    inv = lax.rsqrt(spread + 1e-06)
    return center * inv, inv


def norm_back(unit, inv, gain, grad):
    scaled = grad * gain
    return inv * (
        scaled
        - jnp.mean(scaled, -1, keepdims=True)
        - unit * jnp.mean(scaled * unit, -1, keepdims=True)
    )


def whole(shape):
    return pl.BlockSpec(shape, lambda *_: (0,) * len(shape))


def project_kernel(x_ref, gain_ref, shift_ref, w_ref, bias_ref, n_ref, q_ref, k_ref, v_ref):
    unit, _ = standardize(x_ref[...].astype(f32))
    normed = (unit * gain_ref[...] + shift_ref[...]).astype(bf16)
    n_ref[...] = normed
    scale = HEAD_DIM ** (-0.5)
    q_ref[...] = ((nn(normed, w_ref[0]) + bias_ref[0:1]).astype(bf16).astype(f32) * scale).astype(bf16)
    k_ref[...] = nn(normed, w_ref[1]).astype(bf16)
    v_ref[...] = (nn(normed, w_ref[2]) + bias_ref[1:2]).astype(bf16)


def project(tokens, gain, shift, w3, qv_bias):
    tok, dim = tokens.shape
    width = w3.shape[2]
    rows = lambda n: pl.BlockSpec((TILE, n), lambda i: (i, 0))
    out = jax.ShapeDtypeStruct((tok, width), bf16)
    return pl.pallas_call(
        project_kernel,
        grid=(tok // TILE,),
        in_specs=[rows(dim), whole((1, dim)), whole((1, dim)), whole(w3.shape), whole((2, width))],
        out_specs=[rows(dim), rows(width), rows(width), rows(width)],
        out_shape=[jax.ShapeDtypeStruct((tok, dim), bf16), out, out, out],
        compiler_params=params(60),
        cost_estimate=cost(2 * tok * dim * 3 * width, tok * (2 * dim + 3 * width) * 2 + w3.size * 2),
        name="project",
    )(tokens, gain, shift, w3, qv_bias)


def attend_kernel(half, q_ref, k_ref, v_ref, col_ref, row_ref, w_ref, *refs):
    o_ref, lse_ref, part_ref, *mask_refs = refs[-5:]
    step = pl.program_id(0)
    tiles = TILES[2 * half : 2 * half + 2]

    @pl.when(step == 0)
    def _():
        for (start, count, low, high), mask_ref in zip(tiles, mask_refs):
            at = start - half * HALF
            same = col_ref[at : at + count, :] == row_ref[:, low:high]
            mask_ref[...] = jnp.where(same, 0.0, -1000000000.0)

    first = lax.broadcasted_iota(jnp.int32, (1, PAIR), 1) < HEAD_DIM
    zero = jnp.zeros((), bf16)
    one = jnp.ones((), bf16)
    for tile, ((start, count, low, high), mask_ref) in enumerate(zip(tiles, mask_refs)):
        at = start - half * HALF
        rows = q_ref[at : at + count, :]
        keys = k_ref[low:high, :]
        values = v_ref[low:high, :]
        with_ones = (jnp.where(first, values, one), jnp.where(first, one, values))
        mask = mask_ref[...]
        outs, logs = [], []
        for head in range(2):
            own = jnp.where(first, rows, zero) if head == 0 else jnp.where(first, zero, rows)
            scores = nt(own, keys) + mask
            top = jnp.max(scores, -1, keepdims=True)
            expo = jnp.exp(scores - top).astype(bf16)
            mixed = nn(expo, with_ones[head])
            total = pltpu.roll(mixed, HEAD_DIM, 1)
            outs.append(mixed / total)
            logs.append(top + jnp.log(total))
        mixed = jnp.where(first, outs[0], outs[1]).astype(bf16)
        o_ref[at : at + count, :] = mixed
        turned = jnp.transpose(jnp.where(first, logs[0], logs[1]))
        lse_ref[tile, pl.ds(2 * step, 1), 0:count] = turned[0:1, :]
        lse_ref[tile, pl.ds(2 * step + 1, 1), 0:count] = turned[HEAD_DIM : HEAD_DIM + 1, :]
        part = nn(mixed, w_ref[...])

        @pl.when(step == 0)
        def _():
            part_ref[at : at + count, :] = part

        @pl.when(step > 0)
        def _():
            part_ref[at : at + count, :] += part


def attend(half, q, k, v, ids_col, ids_row, w_out, before=()):
    tok, width = q.shape
    dim = w_out.shape[1]
    pair_rows = pl.BlockSpec((HALF, PAIR), lambda p: (half, p))
    pair_all = pl.BlockSpec((tok, PAIR), lambda p: (0, p))
    tiles = TILES[2 * half : 2 * half + 2]
    return pl.pallas_call(
        functools.partial(attend_kernel, half),
        grid=(width // PAIR,),
        in_specs=[
            pair_rows,
            pair_all,
            pair_all,
            pl.BlockSpec((HALF, 1), lambda p: (half, 0)),
            whole((1, tok)),
            pl.BlockSpec((PAIR, dim), lambda p: (p, 0)),
        ]
        + [pl.BlockSpec(memory_space=pl.ANY)] * len(before),
        out_specs=[pair_rows, whole((2, 8, LANES)), whole((HALF, dim))],
        out_shape=[
            jax.ShapeDtypeStruct((tok, width), bf16),
            jax.ShapeDtypeStruct((2, 8, LANES), f32),
            jax.ShapeDtypeStruct((HALF, dim), f32),
        ],
        scratch_shapes=[pltpu.VMEM((count, high - low), f32) for _, count, low, high in tiles],
        input_output_aliases={6 + i: i for i in range(len(before))},
        compiler_params=params(60),
        cost_estimate=cost(16 * HALF * 650 * width, tok * width * 6 + HALF * dim * 4),
        name="attend",
    )(q, k, v, ids_col, ids_row, w_out, *before)


def hidden_kernel(x_ref, own_ref, peer_ref, ob_ref, gain_ref, shift_ref, w_ref, ib_ref, *refs):
    mid_ref, n_ref, hid_ref, slope_ref = refs[-4:]
    middle = x_ref[...].astype(f32) + (own_ref[...] + peer_ref[...]) + ob_ref[...]
    mid_ref[...] = middle
    unit, _ = standardize(middle)
    normed = (unit * gain_ref[...] + shift_ref[...]).astype(bf16)
    n_ref[...] = normed
    width = w_ref.shape[1]
    piece = 512
    c0 = 0.7978845608028654
    for at in range(0, width, piece):
        u = nn(normed, w_ref[:, at : at + piece]) + ib_ref[:, at : at + piece]
        sq = u * u
        t = jnp.tanh(u * (c0 + (c0 * 0.044715) * sq))
        cdf = 0.5 + 0.5 * t
        hid_ref[:, at : at + piece] = (u * cdf).astype(bf16)
        slope = cdf + (0.5 * u) * (1.0 - t * t) * (c0 + (3.0 * 0.044715 * c0) * sq)
        slope_ref[:, at : at + piece] = slope.astype(bf16)


def hidden_layer(half, tokens, own, peer, out_bias, gain, shift, w_in, in_bias, before=()):
    tok, dim = tokens.shape
    width = w_in.shape[1]
    per = HALF // TILE
    glob = lambda n: pl.BlockSpec((TILE, n), lambda i: (i + per * half, 0))
    loc = lambda n: pl.BlockSpec((TILE, n), lambda i: (i, 0))
    return pl.pallas_call(
        hidden_kernel,
        grid=(per,),
        in_specs=[
            glob(dim),
            loc(dim),
            loc(dim),
            whole((1, dim)),
            whole((1, dim)),
            whole((1, dim)),
            whole(w_in.shape),
            whole((1, width)),
        ]
        + [pl.BlockSpec(memory_space=pl.ANY)] * len(before),
        out_specs=[glob(dim), glob(dim), glob(width), glob(width)],
        out_shape=[
            jax.ShapeDtypeStruct((tok, dim), f32),
            jax.ShapeDtypeStruct((tok, dim), bf16),
            jax.ShapeDtypeStruct((tok, width), bf16),
            jax.ShapeDtypeStruct((tok, width), bf16),
        ],
        input_output_aliases={8 + i: i for i in range(len(before))},
        compiler_params=params(60),
        cost_estimate=cost(2 * HALF * dim * width, HALF * (dim * 16 + width * 4) + w_in.size * 2, HALF * width),
        name="hidden_layer",
    )(tokens, own, peer, out_bias, gain, shift, w_in, in_bias, *before)


def matmul_kernel(a_ref, b_ref, o_ref):
    o_ref[...] = nn(a_ref[...], b_ref[...])


def rows_matmul(a, b):
    tok, depth = a.shape
    width = b.shape[1]
    return pl.pallas_call(
        matmul_kernel,
        grid=(tok // TILE,),
        in_specs=[pl.BlockSpec((TILE, depth), lambda i: (i, 0)), whole(b.shape)],
        out_specs=pl.BlockSpec((TILE, width), lambda i: (i, 0)),
        out_shape=jax.ShapeDtypeStruct((tok, width), f32),
        compiler_params=params(60),
        cost_estimate=cost(2 * tok * depth * width, tok * (depth * 2 + width * 4) + b.size * 2),
        name="mlp_out",
    )(a, b)


def hidden_back_kernel(g_ref, slope_ref, wb_ref, wi_ref, du_ref, dn_ref, db_ref, gb_ref):
    step = pl.program_id(0)
    grad = g_ref[...]
    width = slope_ref.shape[1]
    piece = 512
    total = None
    sums = []
    for at in range(0, width, piece):
        back = nt(grad, wb_ref[at : at + piece, :])
        du = (back * slope_ref[:, at : at + piece].astype(f32)).astype(bf16)
        du_ref[:, at : at + piece] = du
        sums.append(jnp.sum(du.astype(f32), 0, keepdims=True))
    dn_ref[...] = nt(du_ref[...], wi_ref[...])

    @pl.when(step == 0)
    def _():
        db_ref[...] = jnp.zeros_like(db_ref)
        gb_ref[...] = jnp.zeros_like(gb_ref)

    for i, at in enumerate(range(0, width, piece)):
        db_ref[:, at : at + piece] += sums[i]
    gb_ref[...] += jnp.sum(grad.astype(f32), 0, keepdims=True)


def hidden_back(cotangent, slope, w_back, w_in):
    tok, dim = cotangent.shape
    width = slope.shape[1]
    rows = lambda n: pl.BlockSpec((TILE, n), lambda i: (i, 0))
    return pl.pallas_call(
        hidden_back_kernel,
        grid=(tok // TILE,),
        in_specs=[rows(dim), rows(width), whole(w_back.shape), whole(w_in.shape)],
        out_specs=[rows(width), rows(dim), whole((1, width)), whole((1, dim))],
        out_shape=[
            jax.ShapeDtypeStruct((tok, width), bf16),
            jax.ShapeDtypeStruct((tok, dim), f32),
            jax.ShapeDtypeStruct((1, width), f32),
            jax.ShapeDtypeStruct((1, dim), f32),
        ],
        compiler_params=params(60),
        cost_estimate=cost(4 * tok * dim * width, tok * (dim * 6 + width * 4) + w_in.size * 4),
        name="hidden_back",
    )(cotangent, slope, w_back, w_in)


def middle_back_kernel(mid_ref, own_ref, peer_ref, g_ref, gain_ref, w_ref, dh_ref, dr_ref, do_ref, sum_ref):
    step = pl.program_id(0)
    unit, inv = standardize(mid_ref[...])
    grad = own_ref[...] + peer_ref[...]
    dh = g_ref[...].astype(f32) + norm_back(unit, inv, gain_ref[...], grad)
    dh_ref[...] = dh
    dr = dh.astype(bf16)
    dr_ref[...] = dr
    do_ref[...] = nt(dr, w_ref[...]).astype(bf16)

    @pl.when(step == 0)
    def _():
        sum_ref[...] = jnp.zeros_like(sum_ref)

    sum_ref[0:1] += jnp.sum(grad * unit, 0, keepdims=True)
    sum_ref[1:2] += jnp.sum(grad, 0, keepdims=True)
    sum_ref[2:3] += jnp.sum(dr.astype(f32), 0, keepdims=True)


def middle_back(middle, own, peer, cotangent, gain, w_out):
    tok, dim = middle.shape
    width = w_out.shape[0]
    rows = lambda n: pl.BlockSpec((TILE, n), lambda i: (i, 0))
    return pl.pallas_call(
        middle_back_kernel,
        grid=(tok // TILE,),
        in_specs=[rows(dim), rows(dim), rows(dim), rows(dim), whole((1, dim)), whole(w_out.shape)],
        out_specs=[rows(dim), rows(dim), rows(width), whole((8, dim))],
        out_shape=[
            jax.ShapeDtypeStruct((tok, dim), f32),
            jax.ShapeDtypeStruct((tok, dim), bf16),
            jax.ShapeDtypeStruct((tok, width), bf16),
            jax.ShapeDtypeStruct((8, dim), f32),
        ],
        compiler_params=params(60),
        cost_estimate=cost(2 * tok * dim * width, tok * (dim * 20 + width * 2) + w_out.size * 2),
        name="middle_back",
    )(middle, own, peer, cotangent, gain, w_out)


def attend_back_tile(tile, keys, values, rows, grads, mask, lse_rows):
    first = lax.broadcasted_iota(jnp.int32, (1, PAIR), 1) < HEAD_DIM
    zero = jnp.zeros((), bf16)
    parts = []
    for head in range(2):
        pick = lambda a: jnp.where(first, a, zero) if head == 0 else jnp.where(first, zero, a)
        probs = jnp.exp(nt(keys, pick(rows)) + mask - lse_rows[head])
        back = nt(values, pick(grads))
        inner = jnp.sum(probs * back, 0, keepdims=True)
        slant = (probs * (back - inner)).astype(bf16)
        dv = nn(probs.astype(bf16), grads)
        dk = nn(slant, rows)
        dq = tn(slant, keys)
        parts.append((dq, dk, dv))
    dq, dk, dv = (jnp.where(first, a, b) for a, b in zip(*parts))
    return (dq * HEAD_DIM ** (-0.5)).astype(bf16), dk, dv


def attend_back_pair(q, k, v, do, lse, col_ref, row_ref, put_dq, acc_k, acc_v, after=lambda tile: None):
    total = None
    for tile, (start, count, low, high) in enumerate(TILES):
        span = slice(start, start + count)
        mask = jnp.where(col_ref[low:high, 0:1] == row_ref[:, span], 0.0, -1000000000.0)
        dq, dk, dv = attend_back_tile(
            tile, k(slice(low, high)), v(slice(low, high)), q(span), do(span), mask, lse(tile, count)
        )
        put_dq(span, dq)
        top = jnp.sum(dq.astype(f32), 0, keepdims=True)
        total = top if total is None else total + top
        edge = 0 if tile == 0 else TILES[tile - 1][3]
        for acc, part in ((acc_k, dk), (acc_v, dv)):
            if edge > low:
                acc[low:edge, :] += part[: edge - low]
            if edge < high:
                acc[edge:high, :] = part[max(edge - low, 0) :]
        after(tile)
    return total


def attend_back_kernel(q_ref, k_ref, v_ref, do_ref, lse_a, lse_b, col_ref, row_ref, dq_ref, dk_ref, dv_ref, sum_ref, acc_k, acc_v):
    step = pl.program_id(0)

    def lse(tile, count):
        ref = lse_a if tile < 2 else lse_b
        return [ref[tile % 2, pl.ds(2 * step + head, 1), 0:count] for head in range(2)]

    def put_dq(span, value):
        dq_ref[span, :] = value

    take = lambda ref: lambda span: ref[span, :]
    total = attend_back_pair(
        take(q_ref), take(k_ref), take(v_ref), take(do_ref), lse, col_ref, row_ref, put_dq, acc_k, acc_v
    )
    dk_ref[...] = acc_k[...].astype(bf16)
    dv = acc_v[...].astype(bf16)
    dv_ref[...] = dv
    sum_ref[...] = jnp.zeros_like(sum_ref)
    sum_ref[0:1, :] = total
    sum_ref[1:2, :] = jnp.sum(dv.astype(f32), 0, keepdims=True)


def attend_back(q, k, v, do, lse_a, lse_b, ids_col, ids_row):
    tok, width = q.shape
    pair = pl.BlockSpec((tok, PAIR), lambda p: (0, p))
    out = jax.ShapeDtypeStruct((tok, width), bf16)
    return pl.pallas_call(
        attend_back_kernel,
        grid=(width // PAIR,),
        in_specs=[pair, pair, pair, pair, whole(lse_a.shape), whole(lse_b.shape), whole((tok, 1)), whole((1, tok))],
        out_specs=[pair, pair, pair, pl.BlockSpec((8, PAIR), lambda p: (0, p))],
        out_shape=[out, out, out, jax.ShapeDtypeStruct((8, width), f32)],
        scratch_shapes=[pltpu.VMEM((tok, PAIR), f32), pltpu.VMEM((tok, PAIR), f32)],
        compiler_params=params(60),
        cost_estimate=cost(4 * 10 * tok * HALF * width, tok * width * 18),
        name="attend_back",
    )(q, k, v, do, lse_a, lse_b, ids_col, ids_row)


def normed_back_kernel(dq_ref, dk_ref, dv_ref, w_ref, o_ref):
    o_ref[...] = nt(dq_ref[...], w_ref[0]) + nt(dk_ref[...], w_ref[1]) + nt(dv_ref[...], w_ref[2])


def normed_back(dq, dk, dv, w3):
    tok, width = dq.shape
    dim = w3.shape[1]
    rows = lambda n: pl.BlockSpec((TILE, n), lambda i: (i, 0))
    return pl.pallas_call(
        normed_back_kernel,
        grid=(tok // TILE,),
        in_specs=[rows(width), rows(width), rows(width), whole(w3.shape)],
        out_specs=rows(dim),
        out_shape=jax.ShapeDtypeStruct((tok, dim), f32),
        compiler_params=params(60),
        cost_estimate=cost(6 * tok * dim * width, tok * (dim * 4 + width * 6) + w3.size * 2),
        name="normed_back",
    )(dq, dk, dv, w3)


def input_back_kernel(x_ref, own_ref, peer_ref, dh_ref, gain_ref, o_ref, sum_ref):
    step = pl.program_id(0)
    unit, inv = standardize(x_ref[...].astype(f32))
    grad = own_ref[...] + peer_ref[...]
    o_ref[...] = (dh_ref[...] + norm_back(unit, inv, gain_ref[...], grad)).astype(bf16)

    @pl.when(step == 0)
    def _():
        sum_ref[...] = jnp.zeros_like(sum_ref)

    sum_ref[0:1] += jnp.sum(grad * unit, 0, keepdims=True)
    sum_ref[1:2] += jnp.sum(grad, 0, keepdims=True)


def input_back(tokens, own, peer, dh, gain):
    tok, dim = tokens.shape
    rows = pl.BlockSpec((TILE, dim), lambda i: (i, 0))
    return pl.pallas_call(
        input_back_kernel,
        grid=(tok // TILE,),
        in_specs=[rows, rows, rows, rows, whole((1, dim))],
        out_specs=[rows, whole((8, dim))],
        out_shape=[jax.ShapeDtypeStruct((tok, dim), bf16), jax.ShapeDtypeStruct((8, dim), f32)],
        compiler_params=params(60),
        cost_estimate=cost(20 * tok * dim, tok * dim * 16),
        name="input_back",
    )(tokens, own, peer, dh, gain)


def grad_kernel(parts, group, place_ref, a_ref, b_ref, *refs):
    outs, turned = refs[:parts], refs[parts]

    @pl.when(pl.program_id(0) == 0)
    def _():
        flat = jnp.transpose(a_ref[...])
        if group:
            for g in range(flat.shape[0] // group):
                at = pl.multiple_of(place_ref[g] * group, group)
                turned[pl.ds(at, group), :] = flat[g * group : (g + 1) * group, :]
        else:
            turned[...] = flat

    total = nn(turned[...], b_ref[...])
    rows = total.shape[0] // parts
    for i, out in enumerate(outs):
        out[...] = total[i * rows : (i + 1) * rows, :]


def weight_grad(parts, place, a, b):
    tok, dim = a.shape
    width = b.shape[1]
    step = 384
    count = place.shape[0]
    group = dim // count
    if group % 16:
        order = jnp.argsort(place)
        rows = (order[:, None] * group + jnp.arange(group)[None, :]).reshape(dim)
        a = jnp.take(a, rows, axis=1)
        group = 0
    rows = dim // parts
    return pl.pallas_call(
        functools.partial(grad_kernel, parts, group),
        grid_spec=pltpu.PrefetchScalarGridSpec(
            num_scalar_prefetch=1,
            grid=(width // step,),
            in_specs=[
                pl.BlockSpec((tok, dim), lambda i, *_: (0, 0)),
                pl.BlockSpec((tok, step), lambda i, *_: (0, i)),
            ],
            out_specs=[pl.BlockSpec((rows, step), lambda i, *_: (0, i))] * parts,
            scratch_shapes=[pltpu.VMEM((dim, tok), bf16)],
        ),
        out_shape=[jax.ShapeDtypeStruct((rows, width), f32)] * parts,
        compiler_params=params(60),
        cost_estimate=cost(2 * tok * dim * width, tok * (dim + width) * 2 + dim * width * 4),
        name="weight_grad",
    )(place, a, b)


class Exchange:
    def __init__(self, batch):
        side = 1
        while side * side * 4 < batch:
            side *= 2
        self.batch = batch
        sizes = (batch // (side * side), side, side)
        strides = (side * side, side, 1)
        axes = list(zip(sizes, strides))
        slow, mid, fast = axes
        self.orders = ((fast, mid, slow), (mid, fast, slow))
        me = lax.axis_index("batch")
        core = lax.axis_index("tp")
        away = jnp.arange(batch, dtype=jnp.int32) ^ me
        places = []
        for order in self.orders:
            place = jnp.zeros_like(away)
            for size, stride in order:
                place = place * size + (away // stride) % size
            places.append(place)
        self.place = jnp.where(core == 0, places[0], places[1]).astype(jnp.int32)

    def first_parts(self):
        return self.orders[0][0][0]

    def swap(self, block, phase, k):
        perm = []
        for i in range(self.batch):
            for core in range(2):
                _, stride = self.orders[core][phase]
                perm.append((2 * i + core, 2 * (i ^ (k * stride)) + core))
        return lax.ppermute(block, ("batch", "tp"), perm)

    def reduce(self, parts):
        for phase in range(3):
            got = [self.swap(parts[k], phase, k) for k in range(1, len(parts))]
            if phase == 2:
                total = parts[0]
                for g in got:
                    total = total + g
                return total
            size = self.orders[0][phase + 1][0]
            rows = parts[0].shape[0] // size
            cut = lambda a, i: lax.slice_in_dim(a, i * rows, (i + 1) * rows, axis=0)
            following = []
            for i in range(size):
                total = cut(parts[0], i)
                for g in got:
                    total = total + cut(g, i)
                following.append(total)
            parts = following


def other_core(values):
    return lax.ppermute(values, "tp", [(0, 1), (1, 0)])


COUNT = 12
STEPS = 4
ARRIVALS = (
    (9, 0, 0), (16.9, 0, 1), (17.4, 2, 0), (18.6, 1, 0), (26.5, 1, 1), (28.2, 3, 0),
    (30.2, 5, 0), (33.4, 0, 2), (36.2, 3, 1), (37.8, 4, 0), (45.8, 4, 1), (46.2, 8, 0),
    (47.4, 6, 0), (49.4, 1, 2), (51.7, 0, 3), (54.9, 3, 2), (55.4, 6, 1), (57, 7, 0),
    (58.1, 4, 2), (60.3, 1, 3), (61.9, 2, 1), (62.6, 3, 3), (65, 7, 1), (65.8, 6, 2),
    (68.2, 2, 2), (68.3, 5, 1), (73, 5, 2), (73.1, 8, 1), (77.8, 8, 2), (78.6, 11, 0),
    (80.8, 4, 3), (81.1, 9, 0), (84, 7, 2), (86.3, 6, 3), (88.5, 2, 3), (89, 9, 1),
    (90.7, 10, 0), (90.8, 5, 3), (93, 8, 3), (95.3, 7, 3), (95.6, 11, 1), (97.1, 10, 1),
    (98.5, 9, 2), (98.7, 11, 2), (101.9, 10, 2), (104.1, 9, 3), (106.4, 11, 3), (108.6, 10, 3),
)


class Route:
    def __init__(self):
        self.me = lax.axis_index("batch")
        self.core = lax.axis_index("tp")
        self.bits = {s: lax.rem(self.me // s, 2) for s in (1, 2, 4, 8)}
        near = {s: self.me + s * (1 - 2 * self.bits[s]) for s in (1, 2, 4, 8)}
        core = self.core
        side = near[1] * (1 - core) + near[2] * core
        other = near[2] * (1 - core) + near[1] * core
        self.plain = (side, other, near[4], near[8])
        self.turned = (near[4], side, other, near[8])
        self.plain_weight = {1: 8 - 4 * core, 2: 4 + 4 * core, 4: 2, 8: 1}
        self.turned_weight = {4: 8, 1: 4 - 2 * core, 2: 2 + 2 * core, 8: 1}

    def kind(self, chunk):
        return lax.rem(chunk, 3) // 2

    def partner(self, chunk, step):
        kind = self.kind(chunk)
        return self.plain[step] + kind * (self.turned[step] - self.plain[step])

    def places(self, chunk):
        kind = self.kind(chunk)
        terms = {}
        for s in (1, 2, 4, 8):
            weight = self.plain_weight[s] + kind * (self.turned_weight[s] - self.plain_weight[s])
            terms[s] = (self.bits[s] * weight, (1 - self.bits[s]) * weight)
        return [sum(terms[s][(g // s) % 2] for s in (1, 2, 4, 8)) for g in range(16)]


def attend_tile(rows, keys, values, mask):
    first = lax.broadcasted_iota(jnp.int32, (1, PAIR), 1) < HEAD_DIM
    zero = jnp.zeros((), bf16)
    one = jnp.ones((), bf16)
    outs, logs = [], []
    for head in range(2):
        own = jnp.where(first, rows, zero) if head == 0 else jnp.where(first, zero, rows)
        with_ones = jnp.where(first, values, one) if head == 0 else jnp.where(first, one, values)
        scores = nt(own, keys) + mask
        top = jnp.max(scores, -1, keepdims=True)
        mixed = nn(jnp.exp(scores - top).astype(bf16), with_ones)
        total = pltpu.roll(mixed, HEAD_DIM, 1)
        outs.append(mixed / total)
        logs.append(top + jnp.log(total))
    return jnp.where(first, outs[0], outs[1]).astype(bf16), jnp.where(first, logs[0], logs[1])


def layer_kernel(
    tok_h, g_h, w3_h, wo_h, wi_h, wb_h,
    ids_ref, gain1_ref, shift1_ref, qvb_ref, ob_ref, gain2_ref, shift2_ref, ib_ref, bb_ref,
    layer_h, input_h, grads_h, sums_ref, heads_h, dh_h,
    buf_h, buf_d, buf_n, buf_g, buf_t, buf_m, own, peer, wi, wb, wo, acc_k, acc_v, col_ref, row_ref, lse_ref,
    chunks, recv0, recv1, recv2, recv3, sums_in,
    load_sem, send_sem, recv_sem, grad_sem, swap_send, swap_recv, sums_send, sums_recv, put_sem, free_sem,
):
    mesh_id = pl.DeviceIdType.MESH
    route = Route()
    me, core = route.me, route.core
    tok, dim = buf_g.shape
    width = buf_h.shape[1]
    third = wo.shape[0]
    tiles = tok // TILE
    recvs = (recv0, recv1, recv2, recv3)
    vector = lambda ref: ref[...].reshape(1, -1)

    barrier = pltpu.get_barrier_semaphore()
    for other in route.plain:
        pl.semaphore_signal(barrier, inc=1, device_id=(other, core), device_id_type=mesh_id)
    pl.semaphore_signal(barrier, inc=1, device_id=(me, 1 - core), device_id_type=mesh_id)

    def load(source, target, at):
        copy = pltpu.make_async_copy(source, target, load_sem.at[at])
        copy.start()
        return copy

    tok_load = load(tok_h, buf_d.at[:, pl.ds(0, dim)], 0)
    w3_places = (wb.at[pl.ds(0, dim), pl.ds(0, third)], wb.at[pl.ds(0, dim), pl.ds(third, third)], wb.at[pl.ds(dim, dim), pl.ds(0, third)])
    w3_load = [load(w3_h.at[c], w3_places[c], 1 + c) for c in range(3)]
    wo_load = load(wo_h, wo, 4)
    g_load = load(g_h, buf_g, 5)
    wi_load = load(wi_h, wi, 6)


    def hop(chunk, step):
        half = 8 >> step
        return pltpu.make_async_remote_copy(
            src_ref=chunks.at[chunk, pl.ds(half, half)],
            dst_ref=recvs[step].at[chunk],
            send_sem=send_sem.at[step, chunk],
            recv_sem=recv_sem.at[step, chunk],
            device_id=(route.partner(chunk, step), core),
            device_id_type=mesh_id,
        )

    def deliver(chunk):
        return pltpu.make_async_copy(chunks.at[chunk, 0], grads_h.at[chunk], grad_sem.at[chunk])

    def finish(chunk, step):
        got = hop(chunk, step)
        got.wait_send()
        got.wait_recv()

        def add(g, carry):
            chunks[chunk, g] += recvs[step][chunk, g]
            return carry

        lax.fori_loop(0, 8 >> step, add, 0)
        if step < STEPS - 1:
            hop(chunk, step + 1).start()
        else:
            deliver(chunk).start()

    left = list(ARRIVALS)

    def arrivals(until):
        while left and left[0][0] <= until:
            _, chunk, step = left.pop(0)
            finish(chunk, step)

    def gradient(chunk, right):
        places = route.places(chunk)
        total = nn(buf_t[...], right)
        rows = dim // 16
        for g in range(16):
            chunks[chunk, places[g]] = total[g * rows : (g + 1) * rows, :]
        hop(chunk, 0).start()

    def turn(source):
        def body(i, carry):
            at = pl.multiple_of(i * PAIR, PAIR)
            buf_t[pl.ds(at, PAIR), :] = jnp.transpose(source[:, pl.ds(at, PAIR)])
            return carry

        lax.fori_loop(0, dim // PAIR, body, 0)

    def columns(ref, at):
        return ref[:, pl.ds(pl.multiple_of(at, PAIR), LANES)]

    def rows_of(i):
        return pl.ds(pl.multiple_of(i * TILE, TILE), TILE)


    def swap(turn_at, i, rows):
        return pltpu.make_async_remote_copy(
            src_ref=own.at[rows],
            dst_ref=peer.at[rows],
            send_sem=swap_send.at[turn_at, i],
            recv_sem=swap_recv.at[turn_at, i],
            device_id=(me, 1 - core),
            device_id_type=mesh_id,
        )

    def swapped(turn_at, i):
        got = swap(turn_at, i, rows_of(i))
        got.wait_send()
        got.wait_recv()
        return own[rows_of(i), :] + peer[rows_of(i), :]

    def peer_is_free():
        pl.semaphore_signal(free_sem, inc=1, device_id=(me, 1 - core), device_id_type=mesh_id)


    row_ref[...] = vector(ids_ref)
    col_ref[...] = jnp.transpose(jnp.broadcast_to(vector(ids_ref), (PAIR, tok)))
    sums_ref[...] = jnp.zeros_like(sums_ref)
    tok_load.wait()
    for item in w3_load:
        item.wait()

    def first_norm(values):
        unit, inv = standardize(values.astype(f32))
        return unit, inv, (unit * vector(gain1_ref) + vector(shift1_ref)).astype(bf16)

    def body(i, carry):
        _, _, normed = first_norm(buf_d[rows_of(i), 0:dim])
        query = (nn(normed, wb[0:dim, 0:third]) + qvb_ref[0:1, :]).astype(bf16)
        buf_h[rows_of(i), 0:third] = (query.astype(f32) * HEAD_DIM ** (-0.5)).astype(bf16)
        buf_h[rows_of(i), third : 2 * third] = nn(normed, wb[0:dim, third : 2 * third]).astype(bf16)
        buf_h[rows_of(i), 2 * third : 3 * third] = (nn(normed, wb[dim:, 0:third]) + qvb_ref[1:2, :]).astype(bf16)
        return carry

    lax.fori_loop(0, tiles, body, 0)
    wb_load = load(wb_h, wb, 7)
    save_qkv = load(buf_h.at[:, pl.ds(0, 3 * third)], heads_h.at[:, pl.ds(0, 3 * third)], 8)


    wo_load.wait()
    for tile, (start, count, low, high) in enumerate(TILES):
        span = slice(start, start + count)
        mask = jnp.where(col_ref[span, 0:1] == row_ref[:, low:high], 0.0, -1000000000.0)

        def body(p, carry):
            pick = lambda block: pl.ds(pl.multiple_of(block * third + p * PAIR, PAIR), PAIR)
            mixed, logs = attend_tile(
                buf_h[span, pick(0)], buf_h[low:high, pick(1)], buf_h[low:high, pick(2)], mask
            )
            buf_h[span, pick(3)] = mixed
            logs = jnp.transpose(logs)
            lse_ref[tile, pl.ds(2 * p, 1), 0:count] = logs[0:1, :]
            lse_ref[tile, pl.ds(2 * p + 1, 1), 0:count] = logs[HEAD_DIM : HEAD_DIM + 1, :]
            return carry

        lax.fori_loop(0, third // PAIR, body, 0)
        own[span, :] = nn(buf_h[span, 3 * third : 4 * third], wo[...])
        if tile == 0:
            pl.semaphore_wait(barrier, STEPS + 1)
        swap(0, tile, pl.ds(start, count)).start()
    save_o = load(buf_h.at[:, pl.ds(3 * third, third)], heads_h.at[:, pl.ds(3 * third, third)], 9)
    g_load.wait()
    turn(buf_g)


    wi_load.wait()
    save_qkv.wait()
    save_o.wait()
    root = 0.7978845608028654
    for half in range(2):
        for tile in (2 * half, 2 * half + 1):
            start, count = TILES[tile][:2]
            got = swap(0, tile, pl.ds(start, count))
            got.wait_send()
            got.wait_recv()

        def body(j, carry):
            i = j + half * (tiles // 2)
            total = own[rows_of(i), :] + peer[rows_of(i), :]
            middle = buf_d[rows_of(i), 0:dim].astype(f32) + total + vector(ob_ref)
            buf_m[rows_of(i), :] = middle
            unit, _ = standardize(middle)
            normed = (unit * vector(gain2_ref) + vector(shift2_ref)).astype(bf16)
            buf_n[rows_of(i), :] = normed
            bias = vector(ib_ref)
            for at in range(0, width, 512):
                u = nn(normed, wi[:, at : at + 512]) + bias[:, at : at + 512]
                square = u * u
                t = jnp.tanh(u * (root + (root * 0.044715) * square))
                below = 0.5 + 0.5 * t
                buf_h[rows_of(i), at : at + 512] = (u * below).astype(bf16)
                slope = below + (0.5 * u) * (1.0 - t * t) * (root + (3.0 * 0.044715 * root) * square)
                buf_d[rows_of(i), at : at + 512] = slope.astype(bf16)
            return carry

        lax.fori_loop(0, tiles // 2, body, 0)
    peer_is_free()


    def body(i, carry):
        gradient(i, columns(buf_h, i * LANES))
        return carry

    lax.fori_loop(0, 4, body, 0)


    wb_load.wait()
    pl.semaphore_wait(free_sem, 1)

    def body(i, carry):
        grad = buf_g[rows_of(i), :]
        for at in range(0, width, 512):
            back = nt(grad, wb[at : at + 512, :])
            du = (back * buf_d[rows_of(i), at : at + 512].astype(f32)).astype(bf16)
            buf_d[rows_of(i), at : at + 512] = du
            sums_ref[4:5, at : at + 512] += jnp.sum(du.astype(f32), 0, keepdims=True)
        own[rows_of(i), :] = nt(buf_d[rows_of(i), :], wi[...])
        swap(1, i, rows_of(i)).start()
        sums_ref[2:3, dim : 2 * dim] += jnp.sum(grad.astype(f32), 0, keepdims=True)
        return carry

    lax.fori_loop(0, tiles, body, 0)
    w3_late = [load(w3_h.at[c], wi.at[:, pl.ds(c * third, third)], 11 + c) for c in range(3)]
    arrivals(11)


    turn(buf_n)

    def body(i, carry):
        gradient(4 + i, columns(buf_d, i * LANES))
        return carry

    lax.fori_loop(0, 4, body, 0)
    arrivals(16)


    def body(i, carry):
        grad = swapped(1, i)
        unit, inv = standardize(buf_m[rows_of(i), :])
        dh = buf_g[rows_of(i), :].astype(f32) + norm_back(unit, inv, vector(gain2_ref), grad)
        own[rows_of(i), :] = dh
        dr = dh.astype(bf16)
        buf_n[rows_of(i), :] = dr
        buf_d[rows_of(i), 0:third] = nt(dr, wo[...]).astype(bf16)
        sums_ref[1:2, dim : 2 * dim] += jnp.sum(grad * unit, 0, keepdims=True)
        sums_ref[2:3, 0:dim] += jnp.sum(grad, 0, keepdims=True)
        sums_ref[1:2, 0:dim] += jnp.sum(dr.astype(f32), 0, keepdims=True)
        return carry

    lax.fori_loop(0, tiles, body, 0)
    peer_is_free()
    save_dh = load(own, dh_h, 10)
    arrivals(20)


    turn(buf_n)
    save_dh.wait()
    pl.semaphore_wait(free_sem, 1)

    def body(i, carry):
        own[rows_of(i), :] = nn(buf_h[rows_of(i), :], wb[...])
        swap(2, i, rows_of(i)).start()
        return carry

    lax.fori_loop(0, tiles, body, 0)
    heads_load = load(heads_h, buf_h, 8)
    arrivals(24)
    heads_load.wait()
    gradient(8, buf_h[:, 3 * third : 4 * third])
    arrivals(26)


    for p in range(third // PAIR):

        def place(block):
            return pl.ds(block * third + p * PAIR, PAIR)

        def take(ref, block):
            return lambda span: ref[span, place(block)]

        def put(block):
            def store(span, value):
                buf_d[span, place(block)] = value

            return store

        def lse(tile, count):
            return [lse_ref[tile, 2 * p + head : 2 * p + head + 1, 0:count] for head in range(2)]

        total = attend_back_pair(
            take(buf_h, 0), take(buf_h, 1), take(buf_h, 2), take(buf_d, 0), lse, col_ref, row_ref, put(1), acc_k, acc_v,
            lambda tile: arrivals(26 + 6.8 * p + 1.7 * (tile + 1)),
        )
        put(2)(slice(0, tok), acc_k[...].astype(bf16))
        dv = acc_v[...].astype(bf16)
        put(3)(slice(0, tok), dv)
        sums_ref[3:4, p * PAIR : (p + 1) * PAIR] = total
        sums_ref[3:4, third + p * PAIR : third + (p + 1) * PAIR] = jnp.sum(dv.astype(f32), 0, keepdims=True)


    def body(i, carry):
        buf_g[rows_of(i), :] = (buf_m[rows_of(i), :] + swapped(2, i) + vector(bb_ref)).astype(bf16)
        return carry

    lax.fori_loop(0, tiles, body, 0)
    peer_is_free()
    layer_put = pltpu.make_async_copy(buf_g, layer_h, put_sem.at[0])
    layer_put.start()
    dh_load = load(dh_h, buf_m, 14)
    arrivals(48)


    for item in w3_late:
        item.wait()
    pl.semaphore_wait(free_sem, 1)

    def body(i, carry):
        own[rows_of(i), :] = nt(buf_d[rows_of(i), third : 4 * third], wi[:, 0 : 3 * third])
        swap(3, i, rows_of(i)).start()
        return carry

    lax.fori_loop(0, tiles // 2, body, 0)
    layer_put.wait()
    tok_late = load(tok_h, buf_g, 15)
    lax.fori_loop(tiles // 2, tiles, body, 0)
    tok_late.wait()
    arrivals(51)

    def body(i, carry):
        _, _, normed = first_norm(buf_g[rows_of(i), :])
        buf_n[rows_of(i), :] = normed
        return carry

    lax.fori_loop(0, tiles, body, 0)
    turn(buf_n)

    def body(i, carry):
        gradient(9 + i, columns(buf_d, i * LANES + third))
        return carry

    lax.fori_loop(0, 3, body, 0)
    arrivals(57)


    dh_load.wait()

    def body(i, carry):
        grad = swapped(3, i)
        unit, inv, _ = first_norm(buf_g[rows_of(i), :])
        buf_g[rows_of(i), :] = (buf_m[rows_of(i), :] + norm_back(unit, inv, vector(gain1_ref), grad)).astype(bf16)
        sums_ref[0:1, 0:dim] += jnp.sum(grad * unit, 0, keepdims=True)
        sums_ref[0:1, dim : 2 * dim] += jnp.sum(grad, 0, keepdims=True)
        return carry

    lax.fori_loop(0, tiles, body, 0)
    input_put = pltpu.make_async_copy(buf_g, input_h, put_sem.at[1])
    input_put.start()


    def whole_hop(step):
        return pltpu.make_async_remote_copy(
            src_ref=sums_ref,
            dst_ref=sums_in.at[step],
            send_sem=sums_send.at[step],
            recv_sem=sums_recv.at[step],
            device_id=(route.plain[step], core),
            device_id_type=mesh_id,
        )

    for step in range(STEPS):
        whole_hop(step).start()
        arrivals(68 + 8 * step)
        whole_hop(step).wait()
        sums_ref[...] += sums_in[step]
    arrivals(1e9)
    for chunk in range(COUNT):
        deliver(chunk).wait()
    input_put.wait()


def whole_layer(tokens, g, w3, wo, wi, wb, ids, gain1, shift1, qvb, ob, gain2, shift2, ib, bb):
    tok, dim = g.shape
    width = wi.shape[1]
    third = wo.shape[0]
    rows = dim // 16
    hbm = pl.BlockSpec(memory_space=pl.ANY)
    vmem = pl.BlockSpec(memory_space=pltpu.VMEM)
    dma = pltpu.SemaphoreType.DMA
    return pl.pallas_call(
        layer_kernel,
        in_specs=[hbm] * 6 + [vmem] * 9,
        out_specs=[hbm, hbm, hbm, vmem, hbm, hbm],
        out_shape=[
            jax.ShapeDtypeStruct((tok, dim), bf16),
            jax.ShapeDtypeStruct((tok, dim), bf16),
            jax.ShapeDtypeStruct((COUNT, rows, LANES), f32),
            jax.ShapeDtypeStruct((8, width), f32),
            jax.ShapeDtypeStruct((tok, width), bf16),
            jax.ShapeDtypeStruct((tok, dim), f32),
        ],
        scratch_shapes=[
            pltpu.VMEM((tok, width), bf16),
            pltpu.VMEM((tok, width), bf16),
            pltpu.VMEM((tok, dim), bf16),
            pltpu.VMEM((tok, dim), bf16),
            pltpu.VMEM((dim, tok), bf16),
            pltpu.VMEM((tok, dim), f32),
            pltpu.VMEM((tok, dim), f32),
            pltpu.VMEM((tok, dim), f32),
            pltpu.VMEM((dim, width), bf16),
            pltpu.VMEM((width, dim), bf16),
            pltpu.VMEM((third, dim), bf16),
            pltpu.VMEM((tok, PAIR), f32),
            pltpu.VMEM((tok, PAIR), f32),
            pltpu.VMEM((tok, PAIR), jnp.int32),
            pltpu.VMEM((1, tok), jnp.int32),
            pltpu.VMEM((len(TILES), 8, LANES), f32),
            pltpu.VMEM((COUNT, 16, rows, LANES), f32),
            pltpu.VMEM((COUNT, 8, rows, LANES), f32),
            pltpu.VMEM((COUNT, 4, rows, LANES), f32),
            pltpu.VMEM((COUNT, 2, rows, LANES), f32),
            pltpu.VMEM((COUNT, 1, rows, LANES), f32),
            pltpu.VMEM((STEPS, 8, width), f32),
            dma((16,)),
            dma((STEPS, COUNT)),
            dma((STEPS, COUNT)),
            dma((COUNT,)),
            dma((4, 4)),
            dma((4, 4)),
            dma((STEPS,)),
            dma((STEPS,)),
            dma((2,)),
            pltpu.SemaphoreType.REGULAR,
        ],
        compiler_params=pltpu.CompilerParams(vmem_limit_bytes=VMEM_LIMIT, collective_id=0, has_side_effects=True),
        cost_estimate=cost(34e9, 40e6),
        name="whole_layer",
    )(tokens, g, w3, wo, wi, wb, ids, gain1, shift1, qvb, ob, gain2, shift2, ib, bb)


def outputs_kernel(layer_h, input_h, grads_ref, sums_ref, layer_o, input_o, *refs):
    n1g, n1s, qkv, qvb, out, obg, n2g, n2s, inw, ibg, back, bbg, held, sems = refs
    ins = [pltpu.make_async_copy(ref, held.at[i], sems.at[i]) for i, ref in enumerate((layer_h, input_h))]
    outs = [pltpu.make_async_copy(held.at[i], ref, sems.at[2 + i]) for i, ref in enumerate((layer_o, input_o))]
    for item in ins:
        item.start()
    me = lax.axis_index("batch")
    dim = sums_ref.shape[1] // 2
    third = dim // 2

    def mine(row, at, size):
        n = size // 16
        values = jnp.broadcast_to(sums_ref[row : row + 1, at : at + size], (8, size))
        return pltpu.roll(values, size - me * n, 1)[0:1, 0:n]

    for ref, row, at in ((n1g, 0, 0), (n1s, 0, dim), (obg, 1, 0), (n2g, 1, dim), (n2s, 2, 0), (bbg, 2, dim)):
        ref[...] = mine(row, at, dim).reshape(-1)
    ibg[...] = mine(4, 0, 2 * dim).reshape(-1)
    qvb[0:1, :] = mine(3, 0, third)
    qvb[1:2, :] = mine(3, third, third)
    for coming, going in zip(ins, outs):
        coming.wait()
        going.start()
    for c in range(4):
        back[:, c * LANES : (c + 1) * LANES] = grads_ref[c]
        inw[:, c * LANES : (c + 1) * LANES] = grads_ref[4 + c]
    out[...] = grads_ref[8]
    for c in range(3):
        qkv[c] = grads_ref[9 + c]
    for item in outs:
        item.wait()


def outputs(layer, grad, grads, sums):
    rows, width = grads.shape[1], sums.shape[1]
    hbm = pl.BlockSpec(memory_space=pl.ANY)
    vmem = pl.BlockSpec(memory_space=pltpu.VMEM)
    small = jax.ShapeDtypeStruct((rows,), f32)
    shape = lambda *s: jax.ShapeDtypeStruct(s, f32)
    return pl.pallas_call(
        outputs_kernel,
        in_specs=[hbm, hbm, vmem, vmem],
        out_specs=[hbm, hbm] + [vmem] * 12,
        out_shape=[
            jax.ShapeDtypeStruct(layer.shape, bf16),
            jax.ShapeDtypeStruct(grad.shape, bf16),
            small,
            small,
            shape(3, rows, LANES),
            shape(2, rows // 2),
            shape(rows, LANES),
            small,
            small,
            small,
            shape(rows, width),
            shape(2 * rows),
            shape(rows, width),
            small,
        ],
        scratch_shapes=[pltpu.VMEM((2,) + layer.shape, bf16), pltpu.SemaphoreType.DMA((4,))],
        compiler_params=params(60),
        name="outputs",
    )(layer, grad, grads, sums)


def shards(
    tokens,
    seq_ids,
    cotangent,
    norm1_gain,
    norm1_shift,
    w_qkv,
    qv_bias,
    w_out,
    out_bias,
    norm2_gain,
    norm2_shift,
    w_in,
    in_bias,
    w_back,
    back_bias,
    batch,
):
    tok, dim = tokens.shape
    w3 = jnp.transpose(w_qkv, (1, 0, 2))
    if batch == 16:
        layer, grad, grads, sums, _, _ = whole_layer(
            tokens, cotangent, w3, w_out, w_in, w_back, seq_ids,
            norm1_gain, norm1_shift, qv_bias, out_bias, norm2_gain, norm2_shift, in_bias, back_bias,
        )
        results = list(outputs(layer, grad, grads, sums))
        results[4] = jnp.transpose(results[4], (1, 0, 2))
        results[6], results[12] = results[6].T, results[12].T
        return tuple(results)

    row = lambda a: a.reshape(1, -1)
    ids_col, ids_row = seq_ids.reshape(tok, 1), seq_ids.reshape(1, tok)
    exchange = Exchange(batch)
    parts = exchange.first_parts()

    normed, q, k, v = project(tokens, row(norm1_gain), row(norm1_shift), w3, qv_bias)
    mixed, lse_a, part_a = attend(0, q, k, v, ids_col, ids_row, w_out)
    peer_a = other_core(part_a)
    mixed, lse_b, part_b = attend(1, q, k, v, ids_col, ids_row, w_out, (mixed,))
    peer_b = other_core(part_b)
    mlp = (row(out_bias), row(norm2_gain), row(norm2_shift), w_in, row(in_bias))
    state = hidden_layer(0, tokens, part_a, peer_a, *mlp)
    state = hidden_layer(1, tokens, part_b, peer_b, *mlp, before=tuple(state))
    middle, normed_two, hidden, slope = state

    back_parts = weight_grad(parts, exchange.place, cotangent, hidden)
    du, dn2, in_bias_sum, back_bias_sum = hidden_back(cotangent, slope, w_back, w_in)
    dn2_peer = other_core(dn2)
    in_parts = weight_grad(parts, exchange.place, normed_two, du)
    mlp_own = rows_matmul(hidden, w_back)
    mlp_peer = other_core(mlp_own)
    dh, dr, do, middle_sums = middle_back(middle, dn2, dn2_peer, cotangent, row(norm2_gain), w_out)
    out_parts = weight_grad(parts, exchange.place, dr, mixed)
    layer_out = (middle + (mlp_own + mlp_peer) + back_bias).astype(bf16)
    dq, dk, dv, qv_sums = attend_back(q, k, v, do, lse_a, lse_b, ids_col, ids_row)
    q_parts = weight_grad(parts, exchange.place, normed, dq)
    k_parts = weight_grad(parts, exchange.place, normed, dk)
    v_parts = weight_grad(parts, exchange.place, normed, dv)
    dn1 = normed_back(dq, dk, dv, w3)
    dn1_peer = other_core(dn1)
    tokens_grad, input_sums = input_back(tokens, dn1, dn1_peer, dh, row(norm1_gain))

    w_back_grad = jnp.transpose(exchange.reduce(back_parts))
    w_in_grad = exchange.reduce(in_parts)
    w_out_grad = jnp.transpose(exchange.reduce(out_parts))
    w_qkv_grad = jnp.stack([exchange.reduce(p) for p in (q_parts, k_parts, v_parts)], 1)

    pieces = [input_sums[0], input_sums[1], middle_sums[2], middle_sums[0], middle_sums[1], back_bias_sum[0]]
    pieces += [qv_sums[0], qv_sums[1], in_bias_sum[0]]
    packed = jnp.concatenate([p.reshape(batch, -1) for p in pieces], 1)
    vectors = lax.psum_scatter(packed, "batch", scatter_dimension=0, tiled=True)[0]
    out, at = [], 0
    for p in pieces:
        n = p.shape[0] // batch
        out.append(vectors[at : at + n])
        at += n
    n1g, n1s, obg, n2g, n2s, bbg, qb, vb, ibg = out
    return (
        layer_out,
        tokens_grad,
        n1g,
        n1s,
        w_qkv_grad,
        jnp.stack([qb, vb]),
        w_out_grad,
        obg,
        n2g,
        n2s,
        w_in_grad,
        ibg,
        w_back_grad,
        bbg,
    )


def solution(mesh):
    in_specs = (
        P("batch", None),
        P("batch"),
        P("batch", None),
        P(),
        P(),
        P(None, None, "tp"),
        P(None, "tp"),
        P("tp", None),
        P(),
        P(),
        P(),
        P(None, "tp"),
        P("tp"),
        P("tp", None),
        P(),
    )
    out_specs = (
        P("batch", None),
        P("batch", None),
        P("batch"),
        P("batch"),
        P("batch", None, "tp"),
        P(None, ("tp", "batch")),
        P("tp", "batch"),
        P("batch"),
        P("batch"),
        P("batch"),
        P("batch", "tp"),
        P(("tp", "batch")),
        P("tp", "batch"),
        P("batch"),
    )
    body = functools.partial(shards, batch=mesh.shape["batch"])
    return jax.shard_map(body, mesh=mesh, in_specs=in_specs, out_specs=out_specs, check_vma=False)
```

```python
import functools

import jax
import jax.numpy as jnp
from jax import lax
from jax.experimental import pallas as pl
from jax.experimental.pallas import tpu as pltpu
from jax.sharding import PartitionSpec as P

HEAD_DIM = 64
PAIR = 2 * HEAD_DIM
HALF = 608
TILE = 304
LANES = 384
VMEM_LIMIT = 63 << 20
WINDOW = 768
LOW = 448
ROWS = ((0, 128), (128, 128), (256, 128), (384, 128), (512, 96))
TILES = ((0, 256, 0, 608), (256, 352, 0, 688), (608, 256, 448, 1216), (864, 352, 608, 1216))
f32 = jnp.float32
bf16 = jnp.bfloat16


def params(mib):
    return pltpu.CompilerParams(vmem_limit_bytes=mib << 20)


def cost(flops, nbytes, trans=0):
    return pl.CostEstimate(flops=int(flops), bytes_accessed=int(nbytes), transcendentals=int(trans))


def nn(a, b):
    return jnp.dot(a, b, preferred_element_type=f32)


def nt(a, b):
    return lax.dot_general(a, b, (((1,), (1,)), ((), ())), preferred_element_type=f32)


def tn(a, b):
    return lax.dot_general(a, b, (((0,), (0,)), ((), ())), preferred_element_type=f32)


def standardize(values):
    center = values - jnp.mean(values, -1, keepdims=True)
    spread = jnp.mean(center * center, -1, keepdims=True)
    inv = lax.rsqrt(spread + 1e-06)
    return center * inv, inv


def norm_back(unit, inv, gain, grad):
    scaled = grad * gain
    return inv * (
        scaled
        - jnp.mean(scaled, -1, keepdims=True)
        - unit * jnp.mean(scaled * unit, -1, keepdims=True)
    )


def whole(shape):
    return pl.BlockSpec(shape, lambda *_: (0,) * len(shape))


def project_kernel(x_ref, gain_ref, shift_ref, w_ref, bias_ref, n_ref, q_ref, k_ref, v_ref):
    unit, _ = standardize(x_ref[...].astype(f32))
    normed = (unit * gain_ref[...] + shift_ref[...]).astype(bf16)
    n_ref[...] = normed
    scale = HEAD_DIM ** (-0.5)
    q_ref[...] = ((nn(normed, w_ref[0]) + bias_ref[0:1]).astype(bf16).astype(f32) * scale).astype(bf16)
    k_ref[...] = nn(normed, w_ref[1]).astype(bf16)
    v_ref[...] = (nn(normed, w_ref[2]) + bias_ref[1:2]).astype(bf16)


def project(tokens, gain, shift, w3, qv_bias):
    tok, dim = tokens.shape
    width = w3.shape[2]
    rows = lambda n: pl.BlockSpec((TILE, n), lambda i: (i, 0))
    out = jax.ShapeDtypeStruct((tok, width), bf16)
    return pl.pallas_call(
        project_kernel,
        grid=(tok // TILE,),
        in_specs=[rows(dim), whole((1, dim)), whole((1, dim)), whole(w3.shape), whole((2, width))],
        out_specs=[rows(dim), rows(width), rows(width), rows(width)],
        out_shape=[jax.ShapeDtypeStruct((tok, dim), bf16), out, out, out],
        compiler_params=params(60),
        cost_estimate=cost(2 * tok * dim * 3 * width, tok * (2 * dim + 3 * width) * 2 + w3.size * 2),
        name="project",
    )(tokens, gain, shift, w3, qv_bias)


def attend_kernel(half, q_ref, k_ref, v_ref, col_ref, row_ref, w_ref, *refs):
    o_ref, lse_ref, part_ref, *mask_refs = refs[-5:]
    step = pl.program_id(0)
    tiles = TILES[2 * half : 2 * half + 2]

    @pl.when(step == 0)
    def _():
        for (start, count, low, high), mask_ref in zip(tiles, mask_refs):
            at = start - half * HALF
            same = col_ref[at : at + count, :] == row_ref[:, low:high]
            mask_ref[...] = jnp.where(same, 0.0, -1000000000.0)

    first = lax.broadcasted_iota(jnp.int32, (1, PAIR), 1) < HEAD_DIM
    zero = jnp.zeros((), bf16)
    one = jnp.ones((), bf16)
    for tile, ((start, count, low, high), mask_ref) in enumerate(zip(tiles, mask_refs)):
        at = start - half * HALF
        rows = q_ref[at : at + count, :]
        keys = k_ref[low:high, :]
        values = v_ref[low:high, :]
        with_ones = (jnp.where(first, values, one), jnp.where(first, one, values))
        mask = mask_ref[...]
        outs, logs = [], []
        for head in range(2):
            own = jnp.where(first, rows, zero) if head == 0 else jnp.where(first, zero, rows)
            scores = nt(own, keys) + mask
            top = jnp.max(scores, -1, keepdims=True)
            expo = jnp.exp(scores - top).astype(bf16)
            mixed = nn(expo, with_ones[head])
            total = pltpu.roll(mixed, HEAD_DIM, 1)
            outs.append(mixed / total)
            logs.append(top + jnp.log(total))
        mixed = jnp.where(first, outs[0], outs[1]).astype(bf16)
        o_ref[at : at + count, :] = mixed
        turned = jnp.transpose(jnp.where(first, logs[0], logs[1]))
        lse_ref[tile, pl.ds(2 * step, 1), 0:count] = turned[0:1, :]
        lse_ref[tile, pl.ds(2 * step + 1, 1), 0:count] = turned[HEAD_DIM : HEAD_DIM + 1, :]
        part = nn(mixed, w_ref[...])

        @pl.when(step == 0)
        def _():
            part_ref[at : at + count, :] = part

        @pl.when(step > 0)
        def _():
            part_ref[at : at + count, :] += part


def attend(half, q, k, v, ids_col, ids_row, w_out, before=()):
    tok, width = q.shape
    dim = w_out.shape[1]
    pair_rows = pl.BlockSpec((HALF, PAIR), lambda p: (half, p))
    pair_all = pl.BlockSpec((tok, PAIR), lambda p: (0, p))
    tiles = TILES[2 * half : 2 * half + 2]
    return pl.pallas_call(
        functools.partial(attend_kernel, half),
        grid=(width // PAIR,),
        in_specs=[
            pair_rows,
            pair_all,
            pair_all,
            pl.BlockSpec((HALF, 1), lambda p: (half, 0)),
            whole((1, tok)),
            pl.BlockSpec((PAIR, dim), lambda p: (p, 0)),
        ]
        + [pl.BlockSpec(memory_space=pl.ANY)] * len(before),
        out_specs=[pair_rows, whole((2, 8, LANES)), whole((HALF, dim))],
        out_shape=[
            jax.ShapeDtypeStruct((tok, width), bf16),
            jax.ShapeDtypeStruct((2, 8, LANES), f32),
            jax.ShapeDtypeStruct((HALF, dim), f32),
        ],
        scratch_shapes=[pltpu.VMEM((count, high - low), f32) for _, count, low, high in tiles],
        input_output_aliases={6 + i: i for i in range(len(before))},
        compiler_params=params(60),
        cost_estimate=cost(16 * HALF * 650 * width, tok * width * 6 + HALF * dim * 4),
        name="attend",
    )(q, k, v, ids_col, ids_row, w_out, *before)


def hidden_kernel(x_ref, own_ref, peer_ref, ob_ref, gain_ref, shift_ref, w_ref, ib_ref, *refs):
    mid_ref, n_ref, hid_ref, slope_ref = refs[-4:]
    middle = x_ref[...].astype(f32) + (own_ref[...] + peer_ref[...]) + ob_ref[...]
    mid_ref[...] = middle
    unit, _ = standardize(middle)
    normed = (unit * gain_ref[...] + shift_ref[...]).astype(bf16)
    n_ref[...] = normed
    width = w_ref.shape[1]
    piece = 512
    c0 = 0.7978845608028654
    for at in range(0, width, piece):
        u = nn(normed, w_ref[:, at : at + piece]) + ib_ref[:, at : at + piece]
        sq = u * u
        t = jnp.tanh(u * (c0 + (c0 * 0.044715) * sq))
        cdf = 0.5 + 0.5 * t
        hid_ref[:, at : at + piece] = (u * cdf).astype(bf16)
        slope = cdf + (0.5 * u) * (1.0 - t * t) * (c0 + (3.0 * 0.044715 * c0) * sq)
        slope_ref[:, at : at + piece] = slope.astype(bf16)


def hidden_layer(half, tokens, own, peer, out_bias, gain, shift, w_in, in_bias, before=()):
    tok, dim = tokens.shape
    width = w_in.shape[1]
    per = HALF // TILE
    glob = lambda n: pl.BlockSpec((TILE, n), lambda i: (i + per * half, 0))
    loc = lambda n: pl.BlockSpec((TILE, n), lambda i: (i, 0))
    return pl.pallas_call(
        hidden_kernel,
        grid=(per,),
        in_specs=[
            glob(dim),
            loc(dim),
            loc(dim),
            whole((1, dim)),
            whole((1, dim)),
            whole((1, dim)),
            whole(w_in.shape),
            whole((1, width)),
        ]
        + [pl.BlockSpec(memory_space=pl.ANY)] * len(before),
        out_specs=[glob(dim), glob(dim), glob(width), glob(width)],
        out_shape=[
            jax.ShapeDtypeStruct((tok, dim), f32),
            jax.ShapeDtypeStruct((tok, dim), bf16),
            jax.ShapeDtypeStruct((tok, width), bf16),
            jax.ShapeDtypeStruct((tok, width), bf16),
        ],
        input_output_aliases={8 + i: i for i in range(len(before))},
        compiler_params=params(60),
        cost_estimate=cost(2 * HALF * dim * width, HALF * (dim * 16 + width * 4) + w_in.size * 2, HALF * width),
        name="hidden_layer",
    )(tokens, own, peer, out_bias, gain, shift, w_in, in_bias, *before)


def matmul_kernel(a_ref, b_ref, o_ref):
    o_ref[...] = nn(a_ref[...], b_ref[...])


def rows_matmul(a, b):
    tok, depth = a.shape
    width = b.shape[1]
    return pl.pallas_call(
        matmul_kernel,
        grid=(tok // TILE,),
        in_specs=[pl.BlockSpec((TILE, depth), lambda i: (i, 0)), whole(b.shape)],
        out_specs=pl.BlockSpec((TILE, width), lambda i: (i, 0)),
        out_shape=jax.ShapeDtypeStruct((tok, width), f32),
        compiler_params=params(60),
        cost_estimate=cost(2 * tok * depth * width, tok * (depth * 2 + width * 4) + b.size * 2),
        name="mlp_out",
    )(a, b)


def hidden_back_kernel(g_ref, slope_ref, wb_ref, wi_ref, du_ref, dn_ref, db_ref, gb_ref):
    step = pl.program_id(0)
    grad = g_ref[...]
    width = slope_ref.shape[1]
    piece = 512
    total = None
    sums = []
    for at in range(0, width, piece):
        back = nt(grad, wb_ref[at : at + piece, :])
        du = (back * slope_ref[:, at : at + piece].astype(f32)).astype(bf16)
        du_ref[:, at : at + piece] = du
        sums.append(jnp.sum(du.astype(f32), 0, keepdims=True))
    dn_ref[...] = nt(du_ref[...], wi_ref[...])

    @pl.when(step == 0)
    def _():
        db_ref[...] = jnp.zeros_like(db_ref)
        gb_ref[...] = jnp.zeros_like(gb_ref)

    for i, at in enumerate(range(0, width, piece)):
        db_ref[:, at : at + piece] += sums[i]
    gb_ref[...] += jnp.sum(grad.astype(f32), 0, keepdims=True)


def hidden_back(cotangent, slope, w_back, w_in):
    tok, dim = cotangent.shape
    width = slope.shape[1]
    rows = lambda n: pl.BlockSpec((TILE, n), lambda i: (i, 0))
    return pl.pallas_call(
        hidden_back_kernel,
        grid=(tok // TILE,),
        in_specs=[rows(dim), rows(width), whole(w_back.shape), whole(w_in.shape)],
        out_specs=[rows(width), rows(dim), whole((1, width)), whole((1, dim))],
        out_shape=[
            jax.ShapeDtypeStruct((tok, width), bf16),
            jax.ShapeDtypeStruct((tok, dim), f32),
            jax.ShapeDtypeStruct((1, width), f32),
            jax.ShapeDtypeStruct((1, dim), f32),
        ],
        compiler_params=params(60),
        cost_estimate=cost(4 * tok * dim * width, tok * (dim * 6 + width * 4) + w_in.size * 4),
        name="hidden_back",
    )(cotangent, slope, w_back, w_in)


def middle_back_kernel(mid_ref, own_ref, peer_ref, g_ref, gain_ref, w_ref, dh_ref, dr_ref, do_ref, sum_ref):
    step = pl.program_id(0)
    unit, inv = standardize(mid_ref[...])
    grad = own_ref[...] + peer_ref[...]
    dh = g_ref[...].astype(f32) + norm_back(unit, inv, gain_ref[...], grad)
    dh_ref[...] = dh
    dr = dh.astype(bf16)
    dr_ref[...] = dr
    do_ref[...] = nt(dr, w_ref[...]).astype(bf16)

    @pl.when(step == 0)
    def _():
        sum_ref[...] = jnp.zeros_like(sum_ref)

    sum_ref[0:1] += jnp.sum(grad * unit, 0, keepdims=True)
    sum_ref[1:2] += jnp.sum(grad, 0, keepdims=True)
    sum_ref[2:3] += jnp.sum(dr.astype(f32), 0, keepdims=True)


def middle_back(middle, own, peer, cotangent, gain, w_out):
    tok, dim = middle.shape
    width = w_out.shape[0]
    rows = lambda n: pl.BlockSpec((TILE, n), lambda i: (i, 0))
    return pl.pallas_call(
        middle_back_kernel,
        grid=(tok // TILE,),
        in_specs=[rows(dim), rows(dim), rows(dim), rows(dim), whole((1, dim)), whole(w_out.shape)],
        out_specs=[rows(dim), rows(dim), rows(width), whole((8, dim))],
        out_shape=[
            jax.ShapeDtypeStruct((tok, dim), f32),
            jax.ShapeDtypeStruct((tok, dim), bf16),
            jax.ShapeDtypeStruct((tok, width), bf16),
            jax.ShapeDtypeStruct((8, dim), f32),
        ],
        compiler_params=params(60),
        cost_estimate=cost(2 * tok * dim * width, tok * (dim * 20 + width * 2) + w_out.size * 2),
        name="middle_back",
    )(middle, own, peer, cotangent, gain, w_out)


def attend_back_tile(tile, keys, values, rows, grads, mask, lse_rows):
    first = lax.broadcasted_iota(jnp.int32, (1, PAIR), 1) < HEAD_DIM
    zero = jnp.zeros((), bf16)
    parts = []
    for head in range(2):
        pick = lambda a: jnp.where(first, a, zero) if head == 0 else jnp.where(first, zero, a)
        probs = jnp.exp(nt(keys, pick(rows)) + mask - lse_rows[head])
        back = nt(values, pick(grads))
        inner = jnp.sum(probs * back, 0, keepdims=True)
        slant = (probs * (back - inner)).astype(bf16)
        dv = nn(probs.astype(bf16), grads)
        dk = nn(slant, rows)
        dq = tn(slant, keys)
        parts.append((dq, dk, dv))
    dq, dk, dv = (jnp.where(first, a, b) for a, b in zip(*parts))
    return (dq * HEAD_DIM ** (-0.5)).astype(bf16), dk, dv


def attend_back_pair(q, k, v, do, lse, col_ref, row_ref, put_dq, acc_k, acc_v, after=lambda tile: None):
    total = None
    for tile, (start, count, low, high) in enumerate(TILES):
        span = slice(start, start + count)
        mask = jnp.where(col_ref[low:high, 0:1] == row_ref[:, span], 0.0, -1000000000.0)
        dq, dk, dv = attend_back_tile(
            tile, k(slice(low, high)), v(slice(low, high)), q(span), do(span), mask, lse(tile, count)
        )
        put_dq(span, dq)
        top = jnp.sum(dq.astype(f32), 0, keepdims=True)
        total = top if total is None else total + top
        edge = 0 if tile == 0 else TILES[tile - 1][3]
        for acc, part in ((acc_k, dk), (acc_v, dv)):
            if edge > low:
                acc[low:edge, :] += part[: edge - low]
            if edge < high:
                acc[edge:high, :] = part[max(edge - low, 0) :]
        after(tile)
    return total


def attend_back_kernel(q_ref, k_ref, v_ref, do_ref, lse_a, lse_b, col_ref, row_ref, dq_ref, dk_ref, dv_ref, sum_ref, acc_k, acc_v):
    step = pl.program_id(0)

    def lse(tile, count):
        ref = lse_a if tile < 2 else lse_b
        return [ref[tile % 2, pl.ds(2 * step + head, 1), 0:count] for head in range(2)]

    def put_dq(span, value):
        dq_ref[span, :] = value

    take = lambda ref: lambda span: ref[span, :]
    total = attend_back_pair(
        take(q_ref), take(k_ref), take(v_ref), take(do_ref), lse, col_ref, row_ref, put_dq, acc_k, acc_v
    )
    dk_ref[...] = acc_k[...].astype(bf16)
    dv = acc_v[...].astype(bf16)
    dv_ref[...] = dv
    sum_ref[...] = jnp.zeros_like(sum_ref)
    sum_ref[0:1, :] = total
    sum_ref[1:2, :] = jnp.sum(dv.astype(f32), 0, keepdims=True)


def attend_back(q, k, v, do, lse_a, lse_b, ids_col, ids_row):
    tok, width = q.shape
    pair = pl.BlockSpec((tok, PAIR), lambda p: (0, p))
    out = jax.ShapeDtypeStruct((tok, width), bf16)
    return pl.pallas_call(
        attend_back_kernel,
        grid=(width // PAIR,),
        in_specs=[pair, pair, pair, pair, whole(lse_a.shape), whole(lse_b.shape), whole((tok, 1)), whole((1, tok))],
        out_specs=[pair, pair, pair, pl.BlockSpec((8, PAIR), lambda p: (0, p))],
        out_shape=[out, out, out, jax.ShapeDtypeStruct((8, width), f32)],
        scratch_shapes=[pltpu.VMEM((tok, PAIR), f32), pltpu.VMEM((tok, PAIR), f32)],
        compiler_params=params(60),
        cost_estimate=cost(4 * 10 * tok * HALF * width, tok * width * 18),
        name="attend_back",
    )(q, k, v, do, lse_a, lse_b, ids_col, ids_row)


def normed_back_kernel(dq_ref, dk_ref, dv_ref, w_ref, o_ref):
    o_ref[...] = nt(dq_ref[...], w_ref[0]) + nt(dk_ref[...], w_ref[1]) + nt(dv_ref[...], w_ref[2])


def normed_back(dq, dk, dv, w3):
    tok, width = dq.shape
    dim = w3.shape[1]
    rows = lambda n: pl.BlockSpec((TILE, n), lambda i: (i, 0))
    return pl.pallas_call(
        normed_back_kernel,
        grid=(tok // TILE,),
        in_specs=[rows(width), rows(width), rows(width), whole(w3.shape)],
        out_specs=rows(dim),
        out_shape=jax.ShapeDtypeStruct((tok, dim), f32),
        compiler_params=params(60),
        cost_estimate=cost(6 * tok * dim * width, tok * (dim * 4 + width * 6) + w3.size * 2),
        name="normed_back",
    )(dq, dk, dv, w3)


def input_back_kernel(x_ref, own_ref, peer_ref, dh_ref, gain_ref, o_ref, sum_ref):
    step = pl.program_id(0)
    unit, inv = standardize(x_ref[...].astype(f32))
    grad = own_ref[...] + peer_ref[...]
    o_ref[...] = (dh_ref[...] + norm_back(unit, inv, gain_ref[...], grad)).astype(bf16)

    @pl.when(step == 0)
    def _():
        sum_ref[...] = jnp.zeros_like(sum_ref)

    sum_ref[0:1] += jnp.sum(grad * unit, 0, keepdims=True)
    sum_ref[1:2] += jnp.sum(grad, 0, keepdims=True)


def input_back(tokens, own, peer, dh, gain):
    tok, dim = tokens.shape
    rows = pl.BlockSpec((TILE, dim), lambda i: (i, 0))
    return pl.pallas_call(
        input_back_kernel,
        grid=(tok // TILE,),
        in_specs=[rows, rows, rows, rows, whole((1, dim))],
        out_specs=[rows, whole((8, dim))],
        out_shape=[jax.ShapeDtypeStruct((tok, dim), bf16), jax.ShapeDtypeStruct((8, dim), f32)],
        compiler_params=params(60),
        cost_estimate=cost(20 * tok * dim, tok * dim * 16),
        name="input_back",
    )(tokens, own, peer, dh, gain)


def grad_kernel(parts, group, place_ref, a_ref, b_ref, *refs):
    outs, turned = refs[:parts], refs[parts]

    @pl.when(pl.program_id(0) == 0)
    def _():
        flat = jnp.transpose(a_ref[...])
        if group:
            for g in range(flat.shape[0] // group):
                at = pl.multiple_of(place_ref[g] * group, group)
                turned[pl.ds(at, group), :] = flat[g * group : (g + 1) * group, :]
        else:
            turned[...] = flat

    total = nn(turned[...], b_ref[...])
    rows = total.shape[0] // parts
    for i, out in enumerate(outs):
        out[...] = total[i * rows : (i + 1) * rows, :]


def weight_grad(parts, place, a, b):
    tok, dim = a.shape
    width = b.shape[1]
    step = 384
    count = place.shape[0]
    group = dim // count
    if group % 16:
        order = jnp.argsort(place)
        rows = (order[:, None] * group + jnp.arange(group)[None, :]).reshape(dim)
        a = jnp.take(a, rows, axis=1)
        group = 0
    rows = dim // parts
    return pl.pallas_call(
        functools.partial(grad_kernel, parts, group),
        grid_spec=pltpu.PrefetchScalarGridSpec(
            num_scalar_prefetch=1,
            grid=(width // step,),
            in_specs=[
                pl.BlockSpec((tok, dim), lambda i, *_: (0, 0)),
                pl.BlockSpec((tok, step), lambda i, *_: (0, i)),
            ],
            out_specs=[pl.BlockSpec((rows, step), lambda i, *_: (0, i))] * parts,
            scratch_shapes=[pltpu.VMEM((dim, tok), bf16)],
        ),
        out_shape=[jax.ShapeDtypeStruct((rows, width), f32)] * parts,
        compiler_params=params(60),
        cost_estimate=cost(2 * tok * dim * width, tok * (dim + width) * 2 + dim * width * 4),
        name="weight_grad",
    )(place, a, b)


class Exchange:
    def __init__(self, batch):
        side = 1
        while side * side * 4 < batch:
            side *= 2
        self.batch = batch
        sizes = (batch // (side * side), side, side)
        strides = (side * side, side, 1)
        axes = list(zip(sizes, strides))
        slow, mid, fast = axes
        self.orders = ((fast, mid, slow), (mid, fast, slow))
        me = lax.axis_index("batch")
        core = lax.axis_index("tp")
        away = jnp.arange(batch, dtype=jnp.int32) ^ me
        places = []
        for order in self.orders:
            place = jnp.zeros_like(away)
            for size, stride in order:
                place = place * size + (away // stride) % size
            places.append(place)
        self.place = jnp.where(core == 0, places[0], places[1]).astype(jnp.int32)

    def first_parts(self):
        return self.orders[0][0][0]

    def swap(self, block, phase, k):
        perm = []
        for i in range(self.batch):
            for core in range(2):
                _, stride = self.orders[core][phase]
                perm.append((2 * i + core, 2 * (i ^ (k * stride)) + core))
        return lax.ppermute(block, ("batch", "tp"), perm)

    def reduce(self, parts):
        for phase in range(3):
            got = [self.swap(parts[k], phase, k) for k in range(1, len(parts))]
            if phase == 2:
                total = parts[0]
                for g in got:
                    total = total + g
                return total
            size = self.orders[0][phase + 1][0]
            rows = parts[0].shape[0] // size
            cut = lambda a, i: lax.slice_in_dim(a, i * rows, (i + 1) * rows, axis=0)
            following = []
            for i in range(size):
                total = cut(parts[0], i)
                for g in got:
                    total = total + cut(g, i)
                following.append(total)
            parts = following


def other_core(values):
    return lax.ppermute(values, "tp", [(0, 1), (1, 0)])


COUNT = 12
STEPS = 4
PLAN = (
    (), (), (), (), ((0, 0),), (), (), (), ((1, 0),), ((0, 1),), ((2, 0),), (), (), (), (), ((1, 1), (3, 0),), (),
    (), ((5, 0), (3, 1), (4, 0), (0, 2),), ((1, 2),), ((4, 1),), ((6, 0), (2, 1),), ((8, 0),), ((3, 2),), (),
    ((0, 3), (6, 1), (7, 0),), ((1, 3),), ((2, 2),), (), ((4, 2),), (), ((5, 1), (3, 3), (7, 1), (6, 2),),
    ((8, 1),), (), (), ((5, 2),), (), (), ((8, 2),), ((9, 0),), (), (), ((11, 0),),
    ((2, 3), (4, 3), (9, 1), (10, 0), (7, 2), (6, 3), (5, 3), (11, 1), (10, 1), (8, 3), (11, 2), (9, 2), (7, 3), (10, 2), (11, 3), (9, 3), (10, 3),),
)


class Route:
    def __init__(self):
        self.me = lax.axis_index("batch")
        self.core = lax.axis_index("tp")
        self.bits = {s: lax.rem(self.me // s, 2) for s in (1, 2, 4, 8)}
        near = {s: self.me + s * (1 - 2 * self.bits[s]) for s in (1, 2, 4, 8)}
        core = self.core
        side = near[1] * (1 - core) + near[2] * core
        other = near[2] * (1 - core) + near[1] * core
        self.plain = (side, other, near[4], near[8])
        self.turned = (near[4], side, other, near[8])
        self.plain_weight = {1: 8 - 4 * core, 2: 4 + 4 * core, 4: 2, 8: 1}
        self.turned_weight = {4: 8, 1: 4 - 2 * core, 2: 2 + 2 * core, 8: 1}

    def kind(self, chunk):
        return lax.rem(chunk, 3) // 2

    def partner(self, chunk, step):
        kind = self.kind(chunk)
        return self.plain[step] + kind * (self.turned[step] - self.plain[step])

    def places(self, chunk):
        kind = self.kind(chunk)
        terms = {}
        for s in (1, 2, 4, 8):
            weight = self.plain_weight[s] + kind * (self.turned_weight[s] - self.plain_weight[s])
            terms[s] = (self.bits[s] * weight, (1 - self.bits[s]) * weight)
        return [sum(terms[s][(g // s) % 2] for s in (1, 2, 4, 8)) for g in range(16)]


def attend_pair(rows_at, rows, keys, values, mask_ref, put):
    first = lax.broadcasted_iota(jnp.int32, (1, PAIR), 1) < HEAD_DIM
    zero = jnp.zeros((), bf16)
    with_ones = jnp.concatenate([values, jnp.ones_like(values)], 1)
    for at, count in ROWS:
        part = rows(at, count)
        both = jnp.concatenate([jnp.where(first, part, zero), jnp.where(first, zero, part)], 0)
        mask = mask_ref[at : at + count, :]
        scores = nt(both, keys) + jnp.concatenate([mask, mask], 0)
        top = jnp.max(scores, -1, keepdims=True)
        mixed = nn(jnp.exp(scores - top).astype(bf16), with_ones)
        total = mixed[:, PAIR:]
        mixed = mixed[:, :PAIR] / total
        logs = top + jnp.log(total)
        put(at, count, jnp.where(first, mixed[:count], mixed[count:]).astype(bf16), logs[:count], logs[count:])


def layer_kernel(
    tok_h, g_h, w3_h, wo_h, wi_h, wb_h,
    ids_ref, gain1_ref, shift1_ref, qvb_ref, ob_ref, gain2_ref, shift2_ref, ib_ref, bb_ref,
    layer_h, input_h, grads_h, sums_ref, heads_h, hid_h, mid_h,
    buf_h, buf_d, buf_n, buf_g, buf_m, own, peer, wi, wb, wo, acc_k, acc_v, col_ref, query_ids, key_ids, mask_ref,
    bias_ref, lse_ref, chunks, recv0, recv1, recv2, recv3, sums_in,
    load_sem, send_sem, recv_sem, grad_sem, swap_send, swap_recv, sums_send, sums_recv, put_sem, free_sem,
):
    mesh_id = pl.DeviceIdType.MESH
    route = Route()
    me, core = route.me, route.core
    tok, dim = buf_g.shape
    width = buf_h.shape[1]
    third = wo.shape[0]
    tiles = tok // TILE
    blocks = width // LANES
    recvs = (recv0, recv1, recv2, recv3)
    vector = lambda ref: ref[...].reshape(1, -1)

    barrier = pltpu.get_barrier_semaphore()
    for other in route.plain:
        pl.semaphore_signal(barrier, inc=1, device_id=(other, core), device_id_type=mesh_id)
    pl.semaphore_signal(barrier, inc=1, device_id=(me, 1 - core), device_id_type=mesh_id)

    def load(source, target, at):
        copy = pltpu.make_async_copy(source, target, load_sem.at[at])
        copy.start()
        return copy

    def load_w3(at):
        return [load(w3_h.at[c], wi.at[:, pl.ds(c * third, third)], at + c) for c in range(3)]

    tok_load = load(tok_h, buf_d.at[:, pl.ds(0, dim)], 0)
    w3_load = load_w3(1)
    wo_load = load(wo_h, wo, 4)
    g_load = load(g_h, buf_g, 5)
    wb_load = load(wb_h, wb, 7)


    def hop(chunk, step):
        half = 8 >> step
        return pltpu.make_async_remote_copy(
            src_ref=chunks.at[chunk, pl.ds(half, half)],
            dst_ref=recvs[step].at[chunk],
            send_sem=send_sem.at[step, chunk],
            recv_sem=recv_sem.at[step, chunk],
            device_id=(route.partner(chunk, step), core),
            device_id_type=mesh_id,
        )

    def deliver(chunk):
        return pltpu.make_async_copy(chunks.at[chunk, 0], grads_h.at[chunk], grad_sem.at[chunk])

    def finish(chunk, step):
        got = hop(chunk, step)
        got.wait_send()
        got.wait_recv()

        def add(g, carry):
            chunks[chunk, g] += recvs[step][chunk, g]
            return carry

        lax.fori_loop(0, 8 >> step, add, 0)
        if step < STEPS - 1:
            hop(chunk, step + 1).start()
        else:
            deliver(chunk).start()

    left = list(PLAN)

    def arrivals():
        for chunk, step in left.pop(0):
            finish(chunk, step)

    def loop(count, body, planned=True):
        each = [left.pop(0) for _ in range(count)] if planned else []

        def turn(i, carry):
            body(i)
            for at, now in enumerate(each):
                if now:

                    @pl.when(i == at)
                    def _():
                        for chunk, step in now:
                            finish(chunk, step)

            return carry

        lax.fori_loop(0, count, turn, 0)

    def gradient(chunk, source, right):
        places = route.places(chunk)
        total = tn(source[...], right)
        rows = dim // 16
        for g in range(16):
            chunks[chunk, places[g]] = total[g * rows : (g + 1) * rows, :]
        hop(chunk, 0).start()

    def columns(at):
        return pl.ds(pl.multiple_of(at, PAIR), LANES)

    def rows_of(i):
        return pl.ds(pl.multiple_of(i * TILE, TILE), TILE)


    def swap(turn_at, i, rows):
        return pltpu.make_async_remote_copy(
            src_ref=own.at[rows],
            dst_ref=peer.at[rows],
            send_sem=swap_send.at[turn_at, i],
            recv_sem=swap_recv.at[turn_at, i],
            device_id=(me, 1 - core),
            device_id_type=mesh_id,
        )

    def swapped(turn_at, i):
        got = swap(turn_at, i, rows_of(i))
        got.wait_send()
        got.wait_recv()
        return own[rows_of(i), :] + peer[rows_of(i), :]

    def peer_is_free():
        pl.semaphore_signal(free_sem, inc=1, device_id=(me, 1 - core), device_id_type=mesh_id)


    ids = vector(ids_ref)
    for half in range(2):
        query_ids[half, :, 0:HALF] = ids[:, half * HALF : (half + 1) * HALF]
        key_ids[half] = ids[:, half * LOW : half * LOW + WINDOW]
    col_ref[...] = jnp.transpose(jnp.broadcast_to(ids, (PAIR, tok)))
    for c in range(blocks):
        bias_ref[c] = vector(ib_ref)[:, c * LANES : (c + 1) * LANES]
    sums_ref[...] = jnp.zeros_like(sums_ref)
    tok_load.wait()
    for item in w3_load:
        item.wait()

    def first_norm(values):
        unit, inv = standardize(values.astype(f32))
        return unit, inv, (unit * vector(gain1_ref) + vector(shift1_ref)).astype(bf16)

    def body(i):
        _, _, normed = first_norm(buf_d[rows_of(i), 0:dim])
        out = nn(normed, wi[:, 0 : 3 * third])
        query = (out[:, 0:third] + qvb_ref[0:1, :]).astype(bf16)
        buf_h[rows_of(i), 0:third] = (query.astype(f32) * HEAD_DIM ** (-0.5)).astype(bf16)
        buf_h[rows_of(i), third : 2 * third] = out[:, third : 2 * third].astype(bf16)
        buf_h[rows_of(i), 2 * third : 3 * third] = (out[:, 2 * third :] + qvb_ref[1:2, :]).astype(bf16)

    loop(tiles, body, False)
    wi_load = load(wi_h, wi, 6)
    save_qkv = load(buf_h.at[:, pl.ds(0, 3 * third)], heads_h.at[:, pl.ds(0, 3 * third)], 8)


    wo_load.wait()

    def body(half):
        start = pl.multiple_of(half * HALF, TILE)
        window = pl.ds(pl.multiple_of(half * LOW, 64), WINDOW)
        mask_ref[...] = jnp.where(col_ref[pl.ds(start, HALF), 0:1] == key_ids[half], 0.0, -1000000000.0)

        def pair(p):
            pick = lambda block: pl.ds(pl.multiple_of(block * third + p * PAIR, PAIR), PAIR)

            def rows(at, count):
                return buf_h[pl.ds(pl.multiple_of(start + at, 32), count), pick(0)]

            def put(at, count, mixed, *logs):
                buf_h[pl.ds(pl.multiple_of(start + at, 32), count), pick(3)] = mixed
                for head in range(2):
                    lse_ref[half, 2 * p + head, 0:1, at : at + count] = jnp.transpose(logs[head])[0:1, :]

            attend_pair(start, rows, buf_h[window, pick(1)], buf_h[window, pick(2)], mask_ref, put)

        loop(third // PAIR, pair, False)

        @pl.when(half == 0)
        def _():
            pl.semaphore_wait(barrier, STEPS + 1)

        def project(j):
            i = half * (tiles // 2) + j
            own[rows_of(i), :] = nn(buf_h[rows_of(i), 3 * third : 4 * third], wo[...])
            swap(0, i, rows_of(i)).start()

        loop(tiles // 2, project, False)

    loop(2, body, False)
    save_o = load(buf_h.at[:, pl.ds(3 * third, third)], heads_h.at[:, pl.ds(3 * third, third)], 9)


    wi_load.wait()
    save_qkv.wait()
    root = 0.7978845608028654

    def hidden(i, c):
        u = nn(buf_n[rows_of(i), :], wi[:, columns(c * LANES)]) + bias_ref[c]
        t = jnp.tanh(u * (root + (root * 0.044715) * (u * u)))
        buf_h[rows_of(i), columns(c * LANES)] = (u * (0.5 + 0.5 * t)).astype(bf16)
        buf_d[rows_of(i), columns(c * LANES)] = u.astype(bf16)

    def body(i):
        total = swapped(0, i)
        middle = buf_d[rows_of(i), 0:dim].astype(f32) + total + vector(ob_ref)
        buf_m[rows_of(i), :] = middle
        unit, _ = standardize(middle)
        buf_n[rows_of(i), :] = (unit * vector(gain2_ref) + vector(shift2_ref)).astype(bf16)
        hidden(i, 0)

    loop(tiles, body, False)
    peer_is_free()
    save_mid = load(buf_m, mid_h, 10)
    save_o.wait()
    g_load.wait()
    gradient(0, buf_g, buf_h[:, 0:LANES])
    arrivals()

    def body(j):
        c = j + 1
        loop(tiles, lambda i: hidden(i, c), False)
        gradient(c, buf_g, buf_h[:, columns(c * LANES)])

    loop(blocks - 1, body)
    save_hid = load(buf_h, hid_h, 11)


    wb_load.wait()
    pl.semaphore_wait(free_sem, 1)

    def body(i):
        grad = buf_g[rows_of(i), :]
        for at in range(0, width, 512):
            u = buf_d[rows_of(i), at : at + 512].astype(f32)
            square = u * u
            t = jnp.tanh(u * (root + (root * 0.044715) * square))
            slope = 0.5 + 0.5 * t + (0.5 * u) * (1.0 - t * t) * (root + (3.0 * 0.044715 * root) * square)
            du = (nt(grad, wb[at : at + 512, :]) * slope).astype(bf16)
            buf_d[rows_of(i), at : at + 512] = du
            sums_ref[4:5, at : at + 512] += jnp.sum(du.astype(f32), 0, keepdims=True)
        own[rows_of(i), :] = nt(buf_d[rows_of(i), :], wi[...])
        swap(1, i, rows_of(i)).start()
        sums_ref[2:3, dim : 2 * dim] += jnp.sum(grad.astype(f32), 0, keepdims=True)

    loop(tiles, body)
    w3_late = load_w3(1)
    save_hid.wait()
    heads_load = load(heads_h, buf_h, 8)


    loop(4, lambda i: gradient(4 + i, buf_n, buf_d[:, columns(i * LANES)]))


    save_mid.wait()

    def body(i):
        grad = swapped(1, i)
        unit, inv = standardize(buf_m[rows_of(i), :])
        dh = buf_g[rows_of(i), :].astype(f32) + norm_back(unit, inv, vector(gain2_ref), grad)
        buf_m[rows_of(i), :] = dh
        dr = dh.astype(bf16)
        buf_n[rows_of(i), :] = dr
        buf_d[rows_of(i), 0:third] = nt(dr, wo[...]).astype(bf16)
        sums_ref[1:2, dim : 2 * dim] += jnp.sum(grad * unit, 0, keepdims=True)
        sums_ref[2:3, 0:dim] += jnp.sum(grad, 0, keepdims=True)
        sums_ref[1:2, 0:dim] += jnp.sum(dr.astype(f32), 0, keepdims=True)

    loop(tiles, body)
    peer_is_free()
    tok_late = load(tok_h, buf_g, 0)
    heads_load.wait()
    gradient(8, buf_n, buf_h[:, 3 * third : 4 * third])
    arrivals()


    first = lax.broadcasted_iota(jnp.int32, (1, PAIR), 1) < HEAD_DIM
    zero = jnp.zeros((), bf16)

    def body(at):
        p, half = at // 2, lax.rem(at, 2)
        pick = lambda block: pl.ds(pl.multiple_of(block * third + p * PAIR, PAIR), PAIR)
        window = pl.ds(pl.multiple_of(half * LOW, 64), WINDOW)
        keys, values = buf_h[window, pick(1)], buf_h[window, pick(2)]

        @pl.when(half == 0)
        def _():
            acc_k[...] = jnp.zeros_like(acc_k)
            acc_v[...] = jnp.zeros_like(acc_v)

        for begin, count in ((0, 256), (256, 352)):
            span = pl.ds(pl.multiple_of(half * HALF + begin, 32), count)
            rows, grads = buf_h[span, pick(0)], buf_d[span, pick(0)]
            same = col_ref[window, 0:1] == query_ids[half, :, begin : begin + count]
            mask = jnp.where(same, 0.0, -1000000000.0)
            parts = []
            for head in range(2):
                own_part = lambda a: jnp.where(first, a, zero) if head == 0 else jnp.where(first, zero, a)
                lse = lse_ref[half, 2 * p + head, 0:1, begin : begin + count]
                probs = jnp.exp(nt(keys, own_part(rows)) + mask - lse)
                back = nt(values, own_part(grads))
                inner = jnp.sum(probs * back, 0, keepdims=True)
                slant = (probs * (back - inner)).astype(bf16)
                parts.append((tn(slant, keys), nn(slant, rows), nn(probs.astype(bf16), grads)))
            dq, dk, dv = (jnp.where(first, a, b) for a, b in zip(*parts))
            dq = (dq * HEAD_DIM ** (-0.5)).astype(bf16)
            buf_d[span, pick(1)] = dq
            sums_ref[3:4, pick(0)] += jnp.sum(dq.astype(f32), 0, keepdims=True)
            acc_k[window, :] += dk
            acc_v[window, :] += dv

        @pl.when(half == 1)
        def _():
            buf_d[:, pick(2)] = acc_k[...].astype(bf16)
            dv = acc_v[...].astype(bf16)
            buf_d[:, pick(3)] = dv
            sums_ref[3:4, pick(1)] = jnp.sum(dv.astype(f32), 0, keepdims=True)

    loop(2 * (third // PAIR), body)
    hid_load = load(hid_h, buf_h, 8)


    tok_late.wait()

    def body(i):
        _, _, normed = first_norm(buf_g[rows_of(i), :])
        buf_n[rows_of(i), :] = normed

    loop(tiles, body, False)
    arrivals()
    loop(3, lambda i: gradient(9 + i, buf_n, buf_d[:, columns(third + i * LANES)]))


    for item in w3_late:
        item.wait()
    pl.semaphore_wait(free_sem, 1)

    def body(i):
        own[rows_of(i), :] = nt(buf_d[rows_of(i), third : 4 * third], wi[:, 0 : 3 * third])
        swap(2, i, rows_of(i)).start()

    loop(tiles, body)

    def body(i):
        grad = swapped(2, i)
        unit, inv, _ = first_norm(buf_g[rows_of(i), :])
        buf_g[rows_of(i), :] = (buf_m[rows_of(i), :] + norm_back(unit, inv, vector(gain1_ref), grad)).astype(bf16)
        sums_ref[0:1, 0:dim] += jnp.sum(grad * unit, 0, keepdims=True)
        sums_ref[0:1, dim : 2 * dim] += jnp.sum(grad, 0, keepdims=True)

    loop(tiles, body)
    peer_is_free()
    input_put = pltpu.make_async_copy(buf_g, input_h, put_sem.at[1])
    input_put.start()
    mid_load = load(mid_h, buf_m, 10)

    def whole_hop(step):
        return pltpu.make_async_remote_copy(
            src_ref=sums_ref,
            dst_ref=sums_in.at[step],
            send_sem=sums_send.at[step],
            recv_sem=sums_recv.at[step],
            device_id=(route.plain[step], core),
            device_id_type=mesh_id,
        )

    def add_sums(step):
        whole_hop(step).wait()
        sums_ref[...] += sums_in[step]

    whole_hop(0).start()


    hid_load.wait()
    pl.semaphore_wait(free_sem, 1)

    def body(i):
        own[rows_of(i), :] = nn(buf_h[rows_of(i), :], wb[...])
        swap(3, i, rows_of(i)).start()

    loop(tiles, body)
    add_sums(0)
    whole_hop(1).start()
    mid_load.wait()

    def body(i):
        buf_n[rows_of(i), :] = (buf_m[rows_of(i), :] + swapped(3, i) + vector(bb_ref)).astype(bf16)

    loop(tiles, body)
    layer_put = pltpu.make_async_copy(buf_n, layer_h, put_sem.at[0])
    layer_put.start()
    rest = left.pop(0)
    gap = len(rest) // STEPS
    for step in range(1, STEPS):
        for item in rest[(step - 1) * gap : step * gap]:
            finish(*item)
        add_sums(step)
        if step + 1 < STEPS:
            whole_hop(step + 1).start()
    for item in rest[(STEPS - 1) * gap :]:
        finish(*item)
    for chunk in range(COUNT):
        deliver(chunk).wait()
    input_put.wait()
    layer_put.wait()


def whole_layer(tokens, g, w3, wo, wi, wb, ids, gain1, shift1, qvb, ob, gain2, shift2, ib, bb):
    tok, dim = g.shape
    width = wi.shape[1]
    third = wo.shape[0]
    rows = dim // 16
    hbm = pl.BlockSpec(memory_space=pl.ANY)
    vmem = pl.BlockSpec(memory_space=pltpu.VMEM)
    dma = pltpu.SemaphoreType.DMA
    return pl.pallas_call(
        layer_kernel,
        in_specs=[hbm] * 6 + [vmem] * 9,
        out_specs=[hbm, hbm, hbm, vmem, hbm, hbm, hbm],
        out_shape=[
            jax.ShapeDtypeStruct((tok, dim), bf16),
            jax.ShapeDtypeStruct((tok, dim), bf16),
            jax.ShapeDtypeStruct((COUNT, rows, LANES), f32),
            jax.ShapeDtypeStruct((8, width), f32),
            jax.ShapeDtypeStruct((tok, width), bf16),
            jax.ShapeDtypeStruct((tok, width), bf16),
            jax.ShapeDtypeStruct((tok, dim), f32),
        ],
        scratch_shapes=[
            pltpu.VMEM((tok, width), bf16),
            pltpu.VMEM((tok, width), bf16),
            pltpu.VMEM((tok, dim), bf16),
            pltpu.VMEM((tok, dim), bf16),
            pltpu.VMEM((tok, dim), f32),
            pltpu.VMEM((tok, dim), f32),
            pltpu.VMEM((tok, dim), f32),
            pltpu.VMEM((dim, width), bf16),
            pltpu.VMEM((width, dim), bf16),
            pltpu.VMEM((third, dim), bf16),
            pltpu.VMEM((tok, PAIR), f32),
            pltpu.VMEM((tok, PAIR), f32),
            pltpu.VMEM((tok, PAIR), jnp.int32),
            pltpu.VMEM((2, 1, 640), jnp.int32),
            pltpu.VMEM((2, 1, WINDOW), jnp.int32),
            pltpu.VMEM((HALF, WINDOW), f32),
            pltpu.VMEM((width // LANES, 1, LANES), f32),
            pltpu.VMEM((2, third // HEAD_DIM, 8, 640), f32),
            pltpu.VMEM((COUNT, 16, rows, LANES), f32),
            pltpu.VMEM((COUNT, 8, rows, LANES), f32),
            pltpu.VMEM((COUNT, 4, rows, LANES), f32),
            pltpu.VMEM((COUNT, 2, rows, LANES), f32),
            pltpu.VMEM((COUNT, 1, rows, LANES), f32),
            pltpu.VMEM((STEPS, 8, width), f32),
            dma((12,)),
            dma((STEPS, COUNT)),
            dma((STEPS, COUNT)),
            dma((COUNT,)),
            dma((4, tok // TILE)),
            dma((4, tok // TILE)),
            dma((STEPS,)),
            dma((STEPS,)),
            dma((2,)),
            pltpu.SemaphoreType.REGULAR,
        ],
        compiler_params=pltpu.CompilerParams(vmem_limit_bytes=VMEM_LIMIT, collective_id=0, has_side_effects=True),
        cost_estimate=cost(34e9, 40e6),
        name="whole_layer",
    )(tokens, g, w3, wo, wi, wb, ids, gain1, shift1, qvb, ob, gain2, shift2, ib, bb)


def outputs_kernel(layer_h, input_h, grads_h, sums_ref, layer_o, input_o, *refs):
    n1g, n1s, qkv, qvb, out, obg, n2g, n2s, inw, ibg, back, bbg, held, kept, in_sem, out_sem = refs
    me = lax.axis_index("batch")
    dim = sums_ref.shape[1] // 2
    third = dim // 2
    pieces = 4
    rows = held.shape[1] // pieces
    grads_in = pltpu.make_async_copy(grads_h, kept, in_sem.at[2 * pieces])
    grads_in.start()
    moves = []
    for i, (source, target) in enumerate(((layer_h, layer_o), (input_h, input_o))):
        for j in range(pieces):
            span = pl.ds(j * rows, rows)
            at = i * pieces + j
            coming = pltpu.make_async_copy(source.at[span], held.at[i, span], in_sem.at[at])
            coming.start()
            moves.append((coming, pltpu.make_async_copy(held.at[i, span], target.at[span], out_sem.at[at])))

    def mine(row, at, size):
        n = size // 16
        values = jnp.broadcast_to(sums_ref[row : row + 1, at : at + size], (8, size))
        return pltpu.roll(values, size - me * n, 1)[0:1, 0:n]

    for ref, row, at in ((n1g, 0, 0), (n1s, 0, dim), (obg, 1, 0), (n2g, 1, dim), (n2s, 2, 0), (bbg, 2, dim)):
        ref[...] = mine(row, at, dim).reshape(-1)
    ibg[...] = mine(4, 0, 2 * dim).reshape(-1)
    qvb[0:1, :] = mine(3, 0, third)
    qvb[1:2, :] = mine(3, third, third)
    grads_in.wait()
    places = [back.at[:, pl.ds(c * LANES, LANES)] for c in range(4)]
    places += [inw.at[:, pl.ds(c * LANES, LANES)] for c in range(4)]
    places += [out] + [qkv.at[c] for c in range(3)]
    going = [pltpu.make_async_copy(kept.at[c], place, out_sem.at[2 * pieces + c]) for c, place in enumerate(places)]
    for item in going:
        item.start()
    for coming, leaving in moves:
        coming.wait()
        leaving.start()
    for item in going:
        item.wait()
    for _, leaving in moves:
        leaving.wait()


def outputs(layer, grad, grads, sums):
    rows, width = grads.shape[1], sums.shape[1]
    hbm = pl.BlockSpec(memory_space=pl.ANY)
    vmem = pl.BlockSpec(memory_space=pltpu.VMEM)
    small = jax.ShapeDtypeStruct((rows,), f32)
    shape = lambda *s: jax.ShapeDtypeStruct(s, f32)
    return pl.pallas_call(
        outputs_kernel,
        in_specs=[hbm, hbm, hbm, vmem],
        out_specs=[hbm, hbm, vmem, vmem, hbm, vmem, hbm, vmem, vmem, vmem, hbm, vmem, hbm, vmem],
        out_shape=[
            jax.ShapeDtypeStruct(layer.shape, bf16),
            jax.ShapeDtypeStruct(grad.shape, bf16),
            small,
            small,
            shape(3, rows, LANES),
            shape(2, rows // 2),
            shape(rows, LANES),
            small,
            small,
            small,
            shape(rows, width),
            shape(2 * rows),
            shape(rows, width),
            small,
        ],
        scratch_shapes=[
            pltpu.VMEM((2,) + layer.shape, bf16),
            pltpu.VMEM(grads.shape, f32),
            pltpu.SemaphoreType.DMA((9,)),
            pltpu.SemaphoreType.DMA((8 + COUNT,)),
        ],
        compiler_params=params(60),
        name="outputs",
    )(layer, grad, grads, sums)


def shards(
    tokens,
    seq_ids,
    cotangent,
    norm1_gain,
    norm1_shift,
    w_qkv,
    qv_bias,
    w_out,
    out_bias,
    norm2_gain,
    norm2_shift,
    w_in,
    in_bias,
    w_back,
    back_bias,
    batch,
):
    tok, dim = tokens.shape
    w3 = jnp.transpose(w_qkv, (1, 0, 2))
    if batch == 16:
        layer, grad, grads, sums, *_ = whole_layer(
            tokens, cotangent, w3, w_out, w_in, w_back, seq_ids,
            norm1_gain, norm1_shift, qv_bias, out_bias, norm2_gain, norm2_shift, in_bias, back_bias,
        )
        results = list(outputs(layer, grad, grads, sums))
        results[4] = jnp.transpose(results[4], (1, 0, 2))
        results[6], results[12] = results[6].T, results[12].T
        return tuple(results)

    row = lambda a: a.reshape(1, -1)
    ids_col, ids_row = seq_ids.reshape(tok, 1), seq_ids.reshape(1, tok)
    exchange = Exchange(batch)
    parts = exchange.first_parts()

    normed, q, k, v = project(tokens, row(norm1_gain), row(norm1_shift), w3, qv_bias)
    mixed, lse_a, part_a = attend(0, q, k, v, ids_col, ids_row, w_out)
    peer_a = other_core(part_a)
    mixed, lse_b, part_b = attend(1, q, k, v, ids_col, ids_row, w_out, (mixed,))
    peer_b = other_core(part_b)
    mlp = (row(out_bias), row(norm2_gain), row(norm2_shift), w_in, row(in_bias))
    state = hidden_layer(0, tokens, part_a, peer_a, *mlp)
    state = hidden_layer(1, tokens, part_b, peer_b, *mlp, before=tuple(state))
    middle, normed_two, hidden, slope = state

    back_parts = weight_grad(parts, exchange.place, cotangent, hidden)
    du, dn2, in_bias_sum, back_bias_sum = hidden_back(cotangent, slope, w_back, w_in)
    dn2_peer = other_core(dn2)
    in_parts = weight_grad(parts, exchange.place, normed_two, du)
    mlp_own = rows_matmul(hidden, w_back)
    mlp_peer = other_core(mlp_own)
    dh, dr, do, middle_sums = middle_back(middle, dn2, dn2_peer, cotangent, row(norm2_gain), w_out)
    out_parts = weight_grad(parts, exchange.place, dr, mixed)
    layer_out = (middle + (mlp_own + mlp_peer) + back_bias).astype(bf16)
    dq, dk, dv, qv_sums = attend_back(q, k, v, do, lse_a, lse_b, ids_col, ids_row)
    q_parts = weight_grad(parts, exchange.place, normed, dq)
    k_parts = weight_grad(parts, exchange.place, normed, dk)
    v_parts = weight_grad(parts, exchange.place, normed, dv)
    dn1 = normed_back(dq, dk, dv, w3)
    dn1_peer = other_core(dn1)
    tokens_grad, input_sums = input_back(tokens, dn1, dn1_peer, dh, row(norm1_gain))

    w_back_grad = jnp.transpose(exchange.reduce(back_parts))
    w_in_grad = exchange.reduce(in_parts)
    w_out_grad = jnp.transpose(exchange.reduce(out_parts))
    w_qkv_grad = jnp.stack([exchange.reduce(p) for p in (q_parts, k_parts, v_parts)], 1)

    pieces = [input_sums[0], input_sums[1], middle_sums[2], middle_sums[0], middle_sums[1], back_bias_sum[0]]
    pieces += [qv_sums[0], qv_sums[1], in_bias_sum[0]]
    packed = jnp.concatenate([p.reshape(batch, -1) for p in pieces], 1)
    vectors = lax.psum_scatter(packed, "batch", scatter_dimension=0, tiled=True)[0]
    out, at = [], 0
    for p in pieces:
        n = p.shape[0] // batch
        out.append(vectors[at : at + n])
        at += n
    n1g, n1s, obg, n2g, n2s, bbg, qb, vb, ibg = out
    return (
        layer_out,
        tokens_grad,
        n1g,
        n1s,
        w_qkv_grad,
        jnp.stack([qb, vb]),
        w_out_grad,
        obg,
        n2g,
        n2s,
        w_in_grad,
        ibg,
        w_back_grad,
        bbg,
    )


def solution(mesh):
    in_specs = (
        P("batch", None),
        P("batch"),
        P("batch", None),
        P(),
        P(),
        P(None, None, "tp"),
        P(None, "tp"),
        P("tp", None),
        P(),
        P(),
        P(),
        P(None, "tp"),
        P("tp"),
        P("tp", None),
        P(),
    )
    out_specs = (
        P("batch", None),
        P("batch", None),
        P("batch"),
        P("batch"),
        P("batch", None, "tp"),
        P(None, ("tp", "batch")),
        P("tp", "batch"),
        P("batch"),
        P("batch"),
        P("batch"),
        P("batch", "tp"),
        P(("tp", "batch")),
        P("tp", "batch"),
        P("batch"),
    )
    body = functools.partial(shards, batch=mesh.shape["batch"])
    return jax.shard_map(body, mesh=mesh, in_specs=in_specs, out_specs=out_specs, check_vma=False)
```

```python
import functools

import jax
import jax.numpy as jnp
from jax import lax
from jax.experimental import pallas as pl
from jax.experimental.pallas import tpu as pltpu
from jax.sharding import PartitionSpec as P

HEAD_DIM = 64
PAIR = 2 * HEAD_DIM
HALF = 608
TILE = 304
LANES = 384
VMEM_LIMIT = 63 << 20
WINDOW = 768
LOW = 448
ROWS = ((0, 128), (128, 128), (256, 128), (384, 128), (512, 96))
TILES = ((0, 256, 0, 608), (256, 352, 0, 688), (608, 256, 448, 1216), (864, 352, 608, 1216))
f32 = jnp.float32
bf16 = jnp.bfloat16


def params(mib):
    return pltpu.CompilerParams(vmem_limit_bytes=mib << 20)


def cost(flops, nbytes, trans=0):
    return pl.CostEstimate(flops=int(flops), bytes_accessed=int(nbytes), transcendentals=int(trans))


def nn(a, b):
    return jnp.dot(a, b, preferred_element_type=f32)


def nt(a, b):
    return lax.dot_general(a, b, (((1,), (1,)), ((), ())), preferred_element_type=f32)


def tn(a, b):
    return lax.dot_general(a, b, (((0,), (0,)), ((), ())), preferred_element_type=f32)


def standardize(values):
    center = values - jnp.mean(values, -1, keepdims=True)
    spread = jnp.mean(center * center, -1, keepdims=True)
    inv = lax.rsqrt(spread + 1e-06)
    return center * inv, inv


def norm_back(unit, inv, gain, grad):
    scaled = grad * gain
    return inv * (
        scaled
        - jnp.mean(scaled, -1, keepdims=True)
        - unit * jnp.mean(scaled * unit, -1, keepdims=True)
    )


def whole(shape):
    return pl.BlockSpec(shape, lambda *_: (0,) * len(shape))


def project_kernel(x_ref, gain_ref, shift_ref, w_ref, bias_ref, n_ref, q_ref, k_ref, v_ref):
    unit, _ = standardize(x_ref[...].astype(f32))
    normed = (unit * gain_ref[...] + shift_ref[...]).astype(bf16)
    n_ref[...] = normed
    scale = HEAD_DIM ** (-0.5)
    q_ref[...] = ((nn(normed, w_ref[0]) + bias_ref[0:1]).astype(bf16).astype(f32) * scale).astype(bf16)
    k_ref[...] = nn(normed, w_ref[1]).astype(bf16)
    v_ref[...] = (nn(normed, w_ref[2]) + bias_ref[1:2]).astype(bf16)


def project(tokens, gain, shift, w3, qv_bias):
    tok, dim = tokens.shape
    width = w3.shape[2]
    rows = lambda n: pl.BlockSpec((TILE, n), lambda i: (i, 0))
    out = jax.ShapeDtypeStruct((tok, width), bf16)
    return pl.pallas_call(
        project_kernel,
        grid=(tok // TILE,),
        in_specs=[rows(dim), whole((1, dim)), whole((1, dim)), whole(w3.shape), whole((2, width))],
        out_specs=[rows(dim), rows(width), rows(width), rows(width)],
        out_shape=[jax.ShapeDtypeStruct((tok, dim), bf16), out, out, out],
        compiler_params=params(60),
        cost_estimate=cost(2 * tok * dim * 3 * width, tok * (2 * dim + 3 * width) * 2 + w3.size * 2),
        name="project",
    )(tokens, gain, shift, w3, qv_bias)


def attend_kernel(half, q_ref, k_ref, v_ref, col_ref, row_ref, w_ref, *refs):
    o_ref, lse_ref, part_ref, *mask_refs = refs[-5:]
    step = pl.program_id(0)
    tiles = TILES[2 * half : 2 * half + 2]

    @pl.when(step == 0)
    def _():
        for (start, count, low, high), mask_ref in zip(tiles, mask_refs):
            at = start - half * HALF
            same = col_ref[at : at + count, :] == row_ref[:, low:high]
            mask_ref[...] = jnp.where(same, 0.0, -1000000000.0)

    first = lax.broadcasted_iota(jnp.int32, (1, PAIR), 1) < HEAD_DIM
    zero = jnp.zeros((), bf16)
    one = jnp.ones((), bf16)
    for tile, ((start, count, low, high), mask_ref) in enumerate(zip(tiles, mask_refs)):
        at = start - half * HALF
        rows = q_ref[at : at + count, :]
        keys = k_ref[low:high, :]
        values = v_ref[low:high, :]
        with_ones = (jnp.where(first, values, one), jnp.where(first, one, values))
        mask = mask_ref[...]
        outs, logs = [], []
        for head in range(2):
            own = jnp.where(first, rows, zero) if head == 0 else jnp.where(first, zero, rows)
            scores = nt(own, keys) + mask
            top = jnp.max(scores, -1, keepdims=True)
            expo = jnp.exp(scores - top).astype(bf16)
            mixed = nn(expo, with_ones[head])
            total = pltpu.roll(mixed, HEAD_DIM, 1)
            outs.append(mixed / total)
            logs.append(top + jnp.log(total))
        mixed = jnp.where(first, outs[0], outs[1]).astype(bf16)
        o_ref[at : at + count, :] = mixed
        turned = jnp.transpose(jnp.where(first, logs[0], logs[1]))
        lse_ref[tile, pl.ds(2 * step, 1), 0:count] = turned[0:1, :]
        lse_ref[tile, pl.ds(2 * step + 1, 1), 0:count] = turned[HEAD_DIM : HEAD_DIM + 1, :]
        part = nn(mixed, w_ref[...])

        @pl.when(step == 0)
        def _():
            part_ref[at : at + count, :] = part

        @pl.when(step > 0)
        def _():
            part_ref[at : at + count, :] += part


def attend(half, q, k, v, ids_col, ids_row, w_out, before=()):
    tok, width = q.shape
    dim = w_out.shape[1]
    pair_rows = pl.BlockSpec((HALF, PAIR), lambda p: (half, p))
    pair_all = pl.BlockSpec((tok, PAIR), lambda p: (0, p))
    tiles = TILES[2 * half : 2 * half + 2]
    return pl.pallas_call(
        functools.partial(attend_kernel, half),
        grid=(width // PAIR,),
        in_specs=[
            pair_rows,
            pair_all,
            pair_all,
            pl.BlockSpec((HALF, 1), lambda p: (half, 0)),
            whole((1, tok)),
            pl.BlockSpec((PAIR, dim), lambda p: (p, 0)),
        ]
        + [pl.BlockSpec(memory_space=pl.ANY)] * len(before),
        out_specs=[pair_rows, whole((2, 8, LANES)), whole((HALF, dim))],
        out_shape=[
            jax.ShapeDtypeStruct((tok, width), bf16),
            jax.ShapeDtypeStruct((2, 8, LANES), f32),
            jax.ShapeDtypeStruct((HALF, dim), f32),
        ],
        scratch_shapes=[pltpu.VMEM((count, high - low), f32) for _, count, low, high in tiles],
        input_output_aliases={6 + i: i for i in range(len(before))},
        compiler_params=params(60),
        cost_estimate=cost(16 * HALF * 650 * width, tok * width * 6 + HALF * dim * 4),
        name="attend",
    )(q, k, v, ids_col, ids_row, w_out, *before)


def hidden_kernel(x_ref, own_ref, peer_ref, ob_ref, gain_ref, shift_ref, w_ref, ib_ref, *refs):
    mid_ref, n_ref, hid_ref, slope_ref = refs[-4:]
    middle = x_ref[...].astype(f32) + (own_ref[...] + peer_ref[...]) + ob_ref[...]
    mid_ref[...] = middle
    unit, _ = standardize(middle)
    normed = (unit * gain_ref[...] + shift_ref[...]).astype(bf16)
    n_ref[...] = normed
    width = w_ref.shape[1]
    piece = 512
    c0 = 0.7978845608028654
    for at in range(0, width, piece):
        u = nn(normed, w_ref[:, at : at + piece]) + ib_ref[:, at : at + piece]
        sq = u * u
        t = jnp.tanh(u * (c0 + (c0 * 0.044715) * sq))
        cdf = 0.5 + 0.5 * t
        hid_ref[:, at : at + piece] = (u * cdf).astype(bf16)
        slope = cdf + (0.5 * u) * (1.0 - t * t) * (c0 + (3.0 * 0.044715 * c0) * sq)
        slope_ref[:, at : at + piece] = slope.astype(bf16)


def hidden_layer(half, tokens, own, peer, out_bias, gain, shift, w_in, in_bias, before=()):
    tok, dim = tokens.shape
    width = w_in.shape[1]
    per = HALF // TILE
    glob = lambda n: pl.BlockSpec((TILE, n), lambda i: (i + per * half, 0))
    loc = lambda n: pl.BlockSpec((TILE, n), lambda i: (i, 0))
    return pl.pallas_call(
        hidden_kernel,
        grid=(per,),
        in_specs=[
            glob(dim),
            loc(dim),
            loc(dim),
            whole((1, dim)),
            whole((1, dim)),
            whole((1, dim)),
            whole(w_in.shape),
            whole((1, width)),
        ]
        + [pl.BlockSpec(memory_space=pl.ANY)] * len(before),
        out_specs=[glob(dim), glob(dim), glob(width), glob(width)],
        out_shape=[
            jax.ShapeDtypeStruct((tok, dim), f32),
            jax.ShapeDtypeStruct((tok, dim), bf16),
            jax.ShapeDtypeStruct((tok, width), bf16),
            jax.ShapeDtypeStruct((tok, width), bf16),
        ],
        input_output_aliases={8 + i: i for i in range(len(before))},
        compiler_params=params(60),
        cost_estimate=cost(2 * HALF * dim * width, HALF * (dim * 16 + width * 4) + w_in.size * 2, HALF * width),
        name="hidden_layer",
    )(tokens, own, peer, out_bias, gain, shift, w_in, in_bias, *before)


def matmul_kernel(a_ref, b_ref, o_ref):
    o_ref[...] = nn(a_ref[...], b_ref[...])


def rows_matmul(a, b):
    tok, depth = a.shape
    width = b.shape[1]
    return pl.pallas_call(
        matmul_kernel,
        grid=(tok // TILE,),
        in_specs=[pl.BlockSpec((TILE, depth), lambda i: (i, 0)), whole(b.shape)],
        out_specs=pl.BlockSpec((TILE, width), lambda i: (i, 0)),
        out_shape=jax.ShapeDtypeStruct((tok, width), f32),
        compiler_params=params(60),
        cost_estimate=cost(2 * tok * depth * width, tok * (depth * 2 + width * 4) + b.size * 2),
        name="mlp_out",
    )(a, b)


def hidden_back_kernel(g_ref, slope_ref, wb_ref, wi_ref, du_ref, dn_ref, db_ref, gb_ref):
    step = pl.program_id(0)
    grad = g_ref[...]
    width = slope_ref.shape[1]
    piece = 512
    total = None
    sums = []
    for at in range(0, width, piece):
        back = nt(grad, wb_ref[at : at + piece, :])
        du = (back * slope_ref[:, at : at + piece].astype(f32)).astype(bf16)
        du_ref[:, at : at + piece] = du
        sums.append(jnp.sum(du.astype(f32), 0, keepdims=True))
    dn_ref[...] = nt(du_ref[...], wi_ref[...])

    @pl.when(step == 0)
    def _():
        db_ref[...] = jnp.zeros_like(db_ref)
        gb_ref[...] = jnp.zeros_like(gb_ref)

    for i, at in enumerate(range(0, width, piece)):
        db_ref[:, at : at + piece] += sums[i]
    gb_ref[...] += jnp.sum(grad.astype(f32), 0, keepdims=True)


def hidden_back(cotangent, slope, w_back, w_in):
    tok, dim = cotangent.shape
    width = slope.shape[1]
    rows = lambda n: pl.BlockSpec((TILE, n), lambda i: (i, 0))
    return pl.pallas_call(
        hidden_back_kernel,
        grid=(tok // TILE,),
        in_specs=[rows(dim), rows(width), whole(w_back.shape), whole(w_in.shape)],
        out_specs=[rows(width), rows(dim), whole((1, width)), whole((1, dim))],
        out_shape=[
            jax.ShapeDtypeStruct((tok, width), bf16),
            jax.ShapeDtypeStruct((tok, dim), f32),
            jax.ShapeDtypeStruct((1, width), f32),
            jax.ShapeDtypeStruct((1, dim), f32),
        ],
        compiler_params=params(60),
        cost_estimate=cost(4 * tok * dim * width, tok * (dim * 6 + width * 4) + w_in.size * 4),
        name="hidden_back",
    )(cotangent, slope, w_back, w_in)


def middle_back_kernel(mid_ref, own_ref, peer_ref, g_ref, gain_ref, w_ref, dh_ref, dr_ref, do_ref, sum_ref):
    step = pl.program_id(0)
    unit, inv = standardize(mid_ref[...])
    grad = own_ref[...] + peer_ref[...]
    dh = g_ref[...].astype(f32) + norm_back(unit, inv, gain_ref[...], grad)
    dh_ref[...] = dh
    dr = dh.astype(bf16)
    dr_ref[...] = dr
    do_ref[...] = nt(dr, w_ref[...]).astype(bf16)

    @pl.when(step == 0)
    def _():
        sum_ref[...] = jnp.zeros_like(sum_ref)

    sum_ref[0:1] += jnp.sum(grad * unit, 0, keepdims=True)
    sum_ref[1:2] += jnp.sum(grad, 0, keepdims=True)
    sum_ref[2:3] += jnp.sum(dr.astype(f32), 0, keepdims=True)


def middle_back(middle, own, peer, cotangent, gain, w_out):
    tok, dim = middle.shape
    width = w_out.shape[0]
    rows = lambda n: pl.BlockSpec((TILE, n), lambda i: (i, 0))
    return pl.pallas_call(
        middle_back_kernel,
        grid=(tok // TILE,),
        in_specs=[rows(dim), rows(dim), rows(dim), rows(dim), whole((1, dim)), whole(w_out.shape)],
        out_specs=[rows(dim), rows(dim), rows(width), whole((8, dim))],
        out_shape=[
            jax.ShapeDtypeStruct((tok, dim), f32),
            jax.ShapeDtypeStruct((tok, dim), bf16),
            jax.ShapeDtypeStruct((tok, width), bf16),
            jax.ShapeDtypeStruct((8, dim), f32),
        ],
        compiler_params=params(60),
        cost_estimate=cost(2 * tok * dim * width, tok * (dim * 20 + width * 2) + w_out.size * 2),
        name="middle_back",
    )(middle, own, peer, cotangent, gain, w_out)


def attend_back_tile(tile, keys, values, rows, grads, mask, lse_rows):
    first = lax.broadcasted_iota(jnp.int32, (1, PAIR), 1) < HEAD_DIM
    zero = jnp.zeros((), bf16)
    parts = []
    for head in range(2):
        pick = lambda a: jnp.where(first, a, zero) if head == 0 else jnp.where(first, zero, a)
        probs = jnp.exp(nt(keys, pick(rows)) + mask - lse_rows[head])
        back = nt(values, pick(grads))
        inner = jnp.sum(probs * back, 0, keepdims=True)
        slant = (probs * (back - inner)).astype(bf16)
        dv = nn(probs.astype(bf16), grads)
        dk = nn(slant, rows)
        dq = tn(slant, keys)
        parts.append((dq, dk, dv))
    dq, dk, dv = (jnp.where(first, a, b) for a, b in zip(*parts))
    return (dq * HEAD_DIM ** (-0.5)).astype(bf16), dk, dv


def attend_back_pair(q, k, v, do, lse, col_ref, row_ref, put_dq, acc_k, acc_v, after=lambda tile: None):
    total = None
    for tile, (start, count, low, high) in enumerate(TILES):
        span = slice(start, start + count)
        mask = jnp.where(col_ref[low:high, 0:1] == row_ref[:, span], 0.0, -1000000000.0)
        dq, dk, dv = attend_back_tile(
            tile, k(slice(low, high)), v(slice(low, high)), q(span), do(span), mask, lse(tile, count)
        )
        put_dq(span, dq)
        top = jnp.sum(dq.astype(f32), 0, keepdims=True)
        total = top if total is None else total + top
        edge = 0 if tile == 0 else TILES[tile - 1][3]
        for acc, part in ((acc_k, dk), (acc_v, dv)):
            if edge > low:
                acc[low:edge, :] += part[: edge - low]
            if edge < high:
                acc[edge:high, :] = part[max(edge - low, 0) :]
        after(tile)
    return total


def attend_back_kernel(q_ref, k_ref, v_ref, do_ref, lse_a, lse_b, col_ref, row_ref, dq_ref, dk_ref, dv_ref, sum_ref, acc_k, acc_v):
    step = pl.program_id(0)

    def lse(tile, count):
        ref = lse_a if tile < 2 else lse_b
        return [ref[tile % 2, pl.ds(2 * step + head, 1), 0:count] for head in range(2)]

    def put_dq(span, value):
        dq_ref[span, :] = value

    take = lambda ref: lambda span: ref[span, :]
    total = attend_back_pair(
        take(q_ref), take(k_ref), take(v_ref), take(do_ref), lse, col_ref, row_ref, put_dq, acc_k, acc_v
    )
    dk_ref[...] = acc_k[...].astype(bf16)
    dv = acc_v[...].astype(bf16)
    dv_ref[...] = dv
    sum_ref[...] = jnp.zeros_like(sum_ref)
    sum_ref[0:1, :] = total
    sum_ref[1:2, :] = jnp.sum(dv.astype(f32), 0, keepdims=True)


def attend_back(q, k, v, do, lse_a, lse_b, ids_col, ids_row):
    tok, width = q.shape
    pair = pl.BlockSpec((tok, PAIR), lambda p: (0, p))
    out = jax.ShapeDtypeStruct((tok, width), bf16)
    return pl.pallas_call(
        attend_back_kernel,
        grid=(width // PAIR,),
        in_specs=[pair, pair, pair, pair, whole(lse_a.shape), whole(lse_b.shape), whole((tok, 1)), whole((1, tok))],
        out_specs=[pair, pair, pair, pl.BlockSpec((8, PAIR), lambda p: (0, p))],
        out_shape=[out, out, out, jax.ShapeDtypeStruct((8, width), f32)],
        scratch_shapes=[pltpu.VMEM((tok, PAIR), f32), pltpu.VMEM((tok, PAIR), f32)],
        compiler_params=params(60),
        cost_estimate=cost(4 * 10 * tok * HALF * width, tok * width * 18),
        name="attend_back",
    )(q, k, v, do, lse_a, lse_b, ids_col, ids_row)


def normed_back_kernel(dq_ref, dk_ref, dv_ref, w_ref, o_ref):
    o_ref[...] = nt(dq_ref[...], w_ref[0]) + nt(dk_ref[...], w_ref[1]) + nt(dv_ref[...], w_ref[2])


def normed_back(dq, dk, dv, w3):
    tok, width = dq.shape
    dim = w3.shape[1]
    rows = lambda n: pl.BlockSpec((TILE, n), lambda i: (i, 0))
    return pl.pallas_call(
        normed_back_kernel,
        grid=(tok // TILE,),
        in_specs=[rows(width), rows(width), rows(width), whole(w3.shape)],
        out_specs=rows(dim),
        out_shape=jax.ShapeDtypeStruct((tok, dim), f32),
        compiler_params=params(60),
        cost_estimate=cost(6 * tok * dim * width, tok * (dim * 4 + width * 6) + w3.size * 2),
        name="normed_back",
    )(dq, dk, dv, w3)


def input_back_kernel(x_ref, own_ref, peer_ref, dh_ref, gain_ref, o_ref, sum_ref):
    step = pl.program_id(0)
    unit, inv = standardize(x_ref[...].astype(f32))
    grad = own_ref[...] + peer_ref[...]
    o_ref[...] = (dh_ref[...] + norm_back(unit, inv, gain_ref[...], grad)).astype(bf16)

    @pl.when(step == 0)
    def _():
        sum_ref[...] = jnp.zeros_like(sum_ref)

    sum_ref[0:1] += jnp.sum(grad * unit, 0, keepdims=True)
    sum_ref[1:2] += jnp.sum(grad, 0, keepdims=True)


def input_back(tokens, own, peer, dh, gain):
    tok, dim = tokens.shape
    rows = pl.BlockSpec((TILE, dim), lambda i: (i, 0))
    return pl.pallas_call(
        input_back_kernel,
        grid=(tok // TILE,),
        in_specs=[rows, rows, rows, rows, whole((1, dim))],
        out_specs=[rows, whole((8, dim))],
        out_shape=[jax.ShapeDtypeStruct((tok, dim), bf16), jax.ShapeDtypeStruct((8, dim), f32)],
        compiler_params=params(60),
        cost_estimate=cost(20 * tok * dim, tok * dim * 16),
        name="input_back",
    )(tokens, own, peer, dh, gain)


def grad_kernel(parts, group, place_ref, a_ref, b_ref, *refs):
    outs, turned = refs[:parts], refs[parts]

    @pl.when(pl.program_id(0) == 0)
    def _():
        flat = jnp.transpose(a_ref[...])
        if group:
            for g in range(flat.shape[0] // group):
                at = pl.multiple_of(place_ref[g] * group, group)
                turned[pl.ds(at, group), :] = flat[g * group : (g + 1) * group, :]
        else:
            turned[...] = flat

    total = nn(turned[...], b_ref[...])
    rows = total.shape[0] // parts
    for i, out in enumerate(outs):
        out[...] = total[i * rows : (i + 1) * rows, :]


def weight_grad(parts, place, a, b):
    tok, dim = a.shape
    width = b.shape[1]
    step = 384
    count = place.shape[0]
    group = dim // count
    if group % 16:
        order = jnp.argsort(place)
        rows = (order[:, None] * group + jnp.arange(group)[None, :]).reshape(dim)
        a = jnp.take(a, rows, axis=1)
        group = 0
    rows = dim // parts
    return pl.pallas_call(
        functools.partial(grad_kernel, parts, group),
        grid_spec=pltpu.PrefetchScalarGridSpec(
            num_scalar_prefetch=1,
            grid=(width // step,),
            in_specs=[
                pl.BlockSpec((tok, dim), lambda i, *_: (0, 0)),
                pl.BlockSpec((tok, step), lambda i, *_: (0, i)),
            ],
            out_specs=[pl.BlockSpec((rows, step), lambda i, *_: (0, i))] * parts,
            scratch_shapes=[pltpu.VMEM((dim, tok), bf16)],
        ),
        out_shape=[jax.ShapeDtypeStruct((rows, width), f32)] * parts,
        compiler_params=params(60),
        cost_estimate=cost(2 * tok * dim * width, tok * (dim + width) * 2 + dim * width * 4),
        name="weight_grad",
    )(place, a, b)


class Exchange:
    def __init__(self, batch):
        side = 1
        while side * side * 4 < batch:
            side *= 2
        self.batch = batch
        sizes = (batch // (side * side), side, side)
        strides = (side * side, side, 1)
        axes = list(zip(sizes, strides))
        slow, mid, fast = axes
        self.orders = ((fast, mid, slow), (mid, fast, slow))
        me = lax.axis_index("batch")
        core = lax.axis_index("tp")
        away = jnp.arange(batch, dtype=jnp.int32) ^ me
        places = []
        for order in self.orders:
            place = jnp.zeros_like(away)
            for size, stride in order:
                place = place * size + (away // stride) % size
            places.append(place)
        self.place = jnp.where(core == 0, places[0], places[1]).astype(jnp.int32)

    def first_parts(self):
        return self.orders[0][0][0]

    def swap(self, block, phase, k):
        perm = []
        for i in range(self.batch):
            for core in range(2):
                _, stride = self.orders[core][phase]
                perm.append((2 * i + core, 2 * (i ^ (k * stride)) + core))
        return lax.ppermute(block, ("batch", "tp"), perm)

    def reduce(self, parts):
        for phase in range(3):
            got = [self.swap(parts[k], phase, k) for k in range(1, len(parts))]
            if phase == 2:
                total = parts[0]
                for g in got:
                    total = total + g
                return total
            size = self.orders[0][phase + 1][0]
            rows = parts[0].shape[0] // size
            cut = lambda a, i: lax.slice_in_dim(a, i * rows, (i + 1) * rows, axis=0)
            following = []
            for i in range(size):
                total = cut(parts[0], i)
                for g in got:
                    total = total + cut(g, i)
                following.append(total)
            parts = following


def other_core(values):
    return lax.ppermute(values, "tp", [(0, 1), (1, 0)])


COUNT = 12
STEPS = 4
PLAN = (
    (), (), (), (), ((0, 0),), (), (), (), ((1, 0),), ((0, 1),), ((2, 0),), (), (), (), (), ((1, 1), (3, 0),), (),
    (), ((5, 0), (3, 1), (4, 0), (0, 2),), ((1, 2),), ((4, 1),), ((6, 0), (2, 1),), ((8, 0),), ((3, 2),), (),
    ((0, 3), (6, 1), (7, 0),), ((1, 3),), ((2, 2),), (), ((4, 2),), (), ((5, 1), (3, 3), (7, 1), (6, 2),),
    ((8, 1),), (), (), ((5, 2),), (), (), ((8, 2),), ((9, 0),), (), (), ((11, 0),),
    ((2, 3), (4, 3), (9, 1), (10, 0), (7, 2), (6, 3), (5, 3), (11, 1), (10, 1), (8, 3), (11, 2), (9, 2), (7, 3), (10, 2), (11, 3), (9, 3), (10, 3),),
)


ORDERS = ((1, 2, 4, 8), (4, 1, 2, 8), (1, 4, 2, 8))
ORDER_OF = (0, 0, 1, 0, 0, 1, 0, 0, 1, 0, 0, 1)


class Route:
    def __init__(self):
        self.me = lax.axis_index("batch")
        self.core = core = lax.axis_index("tp")
        self.bits = {s: lax.rem(self.me // s, 2) for s in (1, 2, 4, 8)}
        near = {s: self.me + s * (1 - 2 * self.bits[s]) for s in (1, 2, 4, 8)}
        side = near[1] * (1 - core) + near[2] * core
        other = near[2] * (1 - core) + near[1] * core
        self.plain = (side, other, near[4], near[8])
        self.near = {1: side, 2: other, 4: near[4], 8: near[8]}
        self.weights = []
        for order in ORDERS:
            at = {s: 8 >> order.index(s) for s in order}
            first, second = at[1] * (1 - core) + at[2] * core, at[2] * (1 - core) + at[1] * core
            self.weights.append({1: first, 2: second, 4: at[4], 8: at[8]})

    def by_order(self, chunk, values):
        if isinstance(chunk, int):
            return values[ORDER_OF[chunk]]
        total = values[0]
        for kind in range(1, len(ORDERS)):
            own = sum((chunk == c).astype(jnp.int32) for c in range(COUNT) if ORDER_OF[c] == kind)
            total = total + own * (values[kind] - values[0])
        return total

    def partner(self, chunk, step):
        return self.by_order(chunk, [self.near[order[step]] for order in ORDERS])

    def places(self, chunk):
        terms = {}
        for s in (1, 2, 4, 8):
            weight = self.by_order(chunk, [w[s] for w in self.weights])
            terms[s] = (self.bits[s] * weight, (1 - self.bits[s]) * weight)
        return [sum(terms[s][(g // s) % 2] for s in (1, 2, 4, 8)) for g in range(16)]


def attend_pair(rows_at, rows, keys, values, mask_ref, put):
    first = lax.broadcasted_iota(jnp.int32, (1, PAIR), 1) < HEAD_DIM
    zero = jnp.zeros((), bf16)
    with_ones = jnp.concatenate([values, jnp.ones_like(values)], 1)
    for at, count in ROWS:
        part = rows(at, count)
        both = jnp.concatenate([jnp.where(first, part, zero), jnp.where(first, zero, part)], 0)
        mask = mask_ref[at : at + count, :]
        scores = nt(both, keys) + jnp.concatenate([mask, mask], 0)
        top = jnp.max(scores, -1, keepdims=True)
        mixed = nn(jnp.exp(scores - top).astype(bf16), with_ones)
        total = mixed[:, PAIR:]
        mixed = mixed[:, :PAIR] / total
        logs = top + jnp.log(total)
        put(at, count, jnp.where(first, mixed[:count], mixed[count:]).astype(bf16), logs[:count], logs[count:])


def layer_kernel(
    tok_h, g_h, w3_h, wo_h, wi_h, wb_h,
    ids_ref, gain1_ref, shift1_ref, qvb_ref, ob_ref, gain2_ref, shift2_ref, ib_ref, bb_ref,
    layer_h, input_h, grads_h, sums_ref, heads_h, hid_h, mid_h,
    buf_h, buf_d, buf_n, buf_g, buf_m, own, peer, wi, wb, wo, acc_k, acc_v, col_ref, query_ids, key_ids, mask_ref,
    bias_ref, lse_ref, log_ref, chunks, recv0, recv1, recv2, recv3, sums_in,
    load_sem, send_sem, recv_sem, grad_sem, swap_send, swap_recv, sums_send, sums_recv, put_sem, free_sem,
):
    mesh_id = pl.DeviceIdType.MESH
    route = Route()
    me, core = route.me, route.core
    tok, dim = buf_g.shape
    width = buf_h.shape[1]
    third = wo.shape[0]
    tiles = tok // TILE
    blocks = width // LANES
    recvs = (recv0, recv1, recv2, recv3)
    vector = lambda ref: ref[...].reshape(1, -1)

    barrier = pltpu.get_barrier_semaphore()
    for other in route.plain:
        pl.semaphore_signal(barrier, inc=1, device_id=(other, core), device_id_type=mesh_id)
    pl.semaphore_signal(barrier, inc=1, device_id=(me, 1 - core), device_id_type=mesh_id)

    def load(source, target, at):
        copy = pltpu.make_async_copy(source, target, load_sem.at[at])
        copy.start()
        return copy

    def load_w3(at):
        return [load(w3_h.at[c], wi.at[:, pl.ds(c * third, third)], at + c) for c in range(3)]

    tok_load = load(tok_h, buf_d.at[:, pl.ds(0, dim)], 0)
    w3_load = load_w3(1)
    wo_load = load(wo_h, wo, 4)


    def hop(chunk, step):
        half = 8 >> step
        return pltpu.make_async_remote_copy(
            src_ref=chunks.at[chunk, pl.ds(half, half)],
            dst_ref=recvs[step].at[chunk],
            send_sem=send_sem.at[step, chunk],
            recv_sem=recv_sem.at[step, chunk],
            device_id=(route.partner(chunk, step), core),
            device_id_type=mesh_id,
        )

    def deliver(chunk):
        return pltpu.make_async_copy(chunks.at[chunk, 0], grads_h.at[chunk], grad_sem.at[chunk])

    def finish(chunk, step):
        got = hop(chunk, step)
        got.wait_send()
        got.wait_recv()

        def add(g, carry):
            chunks[chunk, g] += recvs[step][chunk, g]
            return carry

        lax.fori_loop(0, 8 >> step, add, 0)
        if step < STEPS - 1:
            hop(chunk, step + 1).start()
        else:
            deliver(chunk).start()

    left = list(PLAN)

    def arrivals():
        for chunk, step in left.pop(0):
            finish(chunk, step)

    def loop(count, body, planned=True):
        each = [left.pop(0) for _ in range(count)] if planned else []

        def turn(i, carry):
            body(i)
            for at, now in enumerate(each):
                if now:

                    @pl.when(i == at)
                    def _():
                        for chunk, step in now:
                            finish(chunk, step)

            return carry

        lax.fori_loop(0, count, turn, 0)

    def gradient(chunk, source, right):
        places = route.places(chunk)
        total = tn(source[...], right)
        rows = dim // 16
        for g in range(16):
            chunks[chunk, places[g]] = total[g * rows : (g + 1) * rows, :]
        hop(chunk, 0).start()

    def columns(at):
        return pl.ds(pl.multiple_of(at, PAIR), LANES)

    def rows_of(i):
        return pl.ds(pl.multiple_of(i * TILE, TILE), TILE)


    def swap(turn_at, i, rows):
        return pltpu.make_async_remote_copy(
            src_ref=own.at[rows],
            dst_ref=peer.at[rows],
            send_sem=swap_send.at[turn_at, i],
            recv_sem=swap_recv.at[turn_at, i],
            device_id=(me, 1 - core),
            device_id_type=mesh_id,
        )

    def swapped(turn_at, i):
        got = swap(turn_at, i, rows_of(i))
        got.wait_send()
        got.wait_recv()
        return own[rows_of(i), :] + peer[rows_of(i), :]

    def peer_is_free():
        pl.semaphore_signal(free_sem, inc=1, device_id=(me, 1 - core), device_id_type=mesh_id)


    ids = vector(ids_ref)
    for half in range(2):
        query_ids[half, :, 0:HALF] = ids[:, half * HALF : (half + 1) * HALF]
        key_ids[half] = ids[:, half * LOW : half * LOW + WINDOW]
    col_ref[...] = jnp.transpose(jnp.broadcast_to(ids, (PAIR, tok)))
    for c in range(blocks):
        bias_ref[c] = vector(ib_ref)[:, c * LANES : (c + 1) * LANES]
    sums_ref[...] = jnp.zeros_like(sums_ref)
    tok_load.wait()
    for item in w3_load:
        item.wait()

    def first_norm(values):
        unit, inv = standardize(values.astype(f32))
        return unit, inv, (unit * vector(gain1_ref) + vector(shift1_ref)).astype(bf16)

    def project_rows(i):
        _, _, normed = first_norm(buf_d[rows_of(i), 0:dim])
        out = nn(normed, wi[:, 0 : 3 * third])
        query = (out[:, 0:third] + qvb_ref[0:1, :]).astype(bf16)
        buf_h[rows_of(i), 0:third] = (query.astype(f32) * HEAD_DIM ** (-0.5)).astype(bf16)
        buf_h[rows_of(i), third : 2 * third] = out[:, third : 2 * third].astype(bf16)
        buf_h[rows_of(i), 2 * third : 3 * third] = (out[:, 2 * third :] + qvb_ref[1:2, :]).astype(bf16)

    def body(i):
        project_rows(2 * i)
        project_rows(2 * i + 1)

    loop(tiles // 2, body, False)
    wi_load = load(wi_h, wi, 6)
    g_load = load(g_h, buf_g, 5)
    wb_load = load(wb_h, wb, 7)
    save_qkv = load(buf_h.at[:, pl.ds(0, 3 * third)], heads_h.at[:, pl.ds(0, 3 * third)], 8)


    wo_load.wait()
    log_ref[...] = jnp.zeros_like(log_ref)
    lane = lax.broadcasted_iota(jnp.int32, (1, PAIR), 1) // 8

    def body(half):
        start = pl.multiple_of(half * HALF, TILE)
        window = pl.ds(pl.multiple_of(half * LOW, 64), WINDOW)
        mask_ref[...] = jnp.where(col_ref[pl.ds(start, HALF), 0:1] == key_ids[half], 0.0, -1000000000.0)

        def pair(p):
            pick = lambda block: pl.ds(pl.multiple_of(block * third + p * PAIR, PAIR), PAIR)

            def rows(at, count):
                return buf_h[pl.ds(pl.multiple_of(start + at, 32), count), pick(0)]

            def put(at, count, mixed, *logs):
                buf_n[pl.ds(pl.multiple_of(start + at, 32), count), pick(0)] = mixed
                old = log_ref[at : at + count, :]
                for head in range(2):
                    old = jnp.where(lane == 2 * p + head, logs[head], old)
                log_ref[at : at + count, :] = old

            attend_pair(start, rows, buf_h[window, pick(1)], buf_h[window, pick(2)], mask_ref, put)

        loop(third // PAIR, pair, False)

        turned = jnp.transpose(log_ref[...])
        for head in range(third // HEAD_DIM):
            lse_ref[half, head, 0:1, 0:HALF] = turned[head * 8 : head * 8 + 1, :]

        @pl.when(half == 0)
        def _():
            pl.semaphore_wait(barrier, STEPS + 1)

        def project(j):
            i = half * (tiles // 2) + j
            own[rows_of(i), :] = nn(buf_n[rows_of(i), 0:third], wo[...])
            swap(0, i, rows_of(i)).start()

        loop(tiles // 2, project, False)

    loop(2, body, False)
    save_o = load(buf_n.at[:, pl.ds(0, third)], heads_h.at[:, pl.ds(3 * third, third)], 9)


    wi_load.wait()
    save_qkv.wait()
    save_o.wait()
    root = 0.7978845608028654

    def hidden(i, c):
        u = nn(buf_n[rows_of(i), :], wi[:, columns(c * LANES)]) + bias_ref[c]
        t = jnp.tanh(u * (root + (root * 0.044715) * (u * u)))
        buf_h[rows_of(i), columns(c * LANES)] = (u * (0.5 + 0.5 * t)).astype(bf16)
        buf_d[rows_of(i), columns(c * LANES)] = u.astype(bf16)

    def body(i):
        total = swapped(0, i)
        middle = buf_d[rows_of(i), 0:dim].astype(f32) + total + vector(ob_ref)
        buf_m[rows_of(i), :] = middle
        unit, _ = standardize(middle)
        buf_n[rows_of(i), :] = (unit * vector(gain2_ref) + vector(shift2_ref)).astype(bf16)
        hidden(i, 0)

    loop(tiles, body, False)
    peer_is_free()
    save_mid = load(buf_m, mid_h, 10)
    g_load.wait()
    gradient(0, buf_g, buf_h[:, 0:LANES])
    arrivals()

    def body(j):
        c = j + 1
        loop(tiles, lambda i: hidden(i, c), False)
        gradient(c, buf_g, buf_h[:, columns(c * LANES)])

    loop(blocks - 1, body)
    save_hid = load(buf_h, hid_h, 11)


    wb_load.wait()
    pl.semaphore_wait(free_sem, 1)

    def body(i):
        grad = buf_g[rows_of(i), :]
        for at in range(0, width, 512):
            u = buf_d[rows_of(i), at : at + 512].astype(f32)
            square = u * u
            t = jnp.tanh(u * (root + (root * 0.044715) * square))
            slope = 0.5 + 0.5 * t + (0.5 * u) * (1.0 - t * t) * (root + (3.0 * 0.044715 * root) * square)
            du = (nt(grad, wb[at : at + 512, :]) * slope).astype(bf16)
            buf_d[rows_of(i), at : at + 512] = du
            sums_ref[4:5, at : at + 512] += jnp.sum(du.astype(f32), 0, keepdims=True)
        own[rows_of(i), :] = nt(buf_d[rows_of(i), :], wi[...])
        swap(1, i, rows_of(i)).start()
        sums_ref[2:3, dim : 2 * dim] += jnp.sum(grad.astype(f32), 0, keepdims=True)

    loop(tiles, body)
    w3_late = load_w3(1)
    save_hid.wait()
    heads_load = load(heads_h, buf_h, 8)


    loop(4, lambda i: gradient(4 + i, buf_n, buf_d[:, columns(i * LANES)]))


    save_mid.wait()

    def body(i):
        grad = swapped(1, i)
        unit, inv = standardize(buf_m[rows_of(i), :])
        dh = buf_g[rows_of(i), :].astype(f32) + norm_back(unit, inv, vector(gain2_ref), grad)
        buf_m[rows_of(i), :] = dh
        dr = dh.astype(bf16)
        buf_n[rows_of(i), :] = dr
        buf_d[rows_of(i), 0:third] = nt(dr, wo[...]).astype(bf16)
        sums_ref[1:2, dim : 2 * dim] += jnp.sum(grad * unit, 0, keepdims=True)
        sums_ref[2:3, 0:dim] += jnp.sum(grad, 0, keepdims=True)
        sums_ref[1:2, 0:dim] += jnp.sum(dr.astype(f32), 0, keepdims=True)

    loop(tiles, body)
    peer_is_free()
    tok_late = load(tok_h, buf_g, 0)
    heads_load.wait()
    gradient(8, buf_n, buf_h[:, 3 * third : 4 * third])
    arrivals()


    first = lax.broadcasted_iota(jnp.int32, (1, PAIR), 1) < HEAD_DIM
    zero = jnp.zeros((), bf16)

    def body(at):
        p, half = at // 2, lax.rem(at, 2)
        pick = lambda block: pl.ds(pl.multiple_of(block * third + p * PAIR, PAIR), PAIR)
        window = pl.ds(pl.multiple_of(half * LOW, 64), WINDOW)
        keys, values = buf_h[window, pick(1)], buf_h[window, pick(2)]

        @pl.when(half == 0)
        def _():
            acc_k[...] = jnp.zeros_like(acc_k)
            acc_v[...] = jnp.zeros_like(acc_v)

        for begin, count in ((0, 256), (256, 352)):
            span = pl.ds(pl.multiple_of(half * HALF + begin, 32), count)
            rows, grads = buf_h[span, pick(0)], buf_d[span, pick(0)]
            same = col_ref[window, 0:1] == query_ids[half, :, begin : begin + count]
            mask = jnp.where(same, 0.0, -1000000000.0)
            parts = []
            for head in range(2):
                own_part = lambda a: jnp.where(first, a, zero) if head == 0 else jnp.where(first, zero, a)
                lse = lse_ref[half, 2 * p + head, 0:1, begin : begin + count]
                probs = jnp.exp(nt(keys, own_part(rows)) + mask - lse)
                back = nt(values, own_part(grads))
                inner = jnp.sum(probs * back, 0, keepdims=True)
                slant = (probs * (back - inner)).astype(bf16)
                parts.append((tn(slant, keys), nn(slant, rows), nn(probs.astype(bf16), grads)))
            dq, dk, dv = (jnp.where(first, a, b) for a, b in zip(*parts))
            dq = (dq * HEAD_DIM ** (-0.5)).astype(bf16)
            buf_d[span, pick(1)] = dq
            sums_ref[3:4, pick(0)] += jnp.sum(dq.astype(f32), 0, keepdims=True)
            acc_k[window, :] += dk
            acc_v[window, :] += dv

        @pl.when(half == 1)
        def _():
            buf_d[:, pick(2)] = acc_k[...].astype(bf16)
            dv = acc_v[...].astype(bf16)
            buf_d[:, pick(3)] = dv
            sums_ref[3:4, pick(1)] = jnp.sum(dv.astype(f32), 0, keepdims=True)

    loop(2 * (third // PAIR), body)
    hid_load = load(hid_h, buf_h, 8)


    tok_late.wait()

    def body(i):
        _, _, normed = first_norm(buf_g[rows_of(i), :])
        buf_n[rows_of(i), :] = normed

    loop(tiles, body, False)
    arrivals()
    loop(3, lambda i: gradient(9 + i, buf_n, buf_d[:, columns(third + i * LANES)]))


    for item in w3_late:
        item.wait()
    pl.semaphore_wait(free_sem, 1)

    def body(i):
        own[rows_of(i), :] = nt(buf_d[rows_of(i), third : 4 * third], wi[:, 0 : 3 * third])
        swap(2, i, rows_of(i)).start()

    loop(tiles, body)

    def body(i):
        grad = swapped(2, i)
        unit, inv, _ = first_norm(buf_g[rows_of(i), :])
        buf_g[rows_of(i), :] = (buf_m[rows_of(i), :] + norm_back(unit, inv, vector(gain1_ref), grad)).astype(bf16)
        sums_ref[0:1, 0:dim] += jnp.sum(grad * unit, 0, keepdims=True)
        sums_ref[0:1, dim : 2 * dim] += jnp.sum(grad, 0, keepdims=True)

    loop(tiles, body)
    peer_is_free()
    input_put = pltpu.make_async_copy(buf_g, input_h, put_sem.at[1])
    input_put.start()
    mid_load = load(mid_h, buf_m, 10)

    def whole_hop(step):
        return pltpu.make_async_remote_copy(
            src_ref=sums_ref,
            dst_ref=sums_in.at[step],
            send_sem=sums_send.at[step],
            recv_sem=sums_recv.at[step],
            device_id=(route.plain[step], core),
            device_id_type=mesh_id,
        )

    def add_sums(step):
        whole_hop(step).wait()
        sums_ref[...] += sums_in[step]

    whole_hop(0).start()


    hid_load.wait()
    pl.semaphore_wait(free_sem, 1)

    def body(i):
        own[rows_of(i), :] = nn(buf_h[rows_of(i), :], wb[...])
        swap(3, i, rows_of(i)).start()

    loop(tiles, body)
    add_sums(0)
    whole_hop(1).start()
    mid_load.wait()

    def body(i):
        buf_n[rows_of(i), :] = (buf_m[rows_of(i), :] + swapped(3, i) + vector(bb_ref)).astype(bf16)

    loop(tiles, body)
    layer_put = pltpu.make_async_copy(buf_n, layer_h, put_sem.at[0])
    layer_put.start()
    rest = left.pop(0)
    gap = len(rest) // STEPS
    for step in range(1, STEPS):
        for item in rest[(step - 1) * gap : step * gap]:
            finish(*item)
        add_sums(step)
        if step + 1 < STEPS:
            whole_hop(step + 1).start()
    for item in rest[(STEPS - 1) * gap :]:
        finish(*item)
    for chunk in range(COUNT):
        deliver(chunk).wait()
    input_put.wait()
    layer_put.wait()


def whole_layer(tokens, g, w3, wo, wi, wb, ids, gain1, shift1, qvb, ob, gain2, shift2, ib, bb):
    tok, dim = g.shape
    width = wi.shape[1]
    third = wo.shape[0]
    rows = dim // 16
    hbm = pl.BlockSpec(memory_space=pl.ANY)
    vmem = pl.BlockSpec(memory_space=pltpu.VMEM)
    dma = pltpu.SemaphoreType.DMA
    return pl.pallas_call(
        layer_kernel,
        in_specs=[hbm] * 6 + [vmem] * 9,
        out_specs=[hbm, hbm, hbm, vmem, hbm, hbm, hbm],
        out_shape=[
            jax.ShapeDtypeStruct((tok, dim), bf16),
            jax.ShapeDtypeStruct((tok, dim), bf16),
            jax.ShapeDtypeStruct((COUNT, rows, LANES), f32),
            jax.ShapeDtypeStruct((8, width), f32),
            jax.ShapeDtypeStruct((tok, width), bf16),
            jax.ShapeDtypeStruct((tok, width), bf16),
            jax.ShapeDtypeStruct((tok, dim), f32),
        ],
        scratch_shapes=[
            pltpu.VMEM((tok, width), bf16),
            pltpu.VMEM((tok, width), bf16),
            pltpu.VMEM((tok, dim), bf16),
            pltpu.VMEM((tok, dim), bf16),
            pltpu.VMEM((tok, dim), f32),
            pltpu.VMEM((tok, dim), f32),
            pltpu.VMEM((tok, dim), f32),
            pltpu.VMEM((dim, width), bf16),
            pltpu.VMEM((width, dim), bf16),
            pltpu.VMEM((third, dim), bf16),
            pltpu.VMEM((tok, PAIR), f32),
            pltpu.VMEM((tok, PAIR), f32),
            pltpu.VMEM((tok, PAIR), jnp.int32),
            pltpu.VMEM((2, 1, 640), jnp.int32),
            pltpu.VMEM((2, 1, WINDOW), jnp.int32),
            pltpu.VMEM((HALF, WINDOW), f32),
            pltpu.VMEM((width // LANES, 1, LANES), f32),
            pltpu.VMEM((2, third // HEAD_DIM, 8, 640), f32),
            pltpu.VMEM((HALF, PAIR), f32),
            pltpu.VMEM((COUNT, 16, rows, LANES), f32),
            pltpu.VMEM((COUNT, 8, rows, LANES), f32),
            pltpu.VMEM((COUNT, 4, rows, LANES), f32),
            pltpu.VMEM((COUNT, 2, rows, LANES), f32),
            pltpu.VMEM((COUNT, 1, rows, LANES), f32),
            pltpu.VMEM((STEPS, 8, width), f32),
            dma((12,)),
            dma((STEPS, COUNT)),
            dma((STEPS, COUNT)),
            dma((COUNT,)),
            dma((4, tok // TILE)),
            dma((4, tok // TILE)),
            dma((STEPS,)),
            dma((STEPS,)),
            dma((2,)),
            pltpu.SemaphoreType.REGULAR,
        ],
        compiler_params=pltpu.CompilerParams(vmem_limit_bytes=VMEM_LIMIT, collective_id=0, has_side_effects=True),
        cost_estimate=cost(34e9, 40e6),
        name="whole_layer",
    )(tokens, g, w3, wo, wi, wb, ids, gain1, shift1, qvb, ob, gain2, shift2, ib, bb)


def outputs_kernel(layer_h, input_h, grads_h, sums_ref, layer_o, input_o, *refs):
    n1g, n1s, qkv, qvb, out, obg, n2g, n2s, inw, ibg, back, bbg, held, kept, in_sem, out_sem = refs
    me = lax.axis_index("batch")
    dim = sums_ref.shape[1] // 2
    third = dim // 2
    pieces = 4
    rows = held.shape[1] // pieces
    grads_in = pltpu.make_async_copy(grads_h, kept, in_sem.at[2 * pieces])
    grads_in.start()
    moves = []
    for i, (source, target) in enumerate(((layer_h, layer_o), (input_h, input_o))):
        for j in range(pieces):
            span = pl.ds(j * rows, rows)
            at = i * pieces + j
            coming = pltpu.make_async_copy(source.at[span], held.at[i, span], in_sem.at[at])
            coming.start()
            moves.append((coming, pltpu.make_async_copy(held.at[i, span], target.at[span], out_sem.at[at])))

    def mine(row, at, size):
        n = size // 16
        values = jnp.broadcast_to(sums_ref[row : row + 1, at : at + size], (8, size))
        return pltpu.roll(values, size - me * n, 1)[0:1, 0:n]

    for ref, row, at in ((n1g, 0, 0), (n1s, 0, dim), (obg, 1, 0), (n2g, 1, dim), (n2s, 2, 0), (bbg, 2, dim)):
        ref[...] = mine(row, at, dim).reshape(-1)
    ibg[...] = mine(4, 0, 2 * dim).reshape(-1)
    qvb[0:1, :] = mine(3, 0, third)
    qvb[1:2, :] = mine(3, third, third)
    grads_in.wait()
    places = [back.at[:, pl.ds(c * LANES, LANES)] for c in range(4)]
    places += [inw.at[:, pl.ds(c * LANES, LANES)] for c in range(4)]
    places += [out] + [qkv.at[c] for c in range(3)]
    going = [pltpu.make_async_copy(kept.at[c], place, out_sem.at[2 * pieces + c]) for c, place in enumerate(places)]
    for item in going:
        item.start()
    for coming, leaving in moves:
        coming.wait()
        leaving.start()
    for item in going:
        item.wait()
    for _, leaving in moves:
        leaving.wait()


def outputs(layer, grad, grads, sums):
    rows, width = grads.shape[1], sums.shape[1]
    hbm = pl.BlockSpec(memory_space=pl.ANY)
    vmem = pl.BlockSpec(memory_space=pltpu.VMEM)
    small = jax.ShapeDtypeStruct((rows,), f32)
    shape = lambda *s: jax.ShapeDtypeStruct(s, f32)
    return pl.pallas_call(
        outputs_kernel,
        in_specs=[hbm, hbm, hbm, vmem],
        out_specs=[hbm, hbm, vmem, vmem, hbm, vmem, hbm, vmem, vmem, vmem, hbm, vmem, hbm, vmem],
        out_shape=[
            jax.ShapeDtypeStruct(layer.shape, bf16),
            jax.ShapeDtypeStruct(grad.shape, bf16),
            small,
            small,
            shape(3, rows, LANES),
            shape(2, rows // 2),
            shape(rows, LANES),
            small,
            small,
            small,
            shape(rows, width),
            shape(2 * rows),
            shape(rows, width),
            small,
        ],
        scratch_shapes=[
            pltpu.VMEM((2,) + layer.shape, bf16),
            pltpu.VMEM(grads.shape, f32),
            pltpu.SemaphoreType.DMA((9,)),
            pltpu.SemaphoreType.DMA((8 + COUNT,)),
        ],
        compiler_params=params(60),
        name="outputs",
    )(layer, grad, grads, sums)


def shards(
    tokens,
    seq_ids,
    cotangent,
    norm1_gain,
    norm1_shift,
    w_qkv,
    qv_bias,
    w_out,
    out_bias,
    norm2_gain,
    norm2_shift,
    w_in,
    in_bias,
    w_back,
    back_bias,
    batch,
):
    tok, dim = tokens.shape
    w3 = jnp.transpose(w_qkv, (1, 0, 2))
    if batch == 16:
        layer, grad, grads, sums, *_ = whole_layer(
            tokens, cotangent, w3, w_out, w_in, w_back, seq_ids,
            norm1_gain, norm1_shift, qv_bias, out_bias, norm2_gain, norm2_shift, in_bias, back_bias,
        )
        results = list(outputs(layer, grad, grads, sums))
        results[4] = jnp.transpose(results[4], (1, 0, 2))
        results[6], results[12] = results[6].T, results[12].T
        return tuple(results)

    row = lambda a: a.reshape(1, -1)
    ids_col, ids_row = seq_ids.reshape(tok, 1), seq_ids.reshape(1, tok)
    exchange = Exchange(batch)
    parts = exchange.first_parts()

    normed, q, k, v = project(tokens, row(norm1_gain), row(norm1_shift), w3, qv_bias)
    mixed, lse_a, part_a = attend(0, q, k, v, ids_col, ids_row, w_out)
    peer_a = other_core(part_a)
    mixed, lse_b, part_b = attend(1, q, k, v, ids_col, ids_row, w_out, (mixed,))
    peer_b = other_core(part_b)
    mlp = (row(out_bias), row(norm2_gain), row(norm2_shift), w_in, row(in_bias))
    state = hidden_layer(0, tokens, part_a, peer_a, *mlp)
    state = hidden_layer(1, tokens, part_b, peer_b, *mlp, before=tuple(state))
    middle, normed_two, hidden, slope = state

    back_parts = weight_grad(parts, exchange.place, cotangent, hidden)
    du, dn2, in_bias_sum, back_bias_sum = hidden_back(cotangent, slope, w_back, w_in)
    dn2_peer = other_core(dn2)
    in_parts = weight_grad(parts, exchange.place, normed_two, du)
    mlp_own = rows_matmul(hidden, w_back)
    mlp_peer = other_core(mlp_own)
    dh, dr, do, middle_sums = middle_back(middle, dn2, dn2_peer, cotangent, row(norm2_gain), w_out)
    out_parts = weight_grad(parts, exchange.place, dr, mixed)
    layer_out = (middle + (mlp_own + mlp_peer) + back_bias).astype(bf16)
    dq, dk, dv, qv_sums = attend_back(q, k, v, do, lse_a, lse_b, ids_col, ids_row)
    q_parts = weight_grad(parts, exchange.place, normed, dq)
    k_parts = weight_grad(parts, exchange.place, normed, dk)
    v_parts = weight_grad(parts, exchange.place, normed, dv)
    dn1 = normed_back(dq, dk, dv, w3)
    dn1_peer = other_core(dn1)
    tokens_grad, input_sums = input_back(tokens, dn1, dn1_peer, dh, row(norm1_gain))

    w_back_grad = jnp.transpose(exchange.reduce(back_parts))
    w_in_grad = exchange.reduce(in_parts)
    w_out_grad = jnp.transpose(exchange.reduce(out_parts))
    w_qkv_grad = jnp.stack([exchange.reduce(p) for p in (q_parts, k_parts, v_parts)], 1)

    pieces = [input_sums[0], input_sums[1], middle_sums[2], middle_sums[0], middle_sums[1], back_bias_sum[0]]
    pieces += [qv_sums[0], qv_sums[1], in_bias_sum[0]]
    packed = jnp.concatenate([p.reshape(batch, -1) for p in pieces], 1)
    vectors = lax.psum_scatter(packed, "batch", scatter_dimension=0, tiled=True)[0]
    out, at = [], 0
    for p in pieces:
        n = p.shape[0] // batch
        out.append(vectors[at : at + n])
        at += n
    n1g, n1s, obg, n2g, n2s, bbg, qb, vb, ibg = out
    return (
        layer_out,
        tokens_grad,
        n1g,
        n1s,
        w_qkv_grad,
        jnp.stack([qb, vb]),
        w_out_grad,
        obg,
        n2g,
        n2s,
        w_in_grad,
        ibg,
        w_back_grad,
        bbg,
    )


def solution(mesh):
    in_specs = (
        P("batch", None),
        P("batch"),
        P("batch", None),
        P(),
        P(),
        P(None, None, "tp"),
        P(None, "tp"),
        P("tp", None),
        P(),
        P(),
        P(),
        P(None, "tp"),
        P("tp"),
        P("tp", None),
        P(),
    )
    out_specs = (
        P("batch", None),
        P("batch", None),
        P("batch"),
        P("batch"),
        P("batch", None, "tp"),
        P(None, ("tp", "batch")),
        P("tp", "batch"),
        P("batch"),
        P("batch"),
        P("batch"),
        P("batch", "tp"),
        P(("tp", "batch")),
        P("tp", "batch"),
        P("batch"),
    )
    body = functools.partial(shards, batch=mesh.shape["batch"])
    return jax.shard_map(body, mesh=mesh, in_specs=in_specs, out_specs=out_specs, check_vma=False)
```

```python
import functools

import jax
import jax.numpy as jnp
from jax import lax
from jax.experimental import pallas as pl
from jax.experimental.pallas import tpu as pltpu
from jax.sharding import PartitionSpec as P

HEAD_DIM = 64
PAIR = 2 * HEAD_DIM
HALF = 608
TILE = 304
LANES = 384
VMEM_LIMIT = 63 << 20
WINDOW = 768
LOW = 448
ROWS = ((0, 128), (128, 128), (256, 128), (384, 128), (512, 96))
TILES = ((0, 256, 0, 608), (256, 352, 0, 688), (608, 256, 448, 1216), (864, 352, 608, 1216))
f32 = jnp.float32
bf16 = jnp.bfloat16


def params(mib):
    return pltpu.CompilerParams(vmem_limit_bytes=mib << 20)


def cost(flops, nbytes, trans=0):
    return pl.CostEstimate(flops=int(flops), bytes_accessed=int(nbytes), transcendentals=int(trans))


def nn(a, b):
    return jnp.dot(a, b, preferred_element_type=f32)


def nt(a, b):
    return lax.dot_general(a, b, (((1,), (1,)), ((), ())), preferred_element_type=f32)


def tn(a, b):
    return lax.dot_general(a, b, (((0,), (0,)), ((), ())), preferred_element_type=f32)


def standardize(values):
    center = values - jnp.mean(values, -1, keepdims=True)
    spread = jnp.mean(center * center, -1, keepdims=True)
    inv = lax.rsqrt(spread + 1e-06)
    return center * inv, inv


def norm_back(unit, inv, gain, grad):
    scaled = grad * gain
    return inv * (
        scaled
        - jnp.mean(scaled, -1, keepdims=True)
        - unit * jnp.mean(scaled * unit, -1, keepdims=True)
    )


def whole(shape):
    return pl.BlockSpec(shape, lambda *_: (0,) * len(shape))


def project_kernel(x_ref, gain_ref, shift_ref, w_ref, bias_ref, n_ref, q_ref, k_ref, v_ref):
    unit, _ = standardize(x_ref[...].astype(f32))
    normed = (unit * gain_ref[...] + shift_ref[...]).astype(bf16)
    n_ref[...] = normed
    scale = HEAD_DIM ** (-0.5)
    q_ref[...] = ((nn(normed, w_ref[0]) + bias_ref[0:1]).astype(bf16).astype(f32) * scale).astype(bf16)
    k_ref[...] = nn(normed, w_ref[1]).astype(bf16)
    v_ref[...] = (nn(normed, w_ref[2]) + bias_ref[1:2]).astype(bf16)


def project(tokens, gain, shift, w3, qv_bias):
    tok, dim = tokens.shape
    width = w3.shape[2]
    rows = lambda n: pl.BlockSpec((TILE, n), lambda i: (i, 0))
    out = jax.ShapeDtypeStruct((tok, width), bf16)
    return pl.pallas_call(
        project_kernel,
        grid=(tok // TILE,),
        in_specs=[rows(dim), whole((1, dim)), whole((1, dim)), whole(w3.shape), whole((2, width))],
        out_specs=[rows(dim), rows(width), rows(width), rows(width)],
        out_shape=[jax.ShapeDtypeStruct((tok, dim), bf16), out, out, out],
        compiler_params=params(60),
        cost_estimate=cost(2 * tok * dim * 3 * width, tok * (2 * dim + 3 * width) * 2 + w3.size * 2),
        name="project",
    )(tokens, gain, shift, w3, qv_bias)


def attend_kernel(half, q_ref, k_ref, v_ref, col_ref, row_ref, w_ref, *refs):
    o_ref, lse_ref, part_ref, *mask_refs = refs[-5:]
    step = pl.program_id(0)
    tiles = TILES[2 * half : 2 * half + 2]

    @pl.when(step == 0)
    def _():
        for (start, count, low, high), mask_ref in zip(tiles, mask_refs):
            at = start - half * HALF
            same = col_ref[at : at + count, :] == row_ref[:, low:high]
            mask_ref[...] = jnp.where(same, 0.0, -1000000000.0)

    first = lax.broadcasted_iota(jnp.int32, (1, PAIR), 1) < HEAD_DIM
    zero = jnp.zeros((), bf16)
    one = jnp.ones((), bf16)
    for tile, ((start, count, low, high), mask_ref) in enumerate(zip(tiles, mask_refs)):
        at = start - half * HALF
        rows = q_ref[at : at + count, :]
        keys = k_ref[low:high, :]
        values = v_ref[low:high, :]
        with_ones = (jnp.where(first, values, one), jnp.where(first, one, values))
        mask = mask_ref[...]
        outs, logs = [], []
        for head in range(2):
            own = jnp.where(first, rows, zero) if head == 0 else jnp.where(first, zero, rows)
            scores = nt(own, keys) + mask
            top = jnp.max(scores, -1, keepdims=True)
            expo = jnp.exp(scores - top).astype(bf16)
            mixed = nn(expo, with_ones[head])
            total = pltpu.roll(mixed, HEAD_DIM, 1)
            outs.append(mixed / total)
            logs.append(top + jnp.log(total))
        mixed = jnp.where(first, outs[0], outs[1]).astype(bf16)
        o_ref[at : at + count, :] = mixed
        turned = jnp.transpose(jnp.where(first, logs[0], logs[1]))
        lse_ref[tile, pl.ds(2 * step, 1), 0:count] = turned[0:1, :]
        lse_ref[tile, pl.ds(2 * step + 1, 1), 0:count] = turned[HEAD_DIM : HEAD_DIM + 1, :]
        part = nn(mixed, w_ref[...])

        @pl.when(step == 0)
        def _():
            part_ref[at : at + count, :] = part

        @pl.when(step > 0)
        def _():
            part_ref[at : at + count, :] += part


def attend(half, q, k, v, ids_col, ids_row, w_out, before=()):
    tok, width = q.shape
    dim = w_out.shape[1]
    pair_rows = pl.BlockSpec((HALF, PAIR), lambda p: (half, p))
    pair_all = pl.BlockSpec((tok, PAIR), lambda p: (0, p))
    tiles = TILES[2 * half : 2 * half + 2]
    return pl.pallas_call(
        functools.partial(attend_kernel, half),
        grid=(width // PAIR,),
        in_specs=[
            pair_rows,
            pair_all,
            pair_all,
            pl.BlockSpec((HALF, 1), lambda p: (half, 0)),
            whole((1, tok)),
            pl.BlockSpec((PAIR, dim), lambda p: (p, 0)),
        ]
        + [pl.BlockSpec(memory_space=pl.ANY)] * len(before),
        out_specs=[pair_rows, whole((2, 8, LANES)), whole((HALF, dim))],
        out_shape=[
            jax.ShapeDtypeStruct((tok, width), bf16),
            jax.ShapeDtypeStruct((2, 8, LANES), f32),
            jax.ShapeDtypeStruct((HALF, dim), f32),
        ],
        scratch_shapes=[pltpu.VMEM((count, high - low), f32) for _, count, low, high in tiles],
        input_output_aliases={6 + i: i for i in range(len(before))},
        compiler_params=params(60),
        cost_estimate=cost(16 * HALF * 650 * width, tok * width * 6 + HALF * dim * 4),
        name="attend",
    )(q, k, v, ids_col, ids_row, w_out, *before)


def hidden_kernel(x_ref, own_ref, peer_ref, ob_ref, gain_ref, shift_ref, w_ref, ib_ref, *refs):
    mid_ref, n_ref, hid_ref, slope_ref = refs[-4:]
    middle = x_ref[...].astype(f32) + (own_ref[...] + peer_ref[...]) + ob_ref[...]
    mid_ref[...] = middle
    unit, _ = standardize(middle)
    normed = (unit * gain_ref[...] + shift_ref[...]).astype(bf16)
    n_ref[...] = normed
    width = w_ref.shape[1]
    piece = 512
    c0 = 0.7978845608028654
    for at in range(0, width, piece):
        u = nn(normed, w_ref[:, at : at + piece]) + ib_ref[:, at : at + piece]
        sq = u * u
        t = jnp.tanh(u * (c0 + (c0 * 0.044715) * sq))
        cdf = 0.5 + 0.5 * t
        hid_ref[:, at : at + piece] = (u * cdf).astype(bf16)
        slope = cdf + (0.5 * u) * (1.0 - t * t) * (c0 + (3.0 * 0.044715 * c0) * sq)
        slope_ref[:, at : at + piece] = slope.astype(bf16)


def hidden_layer(half, tokens, own, peer, out_bias, gain, shift, w_in, in_bias, before=()):
    tok, dim = tokens.shape
    width = w_in.shape[1]
    per = HALF // TILE
    glob = lambda n: pl.BlockSpec((TILE, n), lambda i: (i + per * half, 0))
    loc = lambda n: pl.BlockSpec((TILE, n), lambda i: (i, 0))
    return pl.pallas_call(
        hidden_kernel,
        grid=(per,),
        in_specs=[
            glob(dim),
            loc(dim),
            loc(dim),
            whole((1, dim)),
            whole((1, dim)),
            whole((1, dim)),
            whole(w_in.shape),
            whole((1, width)),
        ]
        + [pl.BlockSpec(memory_space=pl.ANY)] * len(before),
        out_specs=[glob(dim), glob(dim), glob(width), glob(width)],
        out_shape=[
            jax.ShapeDtypeStruct((tok, dim), f32),
            jax.ShapeDtypeStruct((tok, dim), bf16),
            jax.ShapeDtypeStruct((tok, width), bf16),
            jax.ShapeDtypeStruct((tok, width), bf16),
        ],
        input_output_aliases={8 + i: i for i in range(len(before))},
        compiler_params=params(60),
        cost_estimate=cost(2 * HALF * dim * width, HALF * (dim * 16 + width * 4) + w_in.size * 2, HALF * width),
        name="hidden_layer",
    )(tokens, own, peer, out_bias, gain, shift, w_in, in_bias, *before)


def matmul_kernel(a_ref, b_ref, o_ref):
    o_ref[...] = nn(a_ref[...], b_ref[...])


def rows_matmul(a, b):
    tok, depth = a.shape
    width = b.shape[1]
    return pl.pallas_call(
        matmul_kernel,
        grid=(tok // TILE,),
        in_specs=[pl.BlockSpec((TILE, depth), lambda i: (i, 0)), whole(b.shape)],
        out_specs=pl.BlockSpec((TILE, width), lambda i: (i, 0)),
        out_shape=jax.ShapeDtypeStruct((tok, width), f32),
        compiler_params=params(60),
        cost_estimate=cost(2 * tok * depth * width, tok * (depth * 2 + width * 4) + b.size * 2),
        name="mlp_out",
    )(a, b)


def hidden_back_kernel(g_ref, slope_ref, wb_ref, wi_ref, du_ref, dn_ref, db_ref, gb_ref):
    step = pl.program_id(0)
    grad = g_ref[...]
    width = slope_ref.shape[1]
    piece = 512
    total = None
    sums = []
    for at in range(0, width, piece):
        back = nt(grad, wb_ref[at : at + piece, :])
        du = (back * slope_ref[:, at : at + piece].astype(f32)).astype(bf16)
        du_ref[:, at : at + piece] = du
        sums.append(jnp.sum(du.astype(f32), 0, keepdims=True))
    dn_ref[...] = nt(du_ref[...], wi_ref[...])

    @pl.when(step == 0)
    def _():
        db_ref[...] = jnp.zeros_like(db_ref)
        gb_ref[...] = jnp.zeros_like(gb_ref)

    for i, at in enumerate(range(0, width, piece)):
        db_ref[:, at : at + piece] += sums[i]
    gb_ref[...] += jnp.sum(grad.astype(f32), 0, keepdims=True)


def hidden_back(cotangent, slope, w_back, w_in):
    tok, dim = cotangent.shape
    width = slope.shape[1]
    rows = lambda n: pl.BlockSpec((TILE, n), lambda i: (i, 0))
    return pl.pallas_call(
        hidden_back_kernel,
        grid=(tok // TILE,),
        in_specs=[rows(dim), rows(width), whole(w_back.shape), whole(w_in.shape)],
        out_specs=[rows(width), rows(dim), whole((1, width)), whole((1, dim))],
        out_shape=[
            jax.ShapeDtypeStruct((tok, width), bf16),
            jax.ShapeDtypeStruct((tok, dim), f32),
            jax.ShapeDtypeStruct((1, width), f32),
            jax.ShapeDtypeStruct((1, dim), f32),
        ],
        compiler_params=params(60),
        cost_estimate=cost(4 * tok * dim * width, tok * (dim * 6 + width * 4) + w_in.size * 4),
        name="hidden_back",
    )(cotangent, slope, w_back, w_in)


def middle_back_kernel(mid_ref, own_ref, peer_ref, g_ref, gain_ref, w_ref, dh_ref, dr_ref, do_ref, sum_ref):
    step = pl.program_id(0)
    unit, inv = standardize(mid_ref[...])
    grad = own_ref[...] + peer_ref[...]
    dh = g_ref[...].astype(f32) + norm_back(unit, inv, gain_ref[...], grad)
    dh_ref[...] = dh
    dr = dh.astype(bf16)
    dr_ref[...] = dr
    do_ref[...] = nt(dr, w_ref[...]).astype(bf16)

    @pl.when(step == 0)
    def _():
        sum_ref[...] = jnp.zeros_like(sum_ref)

    sum_ref[0:1] += jnp.sum(grad * unit, 0, keepdims=True)
    sum_ref[1:2] += jnp.sum(grad, 0, keepdims=True)
    sum_ref[2:3] += jnp.sum(dr.astype(f32), 0, keepdims=True)


def middle_back(middle, own, peer, cotangent, gain, w_out):
    tok, dim = middle.shape
    width = w_out.shape[0]
    rows = lambda n: pl.BlockSpec((TILE, n), lambda i: (i, 0))
    return pl.pallas_call(
        middle_back_kernel,
        grid=(tok // TILE,),
        in_specs=[rows(dim), rows(dim), rows(dim), rows(dim), whole((1, dim)), whole(w_out.shape)],
        out_specs=[rows(dim), rows(dim), rows(width), whole((8, dim))],
        out_shape=[
            jax.ShapeDtypeStruct((tok, dim), f32),
            jax.ShapeDtypeStruct((tok, dim), bf16),
            jax.ShapeDtypeStruct((tok, width), bf16),
            jax.ShapeDtypeStruct((8, dim), f32),
        ],
        compiler_params=params(60),
        cost_estimate=cost(2 * tok * dim * width, tok * (dim * 20 + width * 2) + w_out.size * 2),
        name="middle_back",
    )(middle, own, peer, cotangent, gain, w_out)


def attend_back_tile(tile, keys, values, rows, grads, mask, lse_rows):
    first = lax.broadcasted_iota(jnp.int32, (1, PAIR), 1) < HEAD_DIM
    zero = jnp.zeros((), bf16)
    parts = []
    for head in range(2):
        pick = lambda a: jnp.where(first, a, zero) if head == 0 else jnp.where(first, zero, a)
        probs = jnp.exp(nt(keys, pick(rows)) + mask - lse_rows[head])
        back = nt(values, pick(grads))
        inner = jnp.sum(probs * back, 0, keepdims=True)
        slant = (probs * (back - inner)).astype(bf16)
        dv = nn(probs.astype(bf16), grads)
        dk = nn(slant, rows)
        dq = tn(slant, keys)
        parts.append((dq, dk, dv))
    dq, dk, dv = (jnp.where(first, a, b) for a, b in zip(*parts))
    return (dq * HEAD_DIM ** (-0.5)).astype(bf16), dk, dv


def attend_back_pair(q, k, v, do, lse, col_ref, row_ref, put_dq, acc_k, acc_v, after=lambda tile: None):
    total = None
    for tile, (start, count, low, high) in enumerate(TILES):
        span = slice(start, start + count)
        mask = jnp.where(col_ref[low:high, 0:1] == row_ref[:, span], 0.0, -1000000000.0)
        dq, dk, dv = attend_back_tile(
            tile, k(slice(low, high)), v(slice(low, high)), q(span), do(span), mask, lse(tile, count)
        )
        put_dq(span, dq)
        top = jnp.sum(dq.astype(f32), 0, keepdims=True)
        total = top if total is None else total + top
        edge = 0 if tile == 0 else TILES[tile - 1][3]
        for acc, part in ((acc_k, dk), (acc_v, dv)):
            if edge > low:
                acc[low:edge, :] += part[: edge - low]
            if edge < high:
                acc[edge:high, :] = part[max(edge - low, 0) :]
        after(tile)
    return total


def attend_back_kernel(q_ref, k_ref, v_ref, do_ref, lse_a, lse_b, col_ref, row_ref, dq_ref, dk_ref, dv_ref, sum_ref, acc_k, acc_v):
    step = pl.program_id(0)

    def lse(tile, count):
        ref = lse_a if tile < 2 else lse_b
        return [ref[tile % 2, pl.ds(2 * step + head, 1), 0:count] for head in range(2)]

    def put_dq(span, value):
        dq_ref[span, :] = value

    take = lambda ref: lambda span: ref[span, :]
    total = attend_back_pair(
        take(q_ref), take(k_ref), take(v_ref), take(do_ref), lse, col_ref, row_ref, put_dq, acc_k, acc_v
    )
    dk_ref[...] = acc_k[...].astype(bf16)
    dv = acc_v[...].astype(bf16)
    dv_ref[...] = dv
    sum_ref[...] = jnp.zeros_like(sum_ref)
    sum_ref[0:1, :] = total
    sum_ref[1:2, :] = jnp.sum(dv.astype(f32), 0, keepdims=True)


def attend_back(q, k, v, do, lse_a, lse_b, ids_col, ids_row):
    tok, width = q.shape
    pair = pl.BlockSpec((tok, PAIR), lambda p: (0, p))
    out = jax.ShapeDtypeStruct((tok, width), bf16)
    return pl.pallas_call(
        attend_back_kernel,
        grid=(width // PAIR,),
        in_specs=[pair, pair, pair, pair, whole(lse_a.shape), whole(lse_b.shape), whole((tok, 1)), whole((1, tok))],
        out_specs=[pair, pair, pair, pl.BlockSpec((8, PAIR), lambda p: (0, p))],
        out_shape=[out, out, out, jax.ShapeDtypeStruct((8, width), f32)],
        scratch_shapes=[pltpu.VMEM((tok, PAIR), f32), pltpu.VMEM((tok, PAIR), f32)],
        compiler_params=params(60),
        cost_estimate=cost(4 * 10 * tok * HALF * width, tok * width * 18),
        name="attend_back",
    )(q, k, v, do, lse_a, lse_b, ids_col, ids_row)


def normed_back_kernel(dq_ref, dk_ref, dv_ref, w_ref, o_ref):
    o_ref[...] = nt(dq_ref[...], w_ref[0]) + nt(dk_ref[...], w_ref[1]) + nt(dv_ref[...], w_ref[2])


def normed_back(dq, dk, dv, w3):
    tok, width = dq.shape
    dim = w3.shape[1]
    rows = lambda n: pl.BlockSpec((TILE, n), lambda i: (i, 0))
    return pl.pallas_call(
        normed_back_kernel,
        grid=(tok // TILE,),
        in_specs=[rows(width), rows(width), rows(width), whole(w3.shape)],
        out_specs=rows(dim),
        out_shape=jax.ShapeDtypeStruct((tok, dim), f32),
        compiler_params=params(60),
        cost_estimate=cost(6 * tok * dim * width, tok * (dim * 4 + width * 6) + w3.size * 2),
        name="normed_back",
    )(dq, dk, dv, w3)


def input_back_kernel(x_ref, own_ref, peer_ref, dh_ref, gain_ref, o_ref, sum_ref):
    step = pl.program_id(0)
    unit, inv = standardize(x_ref[...].astype(f32))
    grad = own_ref[...] + peer_ref[...]
    o_ref[...] = (dh_ref[...] + norm_back(unit, inv, gain_ref[...], grad)).astype(bf16)

    @pl.when(step == 0)
    def _():
        sum_ref[...] = jnp.zeros_like(sum_ref)

    sum_ref[0:1] += jnp.sum(grad * unit, 0, keepdims=True)
    sum_ref[1:2] += jnp.sum(grad, 0, keepdims=True)


def input_back(tokens, own, peer, dh, gain):
    tok, dim = tokens.shape
    rows = pl.BlockSpec((TILE, dim), lambda i: (i, 0))
    return pl.pallas_call(
        input_back_kernel,
        grid=(tok // TILE,),
        in_specs=[rows, rows, rows, rows, whole((1, dim))],
        out_specs=[rows, whole((8, dim))],
        out_shape=[jax.ShapeDtypeStruct((tok, dim), bf16), jax.ShapeDtypeStruct((8, dim), f32)],
        compiler_params=params(60),
        cost_estimate=cost(20 * tok * dim, tok * dim * 16),
        name="input_back",
    )(tokens, own, peer, dh, gain)


def grad_kernel(parts, group, place_ref, a_ref, b_ref, *refs):
    outs, turned = refs[:parts], refs[parts]

    @pl.when(pl.program_id(0) == 0)
    def _():
        flat = jnp.transpose(a_ref[...])
        if group:
            for g in range(flat.shape[0] // group):
                at = pl.multiple_of(place_ref[g] * group, group)
                turned[pl.ds(at, group), :] = flat[g * group : (g + 1) * group, :]
        else:
            turned[...] = flat

    total = nn(turned[...], b_ref[...])
    rows = total.shape[0] // parts
    for i, out in enumerate(outs):
        out[...] = total[i * rows : (i + 1) * rows, :]


def weight_grad(parts, place, a, b):
    tok, dim = a.shape
    width = b.shape[1]
    step = 384
    count = place.shape[0]
    group = dim // count
    if group % 16:
        order = jnp.argsort(place)
        rows = (order[:, None] * group + jnp.arange(group)[None, :]).reshape(dim)
        a = jnp.take(a, rows, axis=1)
        group = 0
    rows = dim // parts
    return pl.pallas_call(
        functools.partial(grad_kernel, parts, group),
        grid_spec=pltpu.PrefetchScalarGridSpec(
            num_scalar_prefetch=1,
            grid=(width // step,),
            in_specs=[
                pl.BlockSpec((tok, dim), lambda i, *_: (0, 0)),
                pl.BlockSpec((tok, step), lambda i, *_: (0, i)),
            ],
            out_specs=[pl.BlockSpec((rows, step), lambda i, *_: (0, i))] * parts,
            scratch_shapes=[pltpu.VMEM((dim, tok), bf16)],
        ),
        out_shape=[jax.ShapeDtypeStruct((rows, width), f32)] * parts,
        compiler_params=params(60),
        cost_estimate=cost(2 * tok * dim * width, tok * (dim + width) * 2 + dim * width * 4),
        name="weight_grad",
    )(place, a, b)


class Exchange:
    def __init__(self, batch):
        side = 1
        while side * side * 4 < batch:
            side *= 2
        self.batch = batch
        sizes = (batch // (side * side), side, side)
        strides = (side * side, side, 1)
        axes = list(zip(sizes, strides))
        slow, mid, fast = axes
        self.orders = ((fast, mid, slow), (mid, fast, slow))
        me = lax.axis_index("batch")
        core = lax.axis_index("tp")
        away = jnp.arange(batch, dtype=jnp.int32) ^ me
        places = []
        for order in self.orders:
            place = jnp.zeros_like(away)
            for size, stride in order:
                place = place * size + (away // stride) % size
            places.append(place)
        self.place = jnp.where(core == 0, places[0], places[1]).astype(jnp.int32)

    def first_parts(self):
        return self.orders[0][0][0]

    def swap(self, block, phase, k):
        perm = []
        for i in range(self.batch):
            for core in range(2):
                _, stride = self.orders[core][phase]
                perm.append((2 * i + core, 2 * (i ^ (k * stride)) + core))
        return lax.ppermute(block, ("batch", "tp"), perm)

    def reduce(self, parts):
        for phase in range(3):
            got = [self.swap(parts[k], phase, k) for k in range(1, len(parts))]
            if phase == 2:
                total = parts[0]
                for g in got:
                    total = total + g
                return total
            size = self.orders[0][phase + 1][0]
            rows = parts[0].shape[0] // size
            cut = lambda a, i: lax.slice_in_dim(a, i * rows, (i + 1) * rows, axis=0)
            following = []
            for i in range(size):
                total = cut(parts[0], i)
                for g in got:
                    total = total + cut(g, i)
                following.append(total)
            parts = following


def other_core(values):
    return lax.ppermute(values, "tp", [(0, 1), (1, 0)])


COUNT = 12
STEPS = 4
PLAN = (
    (), (), (), (), ((0, 0),), (), (), ((1, 0), (0, 1),), ((2, 0),), (), (), ((0, 2),), (), ((1, 1),), ((3, 0),),
    (), (), (), ((3, 1), (5, 0), (4, 0), (0, 3),), ((2, 1), (1, 2),), ((4, 1),), ((2, 2), (6, 0),), ((8, 0),),
    ((3, 2),), ((1, 3), (6, 1),), ((7, 0),), ((4, 2),), (), ((5, 1), (2, 3),), (), ((3, 3),),
    ((7, 1), (6, 2), (8, 1),), (), ((5, 2),), (), (), ((8, 2),), (), (), ((9, 0),), (), ((11, 0),), (),
    ((4, 3), (7, 2), (10, 0), (9, 1), (6, 3), (5, 3), (11, 1), (8, 3), (10, 1), (7, 3), (11, 2), (9, 2), (10, 2), (11, 3), (9, 3), (10, 3),),
)


ORDERS = ((1, 2, 4, 8), (4, 1, 2, 8), (1, 4, 2, 8))
ORDER_OF = (0, 0, 1, 0, 0, 1, 0, 0, 1, 0, 0, 1)


class Route:
    def __init__(self):
        self.me = lax.axis_index("batch")
        self.core = core = lax.axis_index("tp")
        self.bits = {s: lax.rem(self.me // s, 2) for s in (1, 2, 4, 8)}
        near = {s: self.me + s * (1 - 2 * self.bits[s]) for s in (1, 2, 4, 8)}
        side = near[1] * (1 - core) + near[2] * core
        other = near[2] * (1 - core) + near[1] * core
        self.plain = (side, other, near[4], near[8])
        self.near = {1: side, 2: other, 4: near[4], 8: near[8]}
        self.weights = []
        for order in ORDERS:
            at = {s: 8 >> order.index(s) for s in order}
            first, second = at[1] * (1 - core) + at[2] * core, at[2] * (1 - core) + at[1] * core
            self.weights.append({1: first, 2: second, 4: at[4], 8: at[8]})

    def by_order(self, chunk, values):
        if isinstance(chunk, int):
            return values[ORDER_OF[chunk]]
        total = values[0]
        for kind in range(1, len(ORDERS)):
            own = sum((chunk == c).astype(jnp.int32) for c in range(COUNT) if ORDER_OF[c] == kind)
            total = total + own * (values[kind] - values[0])
        return total

    def partner(self, chunk, step):
        return self.by_order(chunk, [self.near[order[step]] for order in ORDERS])

    def places(self, chunk):
        terms = {}
        for s in (1, 2, 4, 8):
            weight = self.by_order(chunk, [w[s] for w in self.weights])
            terms[s] = (self.bits[s] * weight, (1 - self.bits[s]) * weight)
        return [sum(terms[s][(g // s) % 2] for s in (1, 2, 4, 8)) for g in range(16)]


def attend_pair(rows_at, rows, keys, values, mask_ref, put):
    first = lax.broadcasted_iota(jnp.int32, (1, PAIR), 1) < HEAD_DIM
    zero = jnp.zeros((), bf16)
    with_ones = jnp.concatenate([values, jnp.ones_like(values)], 1)
    for at, count in ROWS:
        part = rows(at, count)
        both = jnp.concatenate([jnp.where(first, part, zero), jnp.where(first, zero, part)], 0)
        mask = mask_ref[at : at + count, :]
        scores = nt(both, keys) + jnp.concatenate([mask, mask], 0)
        top = jnp.max(scores, -1, keepdims=True)
        mixed = nn(jnp.exp(scores - top).astype(bf16), with_ones)
        total = mixed[:, PAIR:]
        mixed = mixed[:, :PAIR] / total
        logs = top + jnp.log(total)
        put(at, count, jnp.where(first, mixed[:count], mixed[count:]).astype(bf16), logs[:count], logs[count:])


def layer_kernel(
    tok_h, g_h, w3_h, wo_h, wi_h, wb_h,
    ids_ref, gain1_ref, shift1_ref, qvb_ref, ob_ref, gain2_ref, shift2_ref, ib_ref, bb_ref,
    layer_h, input_h, grads_h, sums_ref, heads_h, hid_h, mid_h,
    buf_h, buf_d, buf_n, buf_g, buf_m, own, peer, wi, wb, wo, acc_k, acc_v, col_ref, query_ids, key_ids, mask_ref,
    bias_ref, lse_ref, log_ref, chunks, recv0, recv1, recv2, recv3, sums_in,
    load_sem, send_sem, recv_sem, grad_sem, swap_send, swap_recv, sums_send, sums_recv, put_sem, free_sem,
):
    mesh_id = pl.DeviceIdType.MESH
    route = Route()
    me, core = route.me, route.core
    tok, dim = buf_g.shape
    width = buf_h.shape[1]
    third = wo.shape[0]
    tiles = tok // TILE
    blocks = width // LANES
    recvs = (recv0, recv1, recv2, recv3)
    vector = lambda ref: ref[...].reshape(1, -1)

    barrier = pltpu.get_barrier_semaphore()
    for other in route.plain:
        pl.semaphore_signal(barrier, inc=1, device_id=(other, core), device_id_type=mesh_id)
    pl.semaphore_signal(barrier, inc=1, device_id=(me, 1 - core), device_id_type=mesh_id)

    def load(source, target, at):
        copy = pltpu.make_async_copy(source, target, load_sem.at[at])
        copy.start()
        return copy

    def load_w3(at):
        return [load(w3_h.at[c], wi.at[:, pl.ds(c * third, third)], at + c) for c in range(3)]

    tok_load = load(tok_h, buf_d.at[:, pl.ds(0, dim)], 0)
    w3_load = load_w3(1)
    wo_load = load(wo_h, wo, 4)


    def hop(chunk, step):
        half = 8 >> step
        return pltpu.make_async_remote_copy(
            src_ref=chunks.at[chunk, pl.ds(half, half)],
            dst_ref=recvs[step].at[chunk],
            send_sem=send_sem.at[step, chunk],
            recv_sem=recv_sem.at[step, chunk],
            device_id=(route.partner(chunk, step), core),
            device_id_type=mesh_id,
        )

    def deliver(chunk):
        return pltpu.make_async_copy(chunks.at[chunk, 0], grads_h.at[chunk], grad_sem.at[chunk])

    def finish(chunk, step):
        got = hop(chunk, step)
        got.wait_send()
        got.wait_recv()

        def add(g, carry):
            chunks[chunk, g] += recvs[step][chunk, g]
            return carry

        lax.fori_loop(0, 8 >> step, add, 0)
        if step < STEPS - 1:
            hop(chunk, step + 1).start()
        else:
            deliver(chunk).start()

    left = list(PLAN)

    def arrivals():
        for chunk, step in left.pop(0):
            finish(chunk, step)

    def loop(count, body, planned=True):
        each = [left.pop(0) for _ in range(count)] if planned else []

        def turn(i, carry):
            body(i)
            for at, now in enumerate(each):
                if now:

                    @pl.when(i == at)
                    def _():
                        for chunk, step in now:
                            finish(chunk, step)

            return carry

        lax.fori_loop(0, count, turn, 0)

    def gradient(chunk, source, right):
        places = route.places(chunk)
        total = tn(source[...], right)
        rows = dim // 16
        for g in range(16):
            chunks[chunk, places[g]] = total[g * rows : (g + 1) * rows, :]
        hop(chunk, 0).start()

    def columns(at):
        return pl.ds(pl.multiple_of(at, PAIR), LANES)

    def rows_of(i):
        return pl.ds(pl.multiple_of(i * TILE, TILE), TILE)


    def swap(turn_at, i, rows):
        return pltpu.make_async_remote_copy(
            src_ref=own.at[rows],
            dst_ref=peer.at[rows],
            send_sem=swap_send.at[turn_at, i],
            recv_sem=swap_recv.at[turn_at, i],
            device_id=(me, 1 - core),
            device_id_type=mesh_id,
        )

    def swapped(turn_at, i):
        got = swap(turn_at, i, rows_of(i))
        got.wait_send()
        got.wait_recv()
        return own[rows_of(i), :] + peer[rows_of(i), :]

    def peer_is_free():
        pl.semaphore_signal(free_sem, inc=1, device_id=(me, 1 - core), device_id_type=mesh_id)


    ids = vector(ids_ref)
    for half in range(2):
        query_ids[half, :, 0:HALF] = ids[:, half * HALF : (half + 1) * HALF]
        key_ids[half] = ids[:, half * LOW : half * LOW + WINDOW]
    col_ref[...] = jnp.transpose(jnp.broadcast_to(ids, (PAIR, tok)))
    for c in range(blocks):
        bias_ref[c] = vector(ib_ref)[:, c * LANES : (c + 1) * LANES]
    sums_ref[...] = jnp.zeros_like(sums_ref)
    tok_load.wait()
    for item in w3_load:
        item.wait()

    def first_norm(values):
        unit, inv = standardize(values.astype(f32))
        return unit, inv, (unit * vector(gain1_ref) + vector(shift1_ref)).astype(bf16)

    def project_rows(i):
        _, _, normed = first_norm(buf_d[rows_of(i), 0:dim])
        out = nn(normed, wi[:, 0 : 3 * third])
        query = (out[:, 0:third] + qvb_ref[0:1, :]).astype(bf16)
        buf_h[rows_of(i), 0:third] = (query.astype(f32) * HEAD_DIM ** (-0.5)).astype(bf16)
        buf_h[rows_of(i), third : 2 * third] = out[:, third : 2 * third].astype(bf16)
        buf_h[rows_of(i), 2 * third : 3 * third] = (out[:, 2 * third :] + qvb_ref[1:2, :]).astype(bf16)

    def body(i):
        project_rows(2 * i)
        project_rows(2 * i + 1)

    loop(tiles // 2, body, False)
    wi_load = load(wi_h, wi, 6)
    g_load = load(g_h, buf_g, 5)
    wb_load = load(wb_h, wb, 7)
    save_qkv = load(buf_h.at[:, pl.ds(0, 3 * third)], heads_h.at[:, pl.ds(0, 3 * third)], 8)


    wo_load.wait()
    log_ref[...] = jnp.zeros_like(log_ref)
    lane = lax.broadcasted_iota(jnp.int32, (1, PAIR), 1) // 8

    def body(half):
        start = pl.multiple_of(half * HALF, TILE)
        window = pl.ds(pl.multiple_of(half * LOW, 64), WINDOW)
        mask_ref[...] = jnp.where(col_ref[pl.ds(start, HALF), 0:1] == key_ids[half], 0.0, -1000000000.0)

        def pair(p):
            pick = lambda block: pl.ds(pl.multiple_of(block * third + p * PAIR, PAIR), PAIR)

            def rows(at, count):
                return buf_h[pl.ds(pl.multiple_of(start + at, 32), count), pick(0)]

            def put(at, count, mixed, *logs):
                buf_n[pl.ds(pl.multiple_of(start + at, 32), count), pick(0)] = mixed
                old = log_ref[at : at + count, :]
                for head in range(2):
                    old = jnp.where(lane == 2 * p + head, logs[head], old)
                log_ref[at : at + count, :] = old

            attend_pair(start, rows, buf_h[window, pick(1)], buf_h[window, pick(2)], mask_ref, put)

        loop(third // PAIR, pair, False)

        turned = jnp.transpose(log_ref[...])
        for head in range(third // HEAD_DIM):
            lse_ref[half, head, 0:1, 0:HALF] = turned[head * 8 : head * 8 + 1, :]

        @pl.when(half == 0)
        def _():
            pl.semaphore_wait(barrier, STEPS + 1)

        def project(j):
            i = half * (tiles // 2) + j
            own[rows_of(i), :] = nn(buf_n[rows_of(i), 0:third], wo[...])
            swap(0, i, rows_of(i)).start()

        loop(tiles // 2, project, False)

    loop(2, body, False)
    save_o = load(buf_n.at[:, pl.ds(0, third)], heads_h.at[:, pl.ds(3 * third, third)], 9)


    wi_load.wait()
    save_qkv.wait()
    save_o.wait()
    root = 0.7978845608028654

    def hidden(i, c):
        u = nn(buf_n[rows_of(i), :], wi[:, columns(c * LANES)]) + bias_ref[c]
        t = jnp.tanh(u * (root + (root * 0.044715) * (u * u)))
        buf_h[rows_of(i), columns(c * LANES)] = (u * (0.5 + 0.5 * t)).astype(bf16)
        buf_d[rows_of(i), columns(c * LANES)] = u.astype(bf16)

    def body(i):
        total = swapped(0, i)
        middle = buf_d[rows_of(i), 0:dim].astype(f32) + total + vector(ob_ref)
        buf_m[rows_of(i), :] = middle
        unit, _ = standardize(middle)
        buf_n[rows_of(i), :] = (unit * vector(gain2_ref) + vector(shift2_ref)).astype(bf16)
        hidden(i, 0)

    loop(tiles, body, False)
    peer_is_free()
    save_mid = load(buf_m, mid_h, 10)
    g_load.wait()
    gradient(0, buf_g, buf_h[:, 0:LANES])
    arrivals()

    def body(j):
        c = j + 1
        loop(tiles, lambda i: hidden(i, c), False)
        gradient(c, buf_g, buf_h[:, columns(c * LANES)])

    loop(blocks - 1, body)
    save_hid = load(buf_h, hid_h, 11)


    wb_load.wait()
    pl.semaphore_wait(free_sem, 1)

    def body(i):
        grad = buf_g[rows_of(i), :]
        for at in range(0, width, 512):
            u = buf_d[rows_of(i), at : at + 512].astype(f32)
            square = u * u
            t = jnp.tanh(u * (root + (root * 0.044715) * square))
            slope = 0.5 + 0.5 * t + (0.5 * u) * (1.0 - t * t) * (root + (3.0 * 0.044715 * root) * square)
            du = (nt(grad, wb[at : at + 512, :]) * slope).astype(bf16)
            buf_d[rows_of(i), at : at + 512] = du
            sums_ref[4:5, at : at + 512] += jnp.sum(du.astype(f32), 0, keepdims=True)
        own[rows_of(i), :] = nt(buf_d[rows_of(i), :], wi[...])
        swap(1, i, rows_of(i)).start()
        sums_ref[2:3, dim : 2 * dim] += jnp.sum(grad.astype(f32), 0, keepdims=True)

    loop(tiles, body)
    w3_late = load_w3(1)
    save_hid.wait()
    heads_load = load(heads_h, buf_h, 8)


    loop(4, lambda i: gradient(4 + i, buf_n, buf_d[:, columns(i * LANES)]))


    save_mid.wait()

    def body(i):
        grad = swapped(1, i)
        unit, inv = standardize(buf_m[rows_of(i), :])
        dh = buf_g[rows_of(i), :].astype(f32) + norm_back(unit, inv, vector(gain2_ref), grad)
        buf_m[rows_of(i), :] = dh
        dr = dh.astype(bf16)
        buf_n[rows_of(i), :] = dr
        buf_d[rows_of(i), 0:third] = nt(dr, wo[...]).astype(bf16)
        sums_ref[1:2, dim : 2 * dim] += jnp.sum(grad * unit, 0, keepdims=True)
        sums_ref[2:3, 0:dim] += jnp.sum(grad, 0, keepdims=True)
        sums_ref[1:2, 0:dim] += jnp.sum(dr.astype(f32), 0, keepdims=True)

    loop(tiles, body)
    peer_is_free()
    tok_late = load(tok_h, buf_g, 0)
    heads_load.wait()
    gradient(8, buf_n, buf_h[:, 3 * third : 4 * third])
    arrivals()


    first = lax.broadcasted_iota(jnp.int32, (1, PAIR), 1) < HEAD_DIM
    zero = jnp.zeros((), bf16)

    def body(at):
        p, half = at // 2, lax.rem(at, 2)
        pick = lambda block: pl.ds(pl.multiple_of(block * third + p * PAIR, PAIR), PAIR)
        window = pl.ds(pl.multiple_of(half * LOW, 64), WINDOW)
        keys, values = buf_h[window, pick(1)], buf_h[window, pick(2)]

        @pl.when(half == 0)
        def _():
            acc_k[...] = jnp.zeros_like(acc_k)
            acc_v[...] = jnp.zeros_like(acc_v)

        for begin, count in ((0, 256), (256, 352)):
            span = pl.ds(pl.multiple_of(half * HALF + begin, 32), count)
            rows, grads = buf_h[span, pick(0)], buf_d[span, pick(0)]
            same = col_ref[window, 0:1] == query_ids[half, :, begin : begin + count]
            mask = jnp.where(same, 0.0, -1000000000.0)
            parts = []
            for head in range(2):
                own_part = lambda a: jnp.where(first, a, zero) if head == 0 else jnp.where(first, zero, a)
                lse = lse_ref[half, 2 * p + head, 0:1, begin : begin + count]
                probs = jnp.exp(nt(keys, own_part(rows)) + mask - lse)
                back = nt(values, own_part(grads))
                inner = jnp.sum(probs * back, 0, keepdims=True)
                slant = (probs * (back - inner)).astype(bf16)
                parts.append((tn(slant, keys), nn(slant, rows), nn(probs.astype(bf16), grads)))
            dq, dk, dv = (jnp.where(first, a, b) for a, b in zip(*parts))
            dq = (dq * HEAD_DIM ** (-0.5)).astype(bf16)
            buf_d[span, pick(1)] = dq
            sums_ref[3:4, pick(0)] += jnp.sum(dq.astype(f32), 0, keepdims=True)
            acc_k[window, :] += dk
            acc_v[window, :] += dv

        @pl.when(half == 1)
        def _():
            buf_d[:, pick(2)] = acc_k[...].astype(bf16)
            dv = acc_v[...].astype(bf16)
            buf_d[:, pick(3)] = dv
            sums_ref[3:4, pick(1)] = jnp.sum(dv.astype(f32), 0, keepdims=True)

    loop(2 * (third // PAIR), body)
    hid_load = load(hid_h, buf_h, 8)


    tok_late.wait()

    def body(i):
        _, _, normed = first_norm(buf_g[rows_of(i), :])
        buf_n[rows_of(i), :] = normed

    loop(tiles, body, False)
    arrivals()
    loop(3, lambda i: gradient(9 + i, buf_n, buf_d[:, columns(third + i * LANES)]))


    for item in w3_late:
        item.wait()
    pl.semaphore_wait(free_sem, 1)

    def body(i):
        own[rows_of(i), :] = nt(buf_d[rows_of(i), third : 4 * third], wi[:, 0 : 3 * third])
        swap(2, i, rows_of(i)).start()

    loop(tiles, body)

    def body(i):
        grad = swapped(2, i)
        unit, inv, _ = first_norm(buf_g[rows_of(i), :])
        buf_g[rows_of(i), :] = (buf_m[rows_of(i), :] + norm_back(unit, inv, vector(gain1_ref), grad)).astype(bf16)
        sums_ref[0:1, 0:dim] += jnp.sum(grad * unit, 0, keepdims=True)
        sums_ref[0:1, dim : 2 * dim] += jnp.sum(grad, 0, keepdims=True)

    loop(tiles, body)
    peer_is_free()
    input_put = pltpu.make_async_copy(buf_g, input_h, put_sem.at[1])
    input_put.start()
    mid_load = load(mid_h, buf_m, 10)

    def whole_hop(step):
        return pltpu.make_async_remote_copy(
            src_ref=sums_ref,
            dst_ref=sums_in.at[step],
            send_sem=sums_send.at[step],
            recv_sem=sums_recv.at[step],
            device_id=(route.plain[step], core),
            device_id_type=mesh_id,
        )

    def add_sums(step):
        whole_hop(step).wait()
        sums_ref[...] += sums_in[step]

    whole_hop(0).start()


    hid_load.wait()
    pl.semaphore_wait(free_sem, 1)

    def body(i):
        own[rows_of(i), :] = nn(buf_h[rows_of(i), :], wb[...])
        swap(3, i, rows_of(i)).start()

    loop(tiles, body)
    add_sums(0)
    whole_hop(1).start()
    mid_load.wait()

    def body(i):
        buf_n[rows_of(i), :] = (buf_m[rows_of(i), :] + swapped(3, i) + vector(bb_ref)).astype(bf16)

    loop(tiles, body)
    layer_put = pltpu.make_async_copy(buf_n, layer_h, put_sem.at[0])
    layer_put.start()
    rest = left.pop(0)
    gap = len(rest) // STEPS
    for step in range(1, STEPS):
        for item in rest[(step - 1) * gap : step * gap]:
            finish(*item)
        add_sums(step)
        if step + 1 < STEPS:
            whole_hop(step + 1).start()
    for item in rest[(STEPS - 1) * gap :]:
        finish(*item)
    for chunk in range(COUNT):
        deliver(chunk).wait()
    input_put.wait()
    layer_put.wait()


def whole_layer(tokens, g, w3, wo, wi, wb, ids, gain1, shift1, qvb, ob, gain2, shift2, ib, bb):
    tok, dim = g.shape
    width = wi.shape[1]
    third = wo.shape[0]
    rows = dim // 16
    hbm = pl.BlockSpec(memory_space=pl.ANY)
    vmem = pl.BlockSpec(memory_space=pltpu.VMEM)
    dma = pltpu.SemaphoreType.DMA
    return pl.pallas_call(
        layer_kernel,
        in_specs=[hbm] * 6 + [vmem] * 9,
        out_specs=[hbm, hbm, hbm, vmem, hbm, hbm, hbm],
        out_shape=[
            jax.ShapeDtypeStruct((tok, dim), bf16),
            jax.ShapeDtypeStruct((tok, dim), bf16),
            jax.ShapeDtypeStruct((COUNT, rows, LANES), f32),
            jax.ShapeDtypeStruct((8, width), f32),
            jax.ShapeDtypeStruct((tok, width), bf16),
            jax.ShapeDtypeStruct((tok, width), bf16),
            jax.ShapeDtypeStruct((tok, dim), f32),
        ],
        scratch_shapes=[
            pltpu.VMEM((tok, width), bf16),
            pltpu.VMEM((tok, width), bf16),
            pltpu.VMEM((tok, dim), bf16),
            pltpu.VMEM((tok, dim), bf16),
            pltpu.VMEM((tok, dim), f32),
            pltpu.VMEM((tok, dim), f32),
            pltpu.VMEM((tok, dim), f32),
            pltpu.VMEM((dim, width), bf16),
            pltpu.VMEM((width, dim), bf16),
            pltpu.VMEM((third, dim), bf16),
            pltpu.VMEM((tok, PAIR), f32),
            pltpu.VMEM((tok, PAIR), f32),
            pltpu.VMEM((tok, PAIR), jnp.int32),
            pltpu.VMEM((2, 1, 640), jnp.int32),
            pltpu.VMEM((2, 1, WINDOW), jnp.int32),
            pltpu.VMEM((HALF, WINDOW), f32),
            pltpu.VMEM((width // LANES, 1, LANES), f32),
            pltpu.VMEM((2, third // HEAD_DIM, 8, 640), f32),
            pltpu.VMEM((HALF, PAIR), f32),
            pltpu.VMEM((COUNT, 16, rows, LANES), f32),
            pltpu.VMEM((COUNT, 8, rows, LANES), f32),
            pltpu.VMEM((COUNT, 4, rows, LANES), f32),
            pltpu.VMEM((COUNT, 2, rows, LANES), f32),
            pltpu.VMEM((COUNT, 1, rows, LANES), f32),
            pltpu.VMEM((STEPS, 8, width), f32),
            dma((12,)),
            dma((STEPS, COUNT)),
            dma((STEPS, COUNT)),
            dma((COUNT,)),
            dma((4, tok // TILE)),
            dma((4, tok // TILE)),
            dma((STEPS,)),
            dma((STEPS,)),
            dma((2,)),
            pltpu.SemaphoreType.REGULAR,
        ],
        compiler_params=pltpu.CompilerParams(vmem_limit_bytes=VMEM_LIMIT, collective_id=0, has_side_effects=True),
        cost_estimate=cost(34e9, 40e6),
        name="whole_layer",
    )(tokens, g, w3, wo, wi, wb, ids, gain1, shift1, qvb, ob, gain2, shift2, ib, bb)


def outputs_kernel(layer_h, input_h, grads_h, sums_ref, layer_o, input_o, *refs):
    n1g, n1s, qkv, qvb, out, obg, n2g, n2s, inw, ibg, back, bbg, held, kept, in_sem, out_sem = refs
    me = lax.axis_index("batch")
    dim = sums_ref.shape[1] // 2
    third = dim // 2
    pieces = 4
    rows = held.shape[1] // pieces
    grads_in = pltpu.make_async_copy(grads_h, kept, in_sem.at[2 * pieces])
    grads_in.start()
    moves = []
    for i, (source, target) in enumerate(((layer_h, layer_o), (input_h, input_o))):
        for j in range(pieces):
            span = pl.ds(j * rows, rows)
            at = i * pieces + j
            coming = pltpu.make_async_copy(source.at[span], held.at[i, span], in_sem.at[at])
            coming.start()
            moves.append((coming, pltpu.make_async_copy(held.at[i, span], target.at[span], out_sem.at[at])))

    def mine(row, at, size):
        n = size // 16
        values = jnp.broadcast_to(sums_ref[row : row + 1, at : at + size], (8, size))
        return pltpu.roll(values, size - me * n, 1)[0:1, 0:n]

    for ref, row, at in ((n1g, 0, 0), (n1s, 0, dim), (obg, 1, 0), (n2g, 1, dim), (n2s, 2, 0), (bbg, 2, dim)):
        ref[...] = mine(row, at, dim).reshape(-1)
    ibg[...] = mine(4, 0, 2 * dim).reshape(-1)
    qvb[0:1, :] = mine(3, 0, third)
    qvb[1:2, :] = mine(3, third, third)
    grads_in.wait()
    places = [back.at[:, pl.ds(c * LANES, LANES)] for c in range(4)]
    places += [inw.at[:, pl.ds(c * LANES, LANES)] for c in range(4)]
    places += [out] + [qkv.at[c] for c in range(3)]
    going = [pltpu.make_async_copy(kept.at[c], place, out_sem.at[2 * pieces + c]) for c, place in enumerate(places)]
    for item in going:
        item.start()
    for coming, leaving in moves:
        coming.wait()
        leaving.start()
    for item in going:
        item.wait()
    for _, leaving in moves:
        leaving.wait()


def outputs(layer, grad, grads, sums):
    rows, width = grads.shape[1], sums.shape[1]
    hbm = pl.BlockSpec(memory_space=pl.ANY)
    vmem = pl.BlockSpec(memory_space=pltpu.VMEM)
    small = jax.ShapeDtypeStruct((rows,), f32)
    shape = lambda *s: jax.ShapeDtypeStruct(s, f32)
    return pl.pallas_call(
        outputs_kernel,
        in_specs=[hbm, hbm, hbm, vmem],
        out_specs=[hbm, hbm, vmem, vmem, hbm, vmem, hbm, vmem, vmem, vmem, hbm, vmem, hbm, vmem],
        out_shape=[
            jax.ShapeDtypeStruct(layer.shape, bf16),
            jax.ShapeDtypeStruct(grad.shape, bf16),
            small,
            small,
            shape(3, rows, LANES),
            shape(2, rows // 2),
            shape(rows, LANES),
            small,
            small,
            small,
            shape(rows, width),
            shape(2 * rows),
            shape(rows, width),
            small,
        ],
        scratch_shapes=[
            pltpu.VMEM((2,) + layer.shape, bf16),
            pltpu.VMEM(grads.shape, f32),
            pltpu.SemaphoreType.DMA((9,)),
            pltpu.SemaphoreType.DMA((8 + COUNT,)),
        ],
        compiler_params=params(60),
        name="outputs",
    )(layer, grad, grads, sums)


def shards(
    tokens,
    seq_ids,
    cotangent,
    norm1_gain,
    norm1_shift,
    w_qkv,
    qv_bias,
    w_out,
    out_bias,
    norm2_gain,
    norm2_shift,
    w_in,
    in_bias,
    w_back,
    back_bias,
    batch,
):
    tok, dim = tokens.shape
    w3 = jnp.transpose(w_qkv, (1, 0, 2))
    if batch == 16:
        layer, grad, grads, sums, *_ = whole_layer(
            tokens, cotangent, w3, w_out, w_in, w_back, seq_ids,
            norm1_gain, norm1_shift, qv_bias, out_bias, norm2_gain, norm2_shift, in_bias, back_bias,
        )
        results = list(outputs(layer, grad, grads, sums))
        results[4] = jnp.transpose(results[4], (1, 0, 2))
        results[6], results[12] = results[6].T, results[12].T
        return tuple(results)

    row = lambda a: a.reshape(1, -1)
    ids_col, ids_row = seq_ids.reshape(tok, 1), seq_ids.reshape(1, tok)
    exchange = Exchange(batch)
    parts = exchange.first_parts()

    normed, q, k, v = project(tokens, row(norm1_gain), row(norm1_shift), w3, qv_bias)
    mixed, lse_a, part_a = attend(0, q, k, v, ids_col, ids_row, w_out)
    peer_a = other_core(part_a)
    mixed, lse_b, part_b = attend(1, q, k, v, ids_col, ids_row, w_out, (mixed,))
    peer_b = other_core(part_b)
    mlp = (row(out_bias), row(norm2_gain), row(norm2_shift), w_in, row(in_bias))
    state = hidden_layer(0, tokens, part_a, peer_a, *mlp)
    state = hidden_layer(1, tokens, part_b, peer_b, *mlp, before=tuple(state))
    middle, normed_two, hidden, slope = state

    back_parts = weight_grad(parts, exchange.place, cotangent, hidden)
    du, dn2, in_bias_sum, back_bias_sum = hidden_back(cotangent, slope, w_back, w_in)
    dn2_peer = other_core(dn2)
    in_parts = weight_grad(parts, exchange.place, normed_two, du)
    mlp_own = rows_matmul(hidden, w_back)
    mlp_peer = other_core(mlp_own)
    dh, dr, do, middle_sums = middle_back(middle, dn2, dn2_peer, cotangent, row(norm2_gain), w_out)
    out_parts = weight_grad(parts, exchange.place, dr, mixed)
    layer_out = (middle + (mlp_own + mlp_peer) + back_bias).astype(bf16)
    dq, dk, dv, qv_sums = attend_back(q, k, v, do, lse_a, lse_b, ids_col, ids_row)
    q_parts = weight_grad(parts, exchange.place, normed, dq)
    k_parts = weight_grad(parts, exchange.place, normed, dk)
    v_parts = weight_grad(parts, exchange.place, normed, dv)
    dn1 = normed_back(dq, dk, dv, w3)
    dn1_peer = other_core(dn1)
    tokens_grad, input_sums = input_back(tokens, dn1, dn1_peer, dh, row(norm1_gain))

    w_back_grad = jnp.transpose(exchange.reduce(back_parts))
    w_in_grad = exchange.reduce(in_parts)
    w_out_grad = jnp.transpose(exchange.reduce(out_parts))
    w_qkv_grad = jnp.stack([exchange.reduce(p) for p in (q_parts, k_parts, v_parts)], 1)

    pieces = [input_sums[0], input_sums[1], middle_sums[2], middle_sums[0], middle_sums[1], back_bias_sum[0]]
    pieces += [qv_sums[0], qv_sums[1], in_bias_sum[0]]
    packed = jnp.concatenate([p.reshape(batch, -1) for p in pieces], 1)
    vectors = lax.psum_scatter(packed, "batch", scatter_dimension=0, tiled=True)[0]
    out, at = [], 0
    for p in pieces:
        n = p.shape[0] // batch
        out.append(vectors[at : at + n])
        at += n
    n1g, n1s, obg, n2g, n2s, bbg, qb, vb, ibg = out
    return (
        layer_out,
        tokens_grad,
        n1g,
        n1s,
        w_qkv_grad,
        jnp.stack([qb, vb]),
        w_out_grad,
        obg,
        n2g,
        n2s,
        w_in_grad,
        ibg,
        w_back_grad,
        bbg,
    )


def solution(mesh):
    in_specs = (
        P("batch", None),
        P("batch"),
        P("batch", None),
        P(),
        P(),
        P(None, None, "tp"),
        P(None, "tp"),
        P("tp", None),
        P(),
        P(),
        P(),
        P(None, "tp"),
        P("tp"),
        P("tp", None),
        P(),
    )
    out_specs = (
        P("batch", None),
        P("batch", None),
        P("batch"),
        P("batch"),
        P("batch", None, "tp"),
        P(None, ("tp", "batch")),
        P("tp", "batch"),
        P("batch"),
        P("batch"),
        P("batch"),
        P("batch", "tp"),
        P(("tp", "batch")),
        P("tp", "batch"),
        P("batch"),
    )
    body = functools.partial(shards, batch=mesh.shape["batch"])
    return jax.shard_map(body, mesh=mesh, in_specs=in_specs, out_specs=out_specs, check_vma=False)
```
